256 devices in a mesh: lon: 16 (over y, x_lo, core), lat: 16 (over x_hi, z).
Axes of the slice: x: 4 (x_hi: 2, x_lo: 2; x = x_hi * 2 + x_lo), y: 4, z: 8, core: 2. Of those that a mesh axis runs over, the one named last changes fastest.
Arguments:
- cells: bfloat16 [2, 96, 576, 384], P(None, 'lat', 'lon'), may hold values from -48 to 48
- qkv_weight: bfloat16 [384, 1152], replicated, may hold values from -0.3125 to 0.3125
- out_weight: bfloat16 [384, 384], replicated, may hold values from -0.3125 to 0.3125
- earth_bias: float32 [16, 12, 3312], P('lat'), may hold values from -3 to 445
- cotangent: bfloat16 [2, 96, 576, 384], P(None, 'lat', 'lon'), may hold values from -6 to 6
Outputs:
- result: bfloat16 [2, 96, 576, 384], P(None, 'lat', 'lon')
- grad_cells: bfloat16 [2, 96, 576, 384], P(None, 'lat', 'lon')
- grad_qkv_weight: float32 [384, 1152], replicated
- grad_out_weight: float32 [384, 384], replicated
- grad_earth_bias: float32 [16, 12, 3312], P('lat')
The draws below stay inside these ranges and needn't reach their ends.
All inputs are finite; a program needn't handle non-finite values.
Results may differ from the reference program's by a relative error of at most 0.0095.
Values may be sent and summed in bfloat16 or wider, within the bound.
A program may use at most 64 MiB of HBM per device.

```python
import math
import jax
import jax.numpy as jnp
from jax import lax

C = 384
HEADS = 12
LEV = 2
WH = 6
WW = 12
NLAT = 96
NLON = 576
TYPES = 16
ENTRIES = 3312
CELLS = 110592


def draw_cells(key, part):
    key = jax.random.fold_in(key, 5)
    noise_key, row_key, column_key = jax.random.split(key, 3)
    full_shape = (LEV, NLAT, NLON, C)
    noise_part = jnp.clip(jax.random.normal(noise_key, full_shape, jnp.float32), -4.0, 4.0)
    row_scale = jnp.exp(jax.random.uniform(row_key, (LEV, NLAT, NLON, 1), jnp.float32, math.log(0.316), math.log(3.16)))
    column_scale = jnp.exp(jax.random.uniform(column_key, (C,), jnp.float32, math.log(0.316), math.log(3.16)))
    return (noise_part * row_scale * column_scale).astype(jnp.bfloat16)


def draw_earth_bias(key, part):
    key = jax.random.fold_in(key, 11)
    base_key, flag_key, block_key, offset_key, strength_key = jax.random.split(key, 5)
    table_shape = (TYPES, HEADS, ENTRIES)
    span_width = 2 * WW - 1
    base_part = jnp.clip(jax.random.normal(base_key, table_shape, jnp.float32), -3.0, 3.0)
    spiked = (jax.random.randint(flag_key, (TYPES, HEADS, 1), 0, 4) == 0).astype(jnp.float32)
    block_index = jax.random.randint(block_key, (TYPES, HEADS, 1), 0, ENTRIES // span_width)
    spot_index = block_index * span_width + jax.random.randint(offset_key, (TYPES, HEADS, 1), 0, span_width - 1)
    strength = jnp.exp(jax.random.uniform(strength_key, (TYPES, HEADS, 1), jnp.float32, math.log(220.0), math.log(440.0)))
    entry_ids = jnp.arange(ENTRIES, dtype=jnp.int32)[None, None, :]
    spike_part = strength * (entry_ids == spot_index).astype(jnp.float32) + (strength + 2.0) * (entry_ids == spot_index + 1).astype(jnp.float32)
    return base_part + spiked * spike_part


def shard_levels(key, shape, cuts, smallest, top_value):
    def one(axis_at, parts):
        heights = jax.random.uniform(jax.random.fold_in(jax.random.fold_in(key, 6), axis_at), (parts,), jnp.float32, smallest / len(cuts), top_value / len(cuts))
        return jnp.repeat(jnp.exp(heights), shape[axis_at] // parts).reshape((-1,) + (1,) * (len(shape) - axis_at - 1))

    gain = one(*cuts[0])
    for cut in cuts[1:]:
        gain = gain * one(*cut)
    return gain


def scatter_about(key, dims, scale, bound, pieces=(), kind=jnp.bfloat16):
    loudness = shard_levels(key, dims, pieces, -0.22, 0.18) if pieces else 1.0
    entries = jax.random.normal(key, dims, jnp.float32) * scale * loudness
    return jnp.minimum(jnp.maximum(entries, -bound), bound).astype(kind)


def setup_inputs(seed: int = 0) -> dict:
    streams_of = jax.random.split(jax.random.key(seed), 6)
    return {
        "cells": draw_cells(jax.random.fold_in(streams_of[5], 71), 0),
        "qkv_weight": scatter_about(streams_of[1], (C, 3 * C), C ** -0.5, 0.3125),
        "out_weight": scatter_about(streams_of[2], (C, C), C ** -0.5, 0.3125),
        "earth_bias": draw_earth_bias(jax.random.fold_in(streams_of[5], 71), 0),
        "cotangent": scatter_about(streams_of[4], (LEV, NLAT, NLON, C), 1.0, 6.0, ((1, 16), (2, 16))),
    }


def normalize(samples):
    average = lax.optimization_barrier(jnp.mean(samples, axis=-1, keepdims=True))
    centred = samples - average
    spread = lax.optimization_barrier(jnp.mean(centred * centred, axis=-1, keepdims=True))
    return centred * lax.rsqrt(spread + 1e-05)

def bias_layout(tokens):
    position = jnp.arange(tokens, dtype=jnp.int32)
    level_of = position // (WH * WW)
    row_of = position // WW % WH
    column = position % WW
    pair_index = (level_of[:, None] * LEV + level_of[None, :]) * (WH * WH) + row_of[:, None] * WH + row_of[None, :]
    return pair_index * (2 * WW - 1) + column[:, None] - column[None, :] + (WW - 1)

def blocked_pairs(tokens, last_rows):
    position = jnp.arange(tokens, dtype=jnp.int32)
    region = position // WW % WH >= WH - WH // 2
    crossing = region[:, None] != region[None, :]
    return jnp.logical_and(last_rows[:, None, None, None, None], crossing[None, None, None, :, :])

def attend(projected, tables, last_rows):
    channels = projected.shape[-1] // 3
    head_count = tables.shape[1]
    head_size = channels // head_count
    split_shape = projected.shape[:3] + (head_count, head_size)
    queries = projected[..., :channels].reshape(split_shape).astype(jnp.float32)
    key_rows = projected[..., channels:2 * channels].reshape(split_shape).astype(jnp.float32)
    values = projected[..., 2 * channels:].reshape(split_shape).astype(jnp.float32)
    scores = jnp.einsum('rwqhd,rwkhd->rwhqk', queries, key_rows) * head_size ** (-0.5)
    layout = bias_layout(projected.shape[2])
    scores = scores + jnp.take(tables, layout, axis=2)[:, None]
    scores = jnp.where(blocked_pairs(projected.shape[2], last_rows), -1000000000.0, scores)
    row_top = lax.stop_gradient(lax.optimization_barrier(jnp.max(scores, axis=-1, keepdims=True)))
    weights = jnp.exp(scores - row_top)
    attention = (weights / lax.optimization_barrier(jnp.sum(weights, axis=-1, keepdims=True))).astype(jnp.bfloat16)
    attention = lax.optimization_barrier(attention)
    mixture = jnp.einsum('rwhqk,rwkhd->rwqhd', attention.astype(jnp.float32), values)
    return mixture.astype(jnp.bfloat16).reshape(projected.shape[:3] + (channels,))

def window_pass(win_cells, win_cot, tables, last_rows, qkv_weight, out_weight):
    channels = win_cells.shape[-1]
    cell_values = win_cells.reshape(-1, channels).astype(jnp.float32)
    normed = normalize(cell_values).astype(jnp.bfloat16)
    projected = jnp.dot(normed, qkv_weight, preferred_element_type=jnp.float32).astype(jnp.bfloat16)
    projected = lax.optimization_barrier(projected).reshape(win_cells.shape[:3] + (3 * channels,))

    def attend_here(projected_in, tables_in):
        return attend(projected_in, tables_in, last_rows)
    mixture, pullback = jax.vjp(attend_here, projected, tables)
    mixture_rows = mixture.reshape(-1, channels)
    out_rows = (cell_values + jnp.dot(mixture_rows, out_weight, preferred_element_type=jnp.float32)).astype(jnp.bfloat16)
    cot_rows = win_cot.reshape(-1, channels)
    grad_out = jnp.dot(mixture_rows.T, cot_rows, preferred_element_type=jnp.float32)
    d_mixture = jnp.dot(cot_rows, out_weight.T, preferred_element_type=jnp.float32).astype(jnp.bfloat16)
    d_projected, d_tables = pullback(d_mixture.reshape(mixture.shape))
    d_rows = d_projected.reshape(-1, 3 * channels)
    grad_qkv = jnp.dot(normed.T, d_rows, preferred_element_type=jnp.float32)
    d_normed = jnp.dot(d_rows, qkv_weight.T, preferred_element_type=jnp.float32)
    d_values = jax.vjp(normalize, cell_values)[1](d_normed)[0]
    d_cells = (d_values + cot_rows.astype(jnp.float32)).astype(jnp.bfloat16)
    return (out_rows, d_cells, grad_qkv, grad_out, d_tables)

def reference(cells, qkv_weight, out_weight, earth_bias, cotangent):
    channels = cells.shape[-1]
    columns = NLON // WW
    tokens = LEV * WH * WW

    def to_windows(field):
        rolled = jnp.roll(field, (-(WH // 2), -(WW // 2)), axis=(1, 2))
        blocked = rolled.reshape(LEV, TYPES, WH, columns, WW, channels)
        return blocked.transpose(1, 3, 0, 2, 4, 5).reshape(TYPES, columns, tokens, channels)

    def from_windows(windowed):
        blocked = windowed.reshape(TYPES, columns, LEV, WH, WW, channels)
        grid_cells = blocked.transpose(2, 0, 3, 1, 4, 5).reshape(LEV, NLAT, NLON, channels)
        return jnp.roll(grid_cells, (WH // 2, WW // 2), axis=(1, 2))
    last_rows = jnp.arange(TYPES, dtype=jnp.int32) == TYPES - 1

    def row_step(totals, row_data):
        row_cells, row_cot, row_table, row_last = row_data
        out_rows, grad_rows, part_qkv, part_out, table_grad = window_pass(row_cells[None], row_cot[None], row_table[None], row_last[None], qkv_weight, out_weight)
        return ((totals[0] + part_qkv, totals[1] + part_out), (out_rows, grad_rows, table_grad[0]))
    initial = (jnp.zeros((channels, 3 * channels), jnp.float32), jnp.zeros((channels, channels), jnp.float32))
    summed, stacked = lax.scan(row_step, initial, (to_windows(cells), to_windows(cotangent), earth_bias, last_rows))
    grad_scale = CELLS ** (-0.5)
    return (from_windows(stacked[0]), from_windows(stacked[1]), summed[0] * grad_scale, summed[1] * grad_scale, stacked[2])
```

```python
import numpy as np
import jax
import jax.numpy as jnp
from jax import lax
from jax.experimental import pallas as pl
from jax.experimental.pallas import tpu as pltpu
from jax.sharding import PartitionSpec as P

LEV = 2
WH = 6
WW = 12
TOK = LEV * WH * WW
SLABS = LEV * WH
SPAN = 2 * WW - 1
GROUP = 4
LANES = GROUP * TOK
F32 = jnp.float32
BF16 = jnp.bfloat16


def nn(a, b):
    return lax.dot_general(a, b, (((1,), (0,)), ((), ())), preferred_element_type=F32)


def nt(a, b):
    return lax.dot_general(a, b, (((1,), (1,)), ((), ())), preferred_element_type=F32)


def constants(heads):
    j1, i2, j2 = np.meshgrid(np.arange(WW), np.arange(WH), np.arange(WW), indexing="ij")
    spot = (i2 * SPAN + j1 - j2 + WW - 1).reshape(-1)
    spread = (spot[:, None] == np.arange(WH * SPAN)[None, :]).astype(np.float32)
    lane = np.arange(LANES)
    lane_col, lane_slab = lane // (SLABS * GROUP), lane // GROUP % SLABS
    token_of_lane = lane_slab * WW + lane_col
    pick = (np.arange(TOK)[:, None] == token_of_lane[None, :]).astype(np.float32)
    row_half = np.arange(TOK) // WW % WH >= WH - WH // 2
    lane_half = lane_slab % WH >= WH - WH // 2
    cross = np.where(row_half[:, None] != lane_half[None, :], -1e9, 0.0).astype(np.float32)
    return (
        jnp.asarray(spread, BF16),
        jnp.asarray(spread.T, BF16),
        jnp.asarray(pick, BF16),
        jnp.asarray(cross, F32),
    )


def window_kernel(windows, groups, scale, grad_scale, last_ref, x_ref, dy_ref, wqkv_ref, wout_ref, r_ref,
                  spread_ref, gather_ref, pick_ref, cross_ref,
                  out_ref, dx_ref, gqkv_ref, gout_ref, dr_ref,
                  bt, db, normed, mix, dproj, wt):
    c = x_ref.shape[-1]
    half = WH * WW
    blk = SLABS * GROUP
    last = last_ref[0]
    for z2 in range(LEV):
        table = r_ref[z2]
        hi = table.astype(BF16)
        rest = table - hi.astype(F32)
        mid = rest.astype(BF16)
        lo = (rest - mid.astype(F32)).astype(BF16)
        spread = spread_ref[...]
        u = nt(spread, hi) + nt(spread, mid) + nt(spread, lo)
        for g in range(groups):
            rows = jnp.concatenate(
                [u[j * half:(j + 1) * half, g * blk:(g + 1) * blk] for j in range(WW)], axis=1
            )
            keep = pl.ds(z2 * half, half)
            bt[g, keep, :] = rows + cross_ref[keep, :] * last
    row = lax.broadcasted_iota(jnp.int32, (c, c), 0)
    col = lax.broadcasted_iota(jnp.int32, (c, c), 1)
    eye = (row == col).astype(F32).astype(BF16)
    head_row = lax.broadcasted_iota(jnp.int32, (GROUP * 32, LANES), 0) // 32
    head_lane = lax.broadcasted_iota(jnp.int32, (GROUP * 32, LANES), 1) % GROUP
    mine = (head_row == head_lane).astype(F32)

    x = x_ref[...].astype(F32)
    average = jnp.mean(x, axis=-1, keepdims=True)
    centred = x - average
    spread_x = jnp.mean(centred * centred, axis=-1, keepdims=True)
    rstd = lax.rsqrt(spread_x + 1e-05)
    normed[...] = (centred * rstd).astype(BF16)
    for part in range(3):
        wt[part * c:(part + 1) * c, :] = nt(eye, wqkv_ref[:, part * c:(part + 1) * c]).astype(BF16)
    pick = pick_ref[...]
    gw = GROUP * 32

    for w in range(windows):
        at = slice(w * TOK, (w + 1) * TOK)
        here = normed[at, :]
        qkv_t = nt(wt[...], here).astype(BF16)
        kv = nn(here, wqkv_ref[:, c:]).astype(BF16)
        dm_t = nt(wout_ref[...], dy_ref[at, :]).astype(BF16)
        for g in range(groups):
            gs = slice(g * gw, (g + 1) * gw)
            k, v = kv[:, g * gw:(g + 1) * gw], kv[:, c + g * gw:c + (g + 1) * gw]
            k_t, v_t = qkv_t[c + g * gw:c + (g + 1) * gw], qkv_t[2 * c + g * gw:2 * c + (g + 1) * gw]
            q_wide = (nn(qkv_t[gs], pick) * mine).astype(BF16)
            dm_wide = (nn(dm_t[gs], pick) * mine).astype(BF16)
            s = nn(k, q_wide) * scale + bt[g]
            top = jnp.max(s, axis=0, keepdims=True)
            e = jnp.exp(s - top)
            soft = e * (1.0 / jnp.sum(e, axis=0, keepdims=True))
            a = soft.astype(BF16)
            da = nn(v, dm_wide)
            ds = soft * (da - jnp.sum(soft * da, axis=0, keepdims=True))
            if w == 0:
                db[g] = ds
            else:
                db[g] += ds
            ds = ds.astype(BF16)
            m_t = (nn(v_t, a) * mine).astype(BF16)
            mix[at, gs] = nt(pick, m_t).astype(BF16)
            dq_t = (nn(k_t, ds) * (mine * scale)).astype(BF16)
            dproj[at, gs] = nt(pick, dq_t).astype(BF16)
            dproj[at, c + g * gw:c + (g + 1) * gw] = (nt(ds, q_wide) * scale).astype(BF16)
            dproj[at, 2 * c + g * gw:2 * c + (g + 1) * gw] = nt(a, dm_wide).astype(BF16)

    for z2 in range(LEV):
        keep = slice(z2 * half, (z2 + 1) * half)
        rows = jnp.concatenate(
            [
                jnp.concatenate([db[g, keep, j * blk:(j + 1) * blk] for g in range(groups)], axis=1)
                for j in range(WW)
            ],
            axis=0,
        ).astype(BF16)
        dr_ref[z2] = nn(gather_ref[...], rows)
    out_ref[...] = (x + nn(mix[...], wout_ref[...])).astype(BF16)
    gout_ref[...] = nn(nt(eye, mix[...]).astype(BF16), dy_ref[...]) * grad_scale
    gqkv_ref[...] = nn(nt(eye, normed[...]).astype(BF16), dproj[...]) * grad_scale
    dn = nt(dproj[...], wqkv_ref[...])
    n = centred * rstd
    dx = (dn - jnp.mean(dn, axis=-1, keepdims=True) - n * jnp.mean(dn * n, axis=-1, keepdims=True)) * rstd
    dx_ref[...] = (dx + dy_ref[...].astype(F32)).astype(BF16)


def window_pass(x, dy, qkv_weight, out_weight, table, last, cells_total):
    rows, c = x.shape
    windows = rows // TOK
    heads = table.shape[0]
    groups = heads // GROUP
    spread, gather, pick, cross = constants(heads)
    table = table.reshape(groups, GROUP, LEV, LEV, WH, WH * SPAN)
    table = table.transpose(3, 0, 2, 4, 1, 5).reshape(LEV, heads * SLABS, WH * SPAN)
    kernel = lambda *refs: window_kernel(
        windows, groups, (c // heads) ** -0.5, cells_total ** -0.5, *refs
    )
    vmem = pl.BlockSpec(memory_space=pltpu.VMEM)
    out, dx, gqkv, gout, dr = pl.pallas_call(
        kernel,
        out_shape=(
            jax.ShapeDtypeStruct((rows, c), BF16),
            jax.ShapeDtypeStruct((rows, c), BF16),
            jax.ShapeDtypeStruct((c, 3 * c), F32),
            jax.ShapeDtypeStruct((c, c), F32),
            jax.ShapeDtypeStruct((LEV, WH * SPAN, heads * SLABS), F32),
        ),
        in_specs=[pl.BlockSpec(memory_space=pltpu.SMEM)] + [vmem] * 9,
        out_specs=(vmem,) * 5,
        scratch_shapes=[
            pltpu.VMEM((groups, TOK, LANES), F32),
            pltpu.VMEM((groups, TOK, LANES), F32),
            pltpu.VMEM((rows, c), BF16),
            pltpu.VMEM((rows, c), BF16),
            pltpu.VMEM((rows, 3 * c), BF16),
            pltpu.VMEM((3 * c, c), BF16),
        ],
        compiler_params=pltpu.CompilerParams(vmem_limit_bytes=48 * 1024 * 1024),
        cost_estimate=pl.CostEstimate(flops=5_500_000_000, bytes_accessed=6_000_000, transcendentals=800_000),
    )(last, x, dy, qkv_weight, out_weight, table, spread, gather, pick, cross)
    return out, dx, gqkv, gout, dr


def table_grad(dr, heads):
    groups = heads // GROUP
    dr = dr.reshape(LEV, WH * SPAN, groups, LEV, WH, GROUP)
    return dr.transpose(2, 5, 3, 0, 4, 1).reshape(1, heads, LEV * LEV * WH * WH * SPAN)


def passed_along(block, axis, distance):
    devices = range(lax.axis_size(axis))
    route = [((i - distance) % len(devices), i) for i in devices]
    return lax.ppermute(block, axis, route)


def on_device(cells, qkv_weight, out_weight, earth_bias, cotangent):
    levels, lat_rows, lon_cols, channels = cells.shape
    half_rows = WH // 2
    half_cols = WW // 2
    rim_cells = passed_along(
        jnp.stack([cells[:, :, :half_cols], cotangent[:, :, :half_cols]]), "lon", -1
    )
    fields = jnp.concatenate(
        [jnp.stack([cells[:, :, half_cols:], cotangent[:, :, half_cols:]]), rim_cells], axis=3
    )
    rim_cells = passed_along(fields[:, :, :half_rows], "lat", -1)
    fields = jnp.concatenate([fields[:, :, half_rows:], rim_cells], axis=2)
    cols_here = lon_cols // WW
    windowed = fields.reshape(2, levels, WH, cols_here, WW, channels)
    windowed = windowed.transpose(0, 3, 1, 2, 4, 5).reshape(2, cols_here * TOK, channels)
    last = (lax.axis_index("lat") == lax.axis_size("lat") - 1).astype(F32).reshape(1)
    cell_count = levels * lat_rows * lon_cols * lax.axis_size("lat") * lax.axis_size("lon")
    out_rows, d_cells, grad_qkv, grad_out, dr = window_pass(
        windowed[0], windowed[1], qkv_weight, out_weight, earth_bias[0], last, cell_count
    )
    grad_qkv, grad_out = lax.psum((grad_qkv, grad_out), ("lon", "lat"))
    grad_tables = table_grad(lax.psum(dr, "lon"), earth_bias.shape[1])
    results = jnp.stack([out_rows, d_cells]).reshape(2, cols_here, levels, WH, WW, channels)
    results = results.transpose(0, 2, 3, 1, 4, 5).reshape(2, levels, lat_rows, lon_cols, channels)
    rim_cells = passed_along(results[:, :, lat_rows - half_rows :], "lat", 1)
    results = jnp.concatenate([rim_cells, results[:, :, : lat_rows - half_rows]], axis=2)
    rim_cells = passed_along(results[:, :, :, lon_cols - half_cols :], "lon", 1)
    results = jnp.concatenate([rim_cells, results[:, :, :, : lon_cols - half_cols]], axis=3)
    return (results[0], results[1], grad_qkv, grad_out, grad_tables)


def solution(mesh):
    grid = P(None, "lat", "lon", None)
    return jax.shard_map(
        on_device,
        mesh=mesh,
        in_specs=(grid, P(), P(), P("lat", None, None), grid),
        out_specs=(grid, grid, P(), P(), P("lat", None, None)),
        check_vma=False,
    )
```

```python
import functools

import numpy as np
import jax
import jax.numpy as jnp
from jax import lax
from jax.experimental import pallas as pl
from jax.experimental.pallas import tpu as pltpu
from jax.sharding import PartitionSpec as P

LEV = 2
WH = 6
WW = 12
TOK = LEV * WH * WW
SLABS = LEV * WH
SPAN = 2 * WW - 1
GROUP = 4
HEAD = 32
LANES = GROUP * TOK
WINDOWS = 3
ROWS = WINDOWS * TOK
COLS = WINDOWS * WW
PITCH = 48
RIMS = ((0, 208), (208, 48), (256, 48))
RIM = 304
TILES = 96
BIAS_TILES = 32
F32 = jnp.float32
BF16 = jnp.bfloat16
MESH = pl.DeviceIdType.MESH


def nn(a, b):
    return lax.dot_general(a, b, (((1,), (0,)), ((), ())), preferred_element_type=F32)


def nt(a, b):
    return lax.dot_general(a, b, (((1,), (1,)), ((), ())), preferred_element_type=F32)


def constants():
    j1, i2, j2 = np.meshgrid(np.arange(WW), np.arange(WH), np.arange(WW), indexing="ij")
    spot = (i2 * SPAN + j1 - j2 + WW - 1).reshape(-1)
    spread = (spot[:, None] == np.arange(WH * SPAN)[None, :]).astype(np.float32)
    gather = np.zeros((144, spread.shape[0]), np.float32)
    gather[: WH * SPAN] = spread.T
    lane = np.arange(LANES)
    lane_col, lane_slab = lane // (SLABS * GROUP), lane // GROUP % SLABS
    token_of_lane = lane_slab * WW + lane_col
    pick = (np.arange(TOK)[:, None] == token_of_lane[None, :]).astype(np.float32)
    row_half = np.arange(TOK) // WW % WH >= WH - WH // 2
    lane_half = lane_slab % WH >= WH - WH // 2
    cross = np.where(row_half[:, None] != lane_half[None, :], -1e9, 0.0).astype(np.float32)
    own = np.zeros((ROWS, SLABS * PITCH), np.float32)
    rim = np.zeros((ROWS, RIM), np.float32)
    send = np.zeros((RIM, SLABS * PITCH), np.float32)
    h = WH // 2
    for w in range(WINDOWS):
        for z in range(LEV):
            for i in range(WH):
                for j in range(WW):
                    t = w * TOK + (z * WH + i) * WW + j
                    col = WW // 2 + w * WW + j
                    below, beside = i >= h, col >= COLS
                    row, k = ((i - h) if below else (i + h)), i % h
                    slab = (z * WH + row) * PITCH + col % COLS
                    if not below and not beside:
                        own[t, slab] = 1
                        continue
                    if beside:
                        at = (256 if below else 208) + z * 18 + k * 6 + j - 6
                    elif w == WINDOWS - 1:
                        at = 160 + z * 18 + k * 6 + j
                    else:
                        at = 80 * w + z * 36 + k * 12 + j
                    rim[t, at] = 1
                    send[at, slab] = 1
    bf = lambda a: jnp.asarray(np.ascontiguousarray(a), BF16)
    return (
        bf(spread), bf(gather), bf(pick), jnp.asarray(cross, F32),
        bf(own), bf(rim), bf(send), bf(own.T), bf(rim.T), bf(send.T),
    )


N_IN = 15


def body(lon_size, lat_size, groups, scale, grad_scale, *refs):
    (cells_h, cot_h, wqkv_h, wout_h, r_h) = refs[:5]
    consts_h = refs[5:N_IN]
    (out_ref, dx_ref, gqkv_ref, gout_ref, dr_ref) = refs[N_IN:N_IN + 5]
    (cells_v, cot_v, wqkv_ref, wout_ref, r_ref,
     spread_ref, gather_ref, pick_ref, cross_ref, own_ref, rim_ref, send_ref, ownt_ref, rimt_ref, sendt_ref,
     load_sem, slab, rim_snd, rim_in, bt, db, x_w, dy_w, normed, normed_t, mix, dproj, wt, ow, rim_osnd, rim_out,
     gb, crecv, xs, xrecv, zbuf, fin, bb, bcrecv, bs, brecv, bfin,
     halo_sem, core_sem, xy_sem, z_sem, ag_sem, fwd_sem, bcore_sem, bxy_sem, bag_sem, bfwd_sem) = refs[N_IN + 5:]
    c = wout_ref.shape[0]
    ny, nz = lon_size // 4, lat_size // 2
    nxy, nb = 4 * ny, 2 * ny
    half = WH * WW
    blk = SLABS * GROUP
    gw = GROUP * HEAD

    lon, lat = lax.axis_index("lon"), lax.axis_index("lat")
    core, x_lo, y = lon % 2, lon // 2 % 2, lon // 4
    x_hi, z = lat // nz, lat % nz
    p = y * 4 + x_hi * 2 + x_lo
    b = y * 2 + x_lo
    other = 1 - core

    def dev(lon_at, lat_at):
        return {"lon": lon_at, "lat": lat_at}

    sibling = dev(lon + 1 - 2 * core, lat)

    def xy_at(o):
        q = (p + o) % nxy
        return q, dev((q // 4 * 2 + q % 2) * 2 + core, q // 2 % 2 * nz + z)

    def b_at(o):
        q = (b + o) % nb
        return q, dev(q * 2 + core, lat)

    def z_at(o):
        q = (z + o) % nz
        return q, dev(lon, x_hi * nz + q)

    lon_prev, lon_next = (lon + lon_size - 1) % lon_size, (lon + 1) % lon_size
    lat_prev, lat_next = (lat + lat_size - 1) % lat_size, (lat + 1) % lat_size
    back = (dev(lon, lat_prev), dev(lon_prev, lat), dev(lon_prev, lat_prev))
    ahead = (dev(lon, lat_next), dev(lon_next, lat), dev(lon_next, lat_next))

    def remote(src, dst, send_sem, recv_sem, device):
        return pltpu.make_async_remote_copy(
            src_ref=src, dst_ref=dst, send_sem=send_sem, recv_sem=recv_sem, device_id=device, device_id_type=MESH
        )

    dsts = (cells_v, cot_v, send_ref, r_ref, spread_ref, cross_ref, wqkv_ref, wout_ref, own_ref, rim_ref, pick_ref,
            gather_ref, ownt_ref, rimt_ref, sendt_ref)
    srcs = (cells_h, cot_h, consts_h[6], r_h, consts_h[0], consts_h[3], wqkv_h, wout_h, consts_h[4], consts_h[5],
            consts_h[2], consts_h[1], consts_h[7], consts_h[8], consts_h[9])
    loads = [pltpu.make_async_copy(s, d, load_sem.at[i]) for i, (s, d) in enumerate(zip(srcs, dsts))]
    for load in loads:
        load.start()

    barrier = pltpu.get_barrier_semaphore()

    def greet(device):
        pl.semaphore_signal(barrier, inc=1, device_id=device, device_id_type=MESH)

    for device in back + ahead + (sibling,):
        greet(device)

    @pl.loop(1, nxy)
    def _(o):
        greet(xy_at(o)[1])

    @pl.loop(1, nz)
    def _(o):
        greet(z_at(o)[1])

    slab[...] = jnp.zeros_like(slab)
    for f in range(2):
        loads[f].wait()
        src = (cells_v, cot_v)[f]
        for s in range(SLABS):
            slab[f, s * PITCH:s * PITCH + COLS, :] = src[s // WH, s % WH]
    loads[2].wait()
    for f in range(2):
        rim_snd[f] = nn(send_ref[...], slab[f]).astype(BF16)
    pl.semaphore_wait(barrier, 7 + (nxy - 1) + (nz - 1))

    def rim_copies(snd, rcv, devices, base):
        return [
            remote(
                snd.at[f, pl.ds(at, size)], rcv.at[f, pl.ds(at, size)],
                halo_sem.at[0, base + f * 3 + k], halo_sem.at[1, base + f * 3 + k], devices[k],
            )
            for f in range(2)
            for k, (at, size) in enumerate(RIMS)
        ]

    rims_in = rim_copies(rim_snd, rim_in, back, 0)
    rims_out = rim_copies(rim_osnd, rim_out, ahead, 6)
    for copy in rims_in:
        copy.start()

    for load in loads[3:6]:
        load.wait()
    last = (lat == lat_size - 1).astype(F32)
    for z2 in range(LEV):
        table = r_ref[z2]
        hi = table.astype(BF16)
        rest = table - hi.astype(F32)
        mid = rest.astype(BF16)
        lo = (rest - mid.astype(F32)).astype(BF16)
        spread = spread_ref[...]
        u = nt(spread, hi) + nt(spread, mid) + nt(spread, lo)
        for g in range(groups):
            rows = jnp.concatenate(
                [u[j * half:(j + 1) * half, g * blk:(g + 1) * blk] for j in range(WW)], axis=1
            )
            keep = pl.ds(z2 * half, half)
            bt[g, keep, :] = rows + cross_ref[keep, :] * last
    row = lax.broadcasted_iota(jnp.int32, (c, c), 0)
    col = lax.broadcasted_iota(jnp.int32, (c, c), 1)
    eye = (row == col).astype(F32).astype(BF16)
    head_row = lax.broadcasted_iota(jnp.int32, (gw, LANES), 0) // HEAD
    head_lane = lax.broadcasted_iota(jnp.int32, (gw, LANES), 1) % GROUP
    mine = (head_row == head_lane).astype(F32)
    for load in loads[6:]:
        load.wait()
    for part in range(3):
        wt[part * c:(part + 1) * c, :] = nt(eye, wqkv_ref[:, part * c:(part + 1) * c]).astype(BF16)
    pick = pick_ref[...]

    for copy in rims_in:
        copy.wait()
    x_w[...] = (nn(own_ref[...], slab[0]) + nn(rim_ref[...], rim_in[0])).astype(BF16)
    dy_w[...] = (nn(own_ref[...], slab[1]) + nn(rim_ref[...], rim_in[1])).astype(BF16)
    x = x_w[...].astype(F32)
    average = jnp.mean(x, axis=-1, keepdims=True)
    centred = x - average
    variance = jnp.mean(centred * centred, axis=-1, keepdims=True)
    rstd = lax.rsqrt(variance + 1e-05)
    normed[...] = (centred * rstd).astype(BF16)
    normed_t[...] = nt(eye, normed[...]).astype(BF16)

    def unit(g, w):
        at = slice(w * TOK, (w + 1) * TOK)
        gs = slice(g * gw, (g + 1) * gw)
        cols = [slice(part * c + g * gw, part * c + (g + 1) * gw) for part in range(3)]
        here = normed[at, :]
        q_t, k_t, v_t = [nt(wt[cols[part], :], here).astype(BF16) for part in range(3)]
        k, v = [nn(here, wqkv_ref[:, cols[part]]).astype(BF16) for part in (1, 2)]
        dm_t = nt(wout_ref[gs, :], dy_w[at, :]).astype(BF16)
        q_wide = (nn(q_t, pick) * mine).astype(BF16)
        dm_wide = (nn(dm_t, pick) * mine).astype(BF16)
        s = nn(k, q_wide) * scale + bt[g]
        top = jnp.max(s, axis=0, keepdims=True)
        e = jnp.exp(s - top)
        soft = e * (1.0 / jnp.sum(e, axis=0, keepdims=True))
        a = soft.astype(BF16)
        da = nn(v, dm_wide)
        ds = soft * (da - jnp.sum(soft * da, axis=0, keepdims=True))
        if w == 0:
            db[g] = ds
        else:
            db[g] += ds
        ds = ds.astype(BF16)
        m_t = (nn(v_t, a) * mine).astype(BF16)
        mix[at, gs] = nt(pick, m_t).astype(BF16)
        dq_t = (nn(k_t, ds) * (mine * scale)).astype(BF16)
        dproj[at, cols[0]] = nt(pick, dq_t).astype(BF16)
        dproj[at, cols[1]] = (nt(ds, q_wide) * scale).astype(BF16)
        dproj[at, cols[2]] = nt(a, dm_wide).astype(BF16)

    share = TILES // 2 // nxy

    def put(g, t, value):
        gb[g, t // (TILES // 2), t % (TILES // 2) // share, t % share] = value.astype(BF16)

    def weight_grads(g):
        for part in range(3):
            grad = nn(normed_t[...], dproj[:, part * c + g * gw:part * c + (g + 1) * gw]) * grad_scale
            for r in range(24):
                put(g, part * 24 + r, grad[r * 16:(r + 1) * 16])
        mix_t = nt(eye[:gw, :gw], mix[:, g * gw:(g + 1) * gw]).astype(BF16)
        grad = nn(mix_t, dy_w[...]) * grad_scale
        for k in range(3):
            for r in range(8):
                put(g, 72 + k * 8 + r, grad[r * 16:(r + 1) * 16, k * 128:(k + 1) * 128])

    def core_copy(g):
        return remote(gb.at[g, other], crecv.at[g], core_sem.at[0, g], core_sem.at[1, g], sibling)

    def xy_copy(g, o):
        q, device = xy_at(o)
        return remote(xs.at[g, q], xrecv.at[g, o], xy_sem.at[0, g, o], xy_sem.at[1, g, o], device)

    def z_copy(g, o):
        return remote(zbuf.at[g, z], zbuf.at[g, z], z_sem.at[0, g, o], z_sem.at[1, g, o], z_at(o)[1])

    def ag_copy(g, o):
        mine_at = fin.at[g, core, p]
        return remote(mine_at, mine_at, ag_sem.at[0, g, o], ag_sem.at[1, g, o], xy_at(o)[1])

    def fwd_copy(g, o):
        from_at = fin.at[g, core, (p + nxy - o) % nxy]
        return remote(from_at, from_at, fwd_sem.at[0, g, o], fwd_sem.at[1, g, o], sibling)

    def each(first, count, act):
        pl.loop(first, count)(act)

    def stage_core(g):
        core_copy(g).start()

    def stage_xy(g):
        core_copy(g).wait()
        xs[g] = (gb[g, core].astype(F32) + crecv[g].astype(F32)).astype(BF16)
        each(1, nxy, lambda o: xy_copy(g, o).start())

    def stage_z(g):
        each(1, nxy, lambda o: xy_copy(g, o).wait())
        total = xs[g, p].astype(F32)
        for o in range(1, nxy):
            total += xrecv[g, o].astype(F32)
        zbuf[g, z] = total.astype(BF16)
        each(1, nz, lambda o: z_copy(g, o).start())

    def z_recv(g, o):
        from_at = zbuf.at[g, (z + nz - o) % nz]
        return remote(from_at, from_at, z_sem.at[0, g, o], z_sem.at[1, g, o], z_at(o)[1])

    def stage_ag(g):
        each(1, nz, lambda o: z_copy(g, o).wait_send())
        each(1, nz, lambda o: z_recv(g, o).wait_recv())
        total = zbuf[g, 0].astype(F32)
        for k in range(1, nz):
            total += zbuf[g, k].astype(F32)
        fin[g, core, p] = total.astype(BF16)
        each(1, nxy, lambda o: ag_copy(g, o).start())
        fwd_copy(g, 0).start()

    def ag_recv(g, o):
        from_at = fin.at[g, core, (p + nxy - o) % nxy]
        return remote(from_at, from_at, ag_sem.at[0, g, o], ag_sem.at[1, g, o], xy_at(o)[1])

    def fwd_recv(g, o):
        from_at = fin.at[g, other, (p + nxy - o) % nxy]
        return remote(from_at, from_at, fwd_sem.at[0, g, o], fwd_sem.at[1, g, o], sibling)

    def stage_fwd(g):
        def pass_on(o):
            ag_recv(g, o).wait_recv()
            fwd_copy(g, o).start()

        each(1, nxy, pass_on)

    def stage_end(g):
        each(1, nxy, lambda o: ag_copy(g, o).wait_send())
        each(0, nxy, lambda o: fwd_copy(g, o).wait_send())
        each(0, nxy, lambda o: fwd_recv(g, o).wait_recv())

        def get(t):
            return fin[g, t // (TILES // 2), t % (TILES // 2) // share, t % share].astype(F32)

        for part in range(3):
            for r in range(24):
                gqkv_ref[r * 16:(r + 1) * 16, part * c + g * gw:part * c + (g + 1) * gw] = get(part * 24 + r)
        for k in range(3):
            for r in range(8):
                gout_ref[g * gw + r * 16:g * gw + (r + 1) * 16, k * 128:(k + 1) * 128] = get(72 + k * 8 + r)

    bshare = BIAS_TILES // 2 // nb

    def bcore_copy():
        return remote(bb.at[other], bcrecv, bcore_sem.at[0], bcore_sem.at[1], sibling)

    def bxy_copy(o):
        q, device = b_at(o)
        return remote(bs.at[q], brecv.at[o], bxy_sem.at[0, o], bxy_sem.at[1, o], device)

    def bag_copy(o):
        at = bfin.at[core, b]
        return remote(at, at, bag_sem.at[0, o], bag_sem.at[1, o], b_at(o)[1])

    def bag_recv(o):
        at = bfin.at[core, (b + nb - o) % nb]
        return remote(at, at, bag_sem.at[0, o], bag_sem.at[1, o], b_at(o)[1])

    def bfwd_copy(o):
        at = bfin.at[core, (b + nb - o) % nb]
        return remote(at, at, bfwd_sem.at[0, o], bfwd_sem.at[1, o], sibling)

    def bfwd_recv(o):
        at = bfin.at[other, (b + nb - o) % nb]
        return remote(at, at, bfwd_sem.at[0, o], bfwd_sem.at[1, o], sibling)

    def bias_core():
        rows = jnp.concatenate(
            [
                jnp.concatenate(
                    [
                        db[g, z2 * half:(z2 + 1) * half, j * blk:(j + 1) * blk]
                        for z2 in range(LEV)
                        for g in range(groups)
                    ]
                    + [jnp.zeros((half, 96), F32)],
                    axis=1,
                )
                for j in range(WW)
            ],
            axis=0,
        ).astype(BF16)
        dr = nn(gather_ref[...], rows).astype(BF16)
        for t in range(BIAS_TILES):
            k, r = t // 9, t % 9
            tile = dr[r * 16:(r + 1) * 16, k * 128:(k + 1) * 128] if k < 3 else jnp.zeros((16, 128), BF16)
            bb[t // 16, t % 16 // bshare, t % bshare] = tile
        bcore_copy().start()

    def bias_xy():
        bcore_copy().wait()
        bs[...] = (bb[core].astype(F32) + bcrecv[...].astype(F32)).astype(BF16)
        each(1, nb, lambda o: bxy_copy(o).start())

    def bias_ag():
        each(1, nb, lambda o: bxy_copy(o).wait())
        total = bs[b].astype(F32)
        for o in range(1, nb):
            total += brecv[o].astype(F32)
        bfin[core, b] = total.astype(BF16)
        each(1, nb, lambda o: bag_copy(o).start())
        bfwd_copy(0).start()

    def bias_fwd():
        def pass_on(o):
            bag_recv(o).wait_recv()
            bfwd_copy(o).start()

        each(1, nb, pass_on)

    def bias_end():
        each(1, nb, lambda o: bag_copy(o).wait_send())
        each(0, nb, lambda o: bfwd_copy(o).wait_send())
        each(0, nb, lambda o: bfwd_recv(o).wait_recv())
        for t in range(27):
            k, r = t // 9, t % 9
            dr_ref[r * 16:(r + 1) * 16, k * 128:(k + 1) * 128] = bfin[
                t // 16, t % 16 // bshare, t % bshare
            ].astype(F32)

    stages = (stage_core, stage_xy, stage_z, stage_ag, stage_fwd, stage_end)
    queue = []

    def advance():
        for item in list(queue):
            g, done = item
            stages[done](g)
            item[1] += 1
            if item[1] == len(stages):
                queue.remove(item)

    for g in range(groups):
        for w in range(WINDOWS):
            unit(g, w)
            advance()
        weight_grads(g)
        queue.append([g, 0])
        advance()

    bias_core()
    ow[0] = (x + nn(mix[...], wout_ref[...])).astype(BF16)
    rim_osnd[0] = nn(rimt_ref[...], ow[0]).astype(BF16)
    for copy in rims_out[:3]:
        copy.start()
    advance()
    dn = nt(dproj[...], wqkv_ref[...])
    n = centred * rstd
    dx = (dn - jnp.mean(dn, axis=-1, keepdims=True) - n * jnp.mean(dn * n, axis=-1, keepdims=True)) * rstd
    ow[1] = (dx + dy_w[...].astype(F32)).astype(BF16)
    rim_osnd[1] = nn(rimt_ref[...], ow[1]).astype(BF16)
    for copy in rims_out[3:]:
        copy.start()
    bias_xy()
    advance()

    def finish(f, ref):
        for copy in rims_out[3 * f:3 * f + 3]:
            copy.wait()
        full = (nn(ownt_ref[...], ow[f]) + nn(sendt_ref[...], rim_out[f])).astype(BF16)
        for s in range(SLABS):
            ref[s // WH, s % WH] = full[s * PITCH:s * PITCH + COLS]

    finish(0, out_ref)
    bias_ag()
    advance()
    finish(1, dx_ref)
    bias_fwd()
    advance()
    bias_end()
    while queue:
        advance()


def fused(cells, cot, qkv_weight, out_weight, table, lon_size, lat_size, cells_total):
    c = out_weight.shape[0]
    heads = table.shape[0]
    groups = heads // GROUP
    consts = constants()
    table = table.reshape(groups, GROUP, LEV, LEV, WH, WH * SPAN)
    table = table.transpose(3, 0, 2, 4, 1, 5).reshape(LEV, heads * SLABS, WH * SPAN)
    ins = (cells, cot, qkv_weight, out_weight, table) + consts
    ny, nz = lon_size // 4, lat_size // 2
    nxy, nb = 4 * ny, 2 * ny
    share, bshare = TILES // 2 // nxy, BIAS_TILES // 2 // nb
    vm = pltpu.VMEM
    dma = pltpu.SemaphoreType.DMA
    scratch = [vm(a.shape, a.dtype) for a in ins] + [
        dma((len(ins),)),
        vm((2, SLABS * PITCH, c), BF16),
        vm((2, RIM, c), BF16),
        vm((2, RIM, c), BF16),
        vm((groups, TOK, LANES), F32),
        vm((groups, TOK, LANES), F32),
        vm((ROWS, c), BF16),
        vm((ROWS, c), BF16),
        vm((ROWS, c), BF16),
        vm((c, ROWS), BF16),
        vm((ROWS, c), BF16),
        vm((ROWS, 3 * c), BF16),
        vm((3 * c, c), BF16),
        vm((2, ROWS, c), BF16),
        vm((2, RIM, c), BF16),
        vm((2, RIM, c), BF16),
        vm((groups, 2, nxy, share, 16, 128), BF16),
        vm((groups, nxy, share, 16, 128), BF16),
        vm((groups, nxy, share, 16, 128), BF16),
        vm((groups, nxy, share, 16, 128), BF16),
        vm((groups, nz, share, 16, 128), BF16),
        vm((groups, 2, nxy, share, 16, 128), BF16),
        vm((2, nb, bshare, 16, 128), BF16),
        vm((nb, bshare, 16, 128), BF16),
        vm((nb, bshare, 16, 128), BF16),
        vm((nb, bshare, 16, 128), BF16),
        vm((2, nb, bshare, 16, 128), BF16),
        dma((2, 12)),
        dma((2, groups)),
        dma((2, groups, nxy)),
        dma((2, groups, nz)),
        dma((2, groups, nxy)),
        dma((2, groups, nxy)),
        dma((2,)),
        dma((2, nb)),
        dma((2, nb)),
        dma((2, nb)),
    ]
    kernel = functools.partial(
        body, lon_size, lat_size, groups, (c // heads) ** -0.5, cells_total ** -0.5
    )
    out_shape = (
        jax.ShapeDtypeStruct(cells.shape, BF16),
        jax.ShapeDtypeStruct(cells.shape, BF16),
        jax.ShapeDtypeStruct((c, 3 * c), F32),
        jax.ShapeDtypeStruct((c, c), F32),
        jax.ShapeDtypeStruct((144, 384), F32),
    )
    return pl.pallas_call(
        kernel,
        out_shape=out_shape,
        in_specs=[pl.BlockSpec(memory_space=pl.ANY)] * len(ins),
        out_specs=(pl.BlockSpec(memory_space=pltpu.VMEM),) * len(out_shape),
        scratch_shapes=scratch,
        compiler_params=pltpu.CompilerParams(
            vmem_limit_bytes=60 * 1024 * 1024, collective_id=0, has_side_effects=True
        ),
        cost_estimate=pl.CostEstimate(flops=6_000_000_000, bytes_accessed=10_000_000, transcendentals=800_000),
    )(*ins)


def on_device(cells, qkv_weight, out_weight, earth_bias, cotangent):
    lon_size, lat_size = lax.axis_size("lon"), lax.axis_size("lat")
    heads = earth_bias.shape[1]
    cells_total = LEV * cells.shape[1] * cells.shape[2] * lon_size * lat_size
    out, dx, gqkv, gout, dr = fused(
        cells, cotangent, qkv_weight, out_weight, earth_bias[0], lon_size, lat_size, cells_total
    )
    dr = dr[: WH * SPAN, : 2 * heads * SLABS].reshape(WH * SPAN, LEV, heads // GROUP, LEV, WH, GROUP)
    dr = dr.transpose(2, 5, 3, 1, 4, 0).reshape(earth_bias.shape)
    return out, dx, gqkv, gout, dr


def solution(mesh):
    grid = P(None, "lat", "lon", None)
    return jax.shard_map(
        on_device,
        mesh=mesh,
        in_specs=(grid, P(), P(), P("lat", None, None), grid),
        out_specs=(grid, grid, P(), P(), P("lat", None, None)),
        check_vma=False,
    )
```

```python
import functools

import numpy as np
import jax
import jax.numpy as jnp
from jax import lax
from jax.experimental import pallas as pl
from jax.experimental.pallas import tpu as pltpu
from jax.sharding import PartitionSpec as P

LEV = 2
WH = 6
WW = 12
TOK = LEV * WH * WW
SLABS = LEV * WH
SPAN = 2 * WW - 1
GROUP = 4
HEAD = 32
LANES = GROUP * TOK
WINDOWS = 3
ROWS = WINDOWS * TOK
COLS = WINDOWS * WW
PITCH = 48
RIMS = ((0, 208), (208, 48), (256, 48))
RIM = 304
TILES = 96
BIAS_TILES = 32
CHUNKS = ((0, 1), (2,))
X_HI = 2
F32 = jnp.float32
BF16 = jnp.bfloat16
MESH = pl.DeviceIdType.MESH


def nn(a, b):
    return lax.dot_general(a, b, (((1,), (0,)), ((), ())), preferred_element_type=F32)


def nt(a, b):
    return lax.dot_general(a, b, (((1,), (1,)), ((), ())), preferred_element_type=F32)


def constants():
    j1, i2, j2 = np.meshgrid(np.arange(WW), np.arange(WH), np.arange(WW), indexing="ij")
    spot = (i2 * SPAN + j1 - j2 + WW - 1).reshape(-1)
    spread = (spot[:, None] == np.arange(WH * SPAN)[None, :]).astype(np.float32)
    gather = np.zeros((144, spread.shape[0]), np.float32)
    gather[: WH * SPAN] = spread.T
    lane = np.arange(LANES)
    lane_col, lane_slab = lane // (SLABS * GROUP), lane // GROUP % SLABS
    token_of_lane = lane_slab * WW + lane_col
    pick = (np.arange(TOK)[:, None] == token_of_lane[None, :]).astype(np.float32)
    row_half = np.arange(TOK) // WW % WH >= WH - WH // 2
    lane_half = lane_slab % WH >= WH - WH // 2
    cross = np.where(row_half[:, None] != lane_half[None, :], -1e9, 0.0).astype(np.float32)
    own = np.zeros((ROWS, SLABS * PITCH), np.float32)
    rim = np.zeros((ROWS, RIM), np.float32)
    send = np.zeros((RIM, SLABS * PITCH), np.float32)
    h = WH // 2
    for w in range(WINDOWS):
        for z in range(LEV):
            for i in range(WH):
                for j in range(WW):
                    t = w * TOK + (z * WH + i) * WW + j
                    col = WW // 2 + w * WW + j
                    below, beside = i >= h, col >= COLS
                    row, k = ((i - h) if below else (i + h)), i % h
                    slab = (z * WH + row) * PITCH + col % COLS
                    if not below and not beside:
                        own[t, slab] = 1
                        continue
                    if beside:
                        at = (256 if below else 208) + z * 18 + k * 6 + j - 6
                    elif w == WINDOWS - 1:
                        at = 160 + z * 18 + k * 6 + j
                    else:
                        at = 80 * w + z * 36 + k * 12 + j
                    rim[t, at] = 1
                    send[at, slab] = 1
    bf = lambda a: jnp.asarray(np.ascontiguousarray(a), BF16)
    return (
        bf(spread), bf(gather), bf(pick), jnp.asarray(cross, F32),
        bf(own), bf(rim), bf(send), bf(own.T), bf(rim.T), bf(send.T),
    )


N_IN = 15


def body(lon_size, lat_size, groups, scale, grad_scale, *refs):
    (cells_h, cot_h, wqkv_h, wout_h, r_h) = refs[:5]
    consts_h = refs[5:N_IN]
    (out_ref, dx_ref, gqkv_ref, gout_ref, dr_ref) = refs[N_IN:N_IN + 5]
    (cells_v, cot_v, wqkv_ref, wout_ref, r_ref,
     spread_ref, gather_ref, pick_ref, cross_ref, own_ref, rim_ref, send_ref, ownt_ref, rimt_ref, sendt_ref,
     load_sem, slab, rim_snd, rim_in, bt, db, x_w, dy_w, normed, normed_t, mix, dproj, wt, ow, rim_osnd, rim_out,
     halo_sem, *comm) = refs[N_IN + 5:]
    chunk_refs = [comm[i * 10:i * 10 + 10] for i in range(len(CHUNKS))]
    (bb, bcrecv, bs, bxrecv, by, byrecv, bfin, b_sem) = comm[len(CHUNKS) * 10:]
    c = wout_ref.shape[0]
    n, nz = lon_size // 4, lat_size // X_HI
    half = WH * WW
    blk = SLABS * GROUP
    gw = GROUP * HEAD

    lon, lat = lax.axis_index("lon"), lax.axis_index("lat")
    core, x_lo, y = lon % 2, lon // 2 % 2, lon // 4
    x_hi, z = lat // nz, lat % nz
    x = x_hi * 2 + x_lo
    other = 1 - core
    one = jnp.where(core == 0, x, y)
    two = jnp.where(core == 0, y, x)

    def dev(lon_at, lat_at):
        return {"lon": lon_at, "lat": lat_at}

    def chip(x_at, y_at):
        return dev((y_at * 2 + x_at % 2) * 2 + core, x_at // 2 * nz + z)

    sibling = dev(lon + 1 - 2 * core, lat)
    ones, twos, zs, ys = [], [], [], []
    for o in range(1, n):
        q = (one + o) % n
        ones.append((q, chip(jnp.where(core == 0, q, x), jnp.where(core == 0, y, q)), (one + n - o) % n))
        q = (two + o) % n
        twos.append((q, chip(jnp.where(core == 0, x, q), jnp.where(core == 0, q, y)), (two + n - o) % n))
        q = (y + o) % n
        ys.append((q, chip(x, q), (y + n - o) % n))
    for o in range(1, nz):
        zs.append((dev(lon, x_hi * nz + (z + o) % nz), (z + nz - o) % nz))
    pair = dev((y * 2 + 1 - x_lo) * 2 + core, lat)

    lon_prev, lon_next = (lon + lon_size - 1) % lon_size, (lon + 1) % lon_size
    lat_prev, lat_next = (lat + lat_size - 1) % lat_size, (lat + 1) % lat_size
    back = (dev(lon, lat_prev), dev(lon_prev, lat), dev(lon_prev, lat_prev))
    ahead = (dev(lon, lat_next), dev(lon_next, lat), dev(lon_next, lat_next))

    def remote(src, dst, send_sem, recv_sem, device):
        return pltpu.make_async_remote_copy(
            src_ref=src, dst_ref=dst, send_sem=send_sem, recv_sem=recv_sem, device_id=device, device_id_type=MESH
        )

    dsts = (cells_v, cot_v, send_ref, r_ref, spread_ref, cross_ref, wqkv_ref, wout_ref, own_ref, rim_ref, pick_ref,
            gather_ref, ownt_ref, rimt_ref, sendt_ref)
    srcs = (cells_h, cot_h, consts_h[6], r_h, consts_h[0], consts_h[3], wqkv_h, wout_h, consts_h[4], consts_h[5],
            consts_h[2], consts_h[1], consts_h[7], consts_h[8], consts_h[9])
    loads = [pltpu.make_async_copy(s, d, load_sem.at[i]) for i, (s, d) in enumerate(zip(srcs, dsts))]
    for load in loads:
        load.start()

    barrier = pltpu.get_barrier_semaphore()

    def greet(device):
        pl.semaphore_signal(barrier, inc=1, device_id=device, device_id_type=MESH)

    partners = back + ahead + (sibling, pair)
    partners += tuple(d for _, d, _ in ones + twos + ys) + tuple(d for d, _ in zs)
    for device in partners:
        greet(device)

    slab[...] = jnp.zeros_like(slab)
    for f in range(2):
        loads[f].wait()
        src = (cells_v, cot_v)[f]
        for s in range(SLABS):
            slab[f, s * PITCH:s * PITCH + COLS, :] = src[s // WH, s % WH]
    loads[2].wait()
    for f in range(2):
        rim_snd[f] = nn(send_ref[...], slab[f]).astype(BF16)
    pl.semaphore_wait(barrier, len(partners))

    def rim_copies(snd, rcv, devices, base):
        return [
            remote(
                snd.at[f, pl.ds(at, size)], rcv.at[f, pl.ds(at, size)],
                halo_sem.at[0, base + f * 3 + k], halo_sem.at[1, base + f * 3 + k], devices[k],
            )
            for f in range(2)
            for k, (at, size) in enumerate(RIMS)
        ]

    rims_in = rim_copies(rim_snd, rim_in, back, 0)
    rims_out = rim_copies(rim_osnd, rim_out, ahead, 6)
    for copy in rims_in:
        copy.start()

    for load in loads[3:6]:
        load.wait()
    last = (lat == lat_size - 1).astype(F32)
    for z2 in range(LEV):
        table = r_ref[z2]
        hi = table.astype(BF16)
        rest = table - hi.astype(F32)
        mid = rest.astype(BF16)
        lo = (rest - mid.astype(F32)).astype(BF16)
        spread = spread_ref[...]
        u = nt(spread, hi) + nt(spread, mid) + nt(spread, lo)
        for g in range(groups):
            rows = jnp.concatenate(
                [u[j * half:(j + 1) * half, g * blk:(g + 1) * blk] for j in range(WW)], axis=1
            )
            keep = pl.ds(z2 * half, half)
            bt[g, keep, :] = rows + cross_ref[keep, :] * last
    row = lax.broadcasted_iota(jnp.int32, (c, c), 0)
    col = lax.broadcasted_iota(jnp.int32, (c, c), 1)
    eye = (row == col).astype(F32).astype(BF16)
    head_row = lax.broadcasted_iota(jnp.int32, (gw, LANES), 0) // HEAD
    head_lane = lax.broadcasted_iota(jnp.int32, (gw, LANES), 1) % GROUP
    mine = (head_row == head_lane).astype(F32)
    for load in loads[6:]:
        load.wait()
    for part in range(3):
        wt[part * c:(part + 1) * c, :] = nt(eye, wqkv_ref[:, part * c:(part + 1) * c]).astype(BF16)
    pick = pick_ref[...]

    for copy in rims_in:
        copy.wait()
    x_w[...] = (nn(own_ref[...], slab[0]) + nn(rim_ref[...], rim_in[0])).astype(BF16)
    dy_w[...] = (nn(own_ref[...], slab[1]) + nn(rim_ref[...], rim_in[1])).astype(BF16)
    cells = x_w[...].astype(F32)
    average = jnp.mean(cells, axis=-1, keepdims=True)
    centred = cells - average
    variance = jnp.mean(centred * centred, axis=-1, keepdims=True)
    rstd = lax.rsqrt(variance + 1e-05)
    normed[...] = (centred * rstd).astype(BF16)
    normed_t[...] = nt(eye, normed[...]).astype(BF16)

    def unit(g, w):
        at = slice(w * TOK, (w + 1) * TOK)
        gs = slice(g * gw, (g + 1) * gw)
        cols = [slice(part * c + g * gw, part * c + (g + 1) * gw) for part in range(3)]
        here = normed[at, :]
        q_t, k_t, v_t = [nt(wt[cols[part], :], here).astype(BF16) for part in range(3)]
        k, v = [nn(here, wqkv_ref[:, cols[part]]).astype(BF16) for part in (1, 2)]
        dm_t = nt(wout_ref[gs, :], dy_w[at, :]).astype(BF16)
        q_wide = (nn(q_t, pick) * mine).astype(BF16)
        dm_wide = (nn(dm_t, pick) * mine).astype(BF16)
        s = nn(k, q_wide) * scale + bt[g]
        top = jnp.max(s, axis=0, keepdims=True)
        e = jnp.exp(s - top)
        soft = e * (1.0 / jnp.sum(e, axis=0, keepdims=True))
        a = soft.astype(BF16)
        da = nn(v, dm_wide)
        ds = soft * (da - jnp.sum(soft * da, axis=0, keepdims=True))
        if w == 0:
            db[g] = ds
        else:
            db[g] += ds
        ds = ds.astype(BF16)
        m_t = (nn(v_t, a) * mine).astype(BF16)
        mix[at, gs] = nt(pick, m_t).astype(BF16)
        dq_t = (nn(k_t, ds) * (mine * scale)).astype(BF16)
        dproj[at, cols[0]] = nt(pick, dq_t).astype(BF16)
        dproj[at, cols[1]] = (nt(ds, q_wide) * scale).astype(BF16)
        dproj[at, cols[2]] = nt(a, dm_wide).astype(BF16)

    def chunk_of(g):
        return next((i, groups_in.index(g)) for i, groups_in in enumerate(CHUNKS) if g in groups_in)

    def tile_at(g, t):
        i, k = chunk_of(g)
        t += k * TILES
        half_tiles = len(CHUNKS[i]) * TILES // 2
        share = half_tiles // (n * n)
        return i, (t // half_tiles, t % half_tiles // (n * share), t % (n * share) // share, t % share)

    def put(g, t, value):
        i, at = tile_at(g, t)
        chunk_refs[i][0][at] = value.astype(BF16)

    def weight_grads(g):
        for part in range(3):
            grad = nn(normed_t[...], dproj[:, part * c + g * gw:part * c + (g + 1) * gw]) * grad_scale
            for r in range(24):
                put(g, part * 24 + r, grad[r * 16:(r + 1) * 16])
        mix_t = nt(eye[:gw, :gw], mix[:, g * gw:(g + 1) * gw]).astype(BF16)
        grad = nn(mix_t, dy_w[...]) * grad_scale
        for k in range(3):
            for r in range(8):
                put(g, 72 + k * 8 + r, grad[r * 16:(r + 1) * 16, k * 128:(k + 1) * 128])

    class Chain:
        def __init__(self, refs):
            (self.gb, self.crecv, self.xs, self.arecv, self.ys, self.brecv, self.zbuf, self.fin,
             self.sem, self.zsem) = refs

        def copy(self, k, src, dst, device):
            return remote(src, dst, self.sem.at[0, k], self.sem.at[1, k], device)

        def core_copy(self):
            return self.copy(0, self.gb.at[other], self.crecv, sibling)

        def one_copies(self):
            return [self.copy(1 + o, self.xs.at[q], self.arecv.at[o], d) for o, (q, d, _) in enumerate(ones)]

        def two_copies(self):
            return [self.copy(4 + o, self.ys.at[q], self.brecv.at[o], d) for o, (q, d, _) in enumerate(twos)]

        def z_copies(self, here=True):
            at = [z if here else q for _, q in zs]
            return [
                remote(self.zbuf.at[at[o]], self.zbuf.at[at[o]], self.zsem.at[0, o], self.zsem.at[1, o], d)
                for o, (d, _) in enumerate(zs)
            ]

        def back_two(self, here=True):
            at = [two if here else q for _, _, q in twos]
            return [
                self.copy(7 + o, self.fin.at[core, one, at[o]], self.fin.at[core, one, at[o]], d)
                for o, (_, d, _) in enumerate(twos)
            ]

        def back_one(self, here=True):
            at = [one if here else q for _, _, q in ones]
            return [
                self.copy(10 + o, self.fin.at[core, at[o]], self.fin.at[core, at[o]], d)
                for o, (_, d, _) in enumerate(ones)
            ]

        def back_core(self, o, half_at):
            at = one if o == 0 else ones[o - 1][2]
            return self.copy(13 + o, self.fin.at[half_at, at], self.fin.at[half_at, at], sibling)

        def start(self):
            self.core_copy().start()

        def first(self):
            self.core_copy().wait()
            self.xs[...] = (self.gb[core].astype(F32) + self.crecv[...].astype(F32)).astype(BF16)
            for copy in self.one_copies():
                copy.start()

        def second(self):
            for copy in self.one_copies():
                copy.wait()
            total = self.xs[one].astype(F32)
            for o in range(n - 1):
                total += self.arecv[o].astype(F32)
            self.ys[...] = total.astype(BF16)
            for copy in self.two_copies():
                copy.start()

        def third(self):
            for copy in self.two_copies():
                copy.wait()
            total = self.ys[two].astype(F32)
            for o in range(n - 1):
                total += self.brecv[o].astype(F32)
            self.zbuf[z] = total.astype(BF16)
            for copy in self.z_copies():
                copy.start()

        def fourth(self):
            for copy in self.z_copies():
                copy.wait_send()
            for copy in self.z_copies(False):
                copy.wait_recv()
            total = self.zbuf[0].astype(F32)
            for k in range(1, nz):
                total += self.zbuf[k].astype(F32)
            self.fin[core, one, two] = total.astype(BF16)
            for copy in self.back_two():
                copy.start()

        def fifth(self):
            for copy in self.back_two():
                copy.wait_send()
            for copy in self.back_two(False):
                copy.wait_recv()
            for copy in self.back_one():
                copy.start()
            self.back_core(0, core).start()

        def sixth(self):
            for o, copy in enumerate(self.back_one(False)):
                copy.wait_recv()
                self.back_core(o + 1, core).start()

        def last(self):
            for copy in self.back_one():
                copy.wait_send()
            for o in range(n):
                self.back_core(o, core).wait_send()
                self.back_core(o, other).wait_recv()

    chains = [Chain(r) for r in chunk_refs]

    def unpack(g):
        def get(t):
            i, at = tile_at(g, t)
            return chains[i].fin[at].astype(F32)

        for part in range(3):
            for r in range(24):
                gqkv_ref[r * 16:(r + 1) * 16, part * c + g * gw:part * c + (g + 1) * gw] = get(part * 24 + r)
        for k in range(3):
            for r in range(8):
                gout_ref[g * gw + r * 16:g * gw + (r + 1) * 16, k * 128:(k + 1) * 128] = get(72 + k * 8 + r)

    bshare = BIAS_TILES // (4 * n)

    def bcopy(k, src, dst, device):
        return remote(src, dst, b_sem.at[0, k], b_sem.at[1, k], device)

    def bcore_copy():
        return bcopy(0, bb.at[other], bcrecv, sibling)

    def bx_copy():
        return bcopy(1, bs.at[1 - x_lo], bxrecv, pair)

    def by_copies():
        return [bcopy(2 + o, by.at[q], byrecv.at[o], d) for o, (q, d, _) in enumerate(ys)]

    def by_back(here=True):
        at = [y if here else q for _, _, q in ys]
        return [
            bcopy(5 + o, bfin.at[core, x_lo, at[o]], bfin.at[core, x_lo, at[o]], d)
            for o, (_, d, _) in enumerate(ys)
        ]

    def bx_back(x_at):
        return bcopy(8, bfin.at[core, x_at], bfin.at[core, x_at], pair)

    def bcore_back(half_at):
        return bcopy(9, bfin.at[half_at], bfin.at[half_at], sibling)

    def bias_core():
        rows = jnp.concatenate(
            [
                jnp.concatenate(
                    [
                        db[g, z2 * half:(z2 + 1) * half, j * blk:(j + 1) * blk]
                        for z2 in range(LEV)
                        for g in range(groups)
                    ]
                    + [jnp.zeros((half, 96), F32)],
                    axis=1,
                )
                for j in range(WW)
            ],
            axis=0,
        ).astype(BF16)
        dr = nn(gather_ref[...], rows).astype(BF16)
        for t in range(BIAS_TILES):
            k, r = t // 9, t % 9
            tile = dr[r * 16:(r + 1) * 16, k * 128:(k + 1) * 128] if k < 3 else jnp.zeros((16, 128), BF16)
            bb[bias_at(t)] = tile
        bcore_copy().start()

    def bias_at(t):
        return t // 16, t % 16 // (n * bshare), t % (n * bshare) // bshare, t % bshare

    def bias_x():
        bcore_copy().wait()
        bs[...] = (bb[core].astype(F32) + bcrecv[...].astype(F32)).astype(BF16)
        bx_copy().start()

    def bias_y():
        bx_copy().wait()
        by[...] = (bs[x_lo].astype(F32) + bxrecv[...].astype(F32)).astype(BF16)
        for copy in by_copies():
            copy.start()

    def bias_back_y():
        for copy in by_copies():
            copy.wait()
        total = by[y].astype(F32)
        for o in range(n - 1):
            total += byrecv[o].astype(F32)
        bfin[core, x_lo, y] = total.astype(BF16)
        for copy in by_back():
            copy.start()

    def bias_back_x():
        for copy in by_back():
            copy.wait_send()
        for copy in by_back(False):
            copy.wait_recv()
        bx_back(x_lo).start()

    def bias_back_core():
        bx_back(x_lo).wait_send()
        bx_back(1 - x_lo).wait_recv()
        bcore_back(core).start()

    def bias_end():
        bcore_back(core).wait_send()
        bcore_back(other).wait_recv()
        for t in range(27):
            k, r = t // 9, t % 9
            dr_ref[r * 16:(r + 1) * 16, k * 128:(k + 1) * 128] = bfin[bias_at(t)].astype(F32)

    def finish(f, ref):
        for copy in rims_out[3 * f:3 * f + 3]:
            copy.wait()
        full = (nn(ownt_ref[...], ow[f]) + nn(sendt_ref[...], rim_out[f])).astype(BF16)
        for s in range(SLABS):
            ref[s // WH, s % WH] = full[s * PITCH:s * PITCH + COLS]

    early, late = chains
    for g in (0, 1):
        for w in range(WINDOWS):
            unit(g, w)
        weight_grads(g)
    early.start()
    unit(2, 0)
    early.first()
    unit(2, 1)
    unit(2, 2)
    weight_grads(2)
    late.start()
    bias_core()
    early.second()
    ow[0] = (cells + nn(mix[...], wout_ref[...])).astype(BF16)
    rim_osnd[0] = nn(rimt_ref[...], ow[0]).astype(BF16)
    late.first()
    for copy in rims_out[:3]:
        copy.start()
    dn = nt(dproj[...], wqkv_ref[...])
    n_w = centred * rstd
    dx = (dn - jnp.mean(dn, axis=-1, keepdims=True) - n_w * jnp.mean(dn * n_w, axis=-1, keepdims=True)) * rstd
    ow[1] = (dx + dy_w[...].astype(F32)).astype(BF16)
    rim_osnd[1] = nn(rimt_ref[...], ow[1]).astype(BF16)
    late.second()
    for copy in rims_out[3:]:
        copy.start()
    bias_x()
    early.third()
    bias_y()
    late.third()
    bias_back_y()
    early.fourth()
    late.fourth()
    bias_back_x()
    early.fifth()
    late.fifth()
    bias_back_core()
    early.sixth()
    finish(0, out_ref)
    late.sixth()
    finish(1, dx_ref)
    bias_end()
    early.last()
    unpack(0)
    unpack(1)
    late.last()
    unpack(2)


def fused(cells, cot, qkv_weight, out_weight, table, lon_size, lat_size, cells_total):
    c = out_weight.shape[0]
    heads = table.shape[0]
    groups = heads // GROUP
    consts = constants()
    table = table.reshape(groups, GROUP, LEV, LEV, WH, WH * SPAN)
    table = table.transpose(3, 0, 2, 4, 1, 5).reshape(LEV, heads * SLABS, WH * SPAN)
    ins = (cells, cot, qkv_weight, out_weight, table) + consts
    n, nz = lon_size // 4, lat_size // X_HI
    bshare = BIAS_TILES // (4 * n)
    vm = pltpu.VMEM
    dma = pltpu.SemaphoreType.DMA
    scratch = [vm(a.shape, a.dtype) for a in ins] + [
        dma((len(ins),)),
        vm((2, SLABS * PITCH, c), BF16),
        vm((2, RIM, c), BF16),
        vm((2, RIM, c), BF16),
        vm((groups, TOK, LANES), F32),
        vm((groups, TOK, LANES), F32),
        vm((ROWS, c), BF16),
        vm((ROWS, c), BF16),
        vm((ROWS, c), BF16),
        vm((c, ROWS), BF16),
        vm((ROWS, c), BF16),
        vm((ROWS, 3 * c), BF16),
        vm((3 * c, c), BF16),
        vm((2, ROWS, c), BF16),
        vm((2, RIM, c), BF16),
        vm((2, RIM, c), BF16),
        dma((2, 12)),
    ]
    tile = (16, 128)
    for groups_in in CHUNKS:
        share = len(groups_in) * TILES // (2 * n * n)
        scratch += [
            vm((2, n, n, share) + tile, BF16),
            vm((n, n, share) + tile, BF16),
            vm((n, n, share) + tile, BF16),
            vm((n - 1, n, share) + tile, BF16),
            vm((n, share) + tile, BF16),
            vm((n - 1, share) + tile, BF16),
            vm((nz, share) + tile, BF16),
            vm((2, n, n, share) + tile, BF16),
            dma((2, 17)),
            dma((2, nz)),
        ]
    scratch += [
        vm((2, 2, n, bshare) + tile, BF16),
        vm((2, n, bshare) + tile, BF16),
        vm((2, n, bshare) + tile, BF16),
        vm((n, bshare) + tile, BF16),
        vm((n, bshare) + tile, BF16),
        vm((n - 1, bshare) + tile, BF16),
        vm((2, 2, n, bshare) + tile, BF16),
        dma((2, 10)),
    ]
    kernel = functools.partial(
        body, lon_size, lat_size, groups, (c // heads) ** -0.5, cells_total ** -0.5
    )
    out_shape = (
        jax.ShapeDtypeStruct(cells.shape, BF16),
        jax.ShapeDtypeStruct(cells.shape, BF16),
        jax.ShapeDtypeStruct((c, 3 * c), F32),
        jax.ShapeDtypeStruct((c, c), F32),
        jax.ShapeDtypeStruct((144, 384), F32),
    )
    return pl.pallas_call(
        kernel,
        out_shape=out_shape,
        in_specs=[pl.BlockSpec(memory_space=pl.ANY)] * len(ins),
        out_specs=(pl.BlockSpec(memory_space=pltpu.VMEM),) * len(out_shape),
        scratch_shapes=scratch,
        compiler_params=pltpu.CompilerParams(
            vmem_limit_bytes=60 * 1024 * 1024, collective_id=0, has_side_effects=True
        ),
        cost_estimate=pl.CostEstimate(flops=6_000_000_000, bytes_accessed=10_000_000, transcendentals=800_000),
    )(*ins)


def on_device(cells, qkv_weight, out_weight, earth_bias, cotangent):
    lon_size, lat_size = lax.axis_size("lon"), lax.axis_size("lat")
    heads = earth_bias.shape[1]
    cells_total = LEV * cells.shape[1] * cells.shape[2] * lon_size * lat_size
    out, dx, gqkv, gout, dr = fused(
        cells, cotangent, qkv_weight, out_weight, earth_bias[0], lon_size, lat_size, cells_total
    )
    dr = dr[: WH * SPAN, : 2 * heads * SLABS].reshape(WH * SPAN, LEV, heads // GROUP, LEV, WH, GROUP)
    dr = dr.transpose(2, 5, 3, 1, 4, 0).reshape(earth_bias.shape)
    return out, dx, gqkv, gout, dr


def solution(mesh):
    grid = P(None, "lat", "lon", None)
    return jax.shard_map(
        on_device,
        mesh=mesh,
        in_specs=(grid, P(), P(), P("lat", None, None), grid),
        out_specs=(grid, grid, P(), P(), P("lat", None, None)),
        check_vma=False,
    )
```

```python
import functools

import numpy as np
import jax
import jax.numpy as jnp
from jax import lax
from jax.experimental import pallas as pl
from jax.experimental.pallas import tpu as pltpu
from jax.sharding import PartitionSpec as P

LEV = 2
WH = 6
WW = 12
TOK = LEV * WH * WW
SLABS = LEV * WH
SPAN = 2 * WW - 1
GROUP = 4
HEAD = 32
LANES = GROUP * TOK
WINDOWS = 3
ROWS = WINDOWS * TOK
COLS = WINDOWS * WW
PITCH = 48
RIMS = ((0, 208), (208, 48), (256, 48))
RIM = 304
BIAS_TILES = 32
CHUNKS = (64, 128, 96)
X_HI = 2
F32 = jnp.float32
BF16 = jnp.bfloat16
MESH = pl.DeviceIdType.MESH


def nn(a, b):
    return lax.dot_general(a, b, (((1,), (0,)), ((), ())), preferred_element_type=F32)


def nt(a, b):
    return lax.dot_general(a, b, (((1,), (1,)), ((), ())), preferred_element_type=F32)


def constants():
    j1, i2, j2 = np.meshgrid(np.arange(WW), np.arange(WH), np.arange(WW), indexing="ij")
    spot = (i2 * SPAN + j1 - j2 + WW - 1).reshape(-1)
    spread = (spot[:, None] == np.arange(WH * SPAN)[None, :]).astype(np.float32)
    gather = np.zeros((144, spread.shape[0]), np.float32)
    gather[: WH * SPAN] = spread.T
    lane = np.arange(LANES)
    lane_col, lane_slab = lane // (SLABS * GROUP), lane // GROUP % SLABS
    token_of_lane = lane_slab * WW + lane_col
    pick = (np.arange(TOK)[:, None] == token_of_lane[None, :]).astype(np.float32)
    row_half = np.arange(TOK) // WW % WH >= WH - WH // 2
    lane_half = lane_slab % WH >= WH - WH // 2
    cross = np.where(row_half[:, None] != lane_half[None, :], -1e9, 0.0).astype(np.float32)
    own = np.zeros((ROWS, SLABS * PITCH), np.float32)
    rim = np.zeros((ROWS, RIM), np.float32)
    send = np.zeros((RIM, SLABS * PITCH), np.float32)
    h = WH // 2
    for w in range(WINDOWS):
        for z in range(LEV):
            for i in range(WH):
                for j in range(WW):
                    t = w * TOK + (z * WH + i) * WW + j
                    col = WW // 2 + w * WW + j
                    below, beside = i >= h, col >= COLS
                    row, k = ((i - h) if below else (i + h)), i % h
                    slab = (z * WH + row) * PITCH + col % COLS
                    if not below and not beside:
                        own[t, slab] = 1
                        continue
                    if beside:
                        at = (256 if below else 208) + z * 18 + k * 6 + j - 6
                    elif w == WINDOWS - 1:
                        at = 160 + z * 18 + k * 6 + j
                    else:
                        at = 80 * w + z * 36 + k * 12 + j
                    rim[t, at] = 1
                    send[at, slab] = 1
    bf = lambda a: jnp.asarray(np.ascontiguousarray(a), BF16)
    return (
        bf(spread), bf(gather), bf(pick), jnp.asarray(cross, F32),
        bf(own), bf(rim), bf(send), bf(own.T), bf(rim.T), bf(send.T),
    )


N_IN = 15


def body(lon_size, lat_size, groups, scale, grad_scale, *refs):
    (cells_h, cot_h, wqkv_h, wout_h, r_h) = refs[:5]
    consts_h = refs[5:N_IN]
    (out_ref, dx_ref, gqkv_ref, gout_ref, dr_ref) = refs[N_IN:N_IN + 5]
    (cells_v, cot_v, wqkv_ref, wout_ref, r_ref,
     spread_ref, gather_ref, pick_ref, cross_ref, own_ref, rim_ref, send_ref, ownt_ref, rimt_ref, sendt_ref,
     load_sem, slab, rim_snd, rim_in, bt, db, x_w, dy_w, normed, normed_t, mix, dproj, wt, ow, rim_osnd, rim_out,
     kv, k_ts, q_ws, soft_s, m_ts, dm_ws, dq_ts,
     halo_sem, *comm) = refs[N_IN + 5:]
    chunk_refs = [comm[i * 10:i * 10 + 10] for i in range(len(CHUNKS))]
    (bb, bcrecv, bs, bxrecv, by, byrecv, bfin, b_sem) = comm[len(CHUNKS) * 10:]
    c = wout_ref.shape[0]
    n, nz = lon_size // 4, lat_size // X_HI
    half = WH * WW
    blk = SLABS * GROUP
    gw = GROUP * HEAD

    lon, lat = lax.axis_index("lon"), lax.axis_index("lat")
    core, x_lo, y = lon % 2, lon // 2 % 2, lon // 4
    x_hi, z = lat // nz, lat % nz
    x = x_hi * 2 + x_lo
    other = 1 - core
    one = jnp.where(core == 0, x, y)
    two = jnp.where(core == 0, y, x)

    def dev(lon_at, lat_at):
        return {"lon": lon_at, "lat": lat_at}

    def chip(x_at, y_at):
        return dev((y_at * 2 + x_at % 2) * 2 + core, x_at // 2 * nz + z)

    sibling = dev(lon + 1 - 2 * core, lat)
    ones, twos, zs, ys = [], [], [], []
    for o in range(1, n):
        q = (one + o) % n
        ones.append((q, chip(jnp.where(core == 0, q, x), jnp.where(core == 0, y, q)), (one + n - o) % n))
        q = (two + o) % n
        twos.append((q, chip(jnp.where(core == 0, x, q), jnp.where(core == 0, q, y)), (two + n - o) % n))
        q = (y + o) % n
        ys.append((q, chip(x, q), (y + n - o) % n))
    for o in range(1, nz):
        zs.append((dev(lon, x_hi * nz + (z + o) % nz), (z + nz - o) % nz))
    pair = dev((y * 2 + 1 - x_lo) * 2 + core, lat)

    lon_prev, lon_next = (lon + lon_size - 1) % lon_size, (lon + 1) % lon_size
    lat_prev, lat_next = (lat + lat_size - 1) % lat_size, (lat + 1) % lat_size
    back = (dev(lon, lat_prev), dev(lon_prev, lat), dev(lon_prev, lat_prev))
    ahead = (dev(lon, lat_next), dev(lon_next, lat), dev(lon_next, lat_next))

    def remote(src, dst, send_sem, recv_sem, device):
        return pltpu.make_async_remote_copy(
            src_ref=src, dst_ref=dst, send_sem=send_sem, recv_sem=recv_sem, device_id=device, device_id_type=MESH
        )

    order = (
        (cells_h, cells_v), (consts_h[6], send_ref), (cot_h, cot_v), (r_h, r_ref), (consts_h[0], spread_ref),
        (consts_h[3], cross_ref), (wqkv_h, wqkv_ref), (consts_h[4], own_ref), (consts_h[5], rim_ref),
        (consts_h[2], pick_ref), (wout_h, wout_ref), (consts_h[8], rimt_ref), (consts_h[7], ownt_ref),
        (consts_h[9], sendt_ref), (consts_h[1], gather_ref),
    )
    loads = [pltpu.make_async_copy(s, d, load_sem.at[i]) for i, (s, d) in enumerate(order)]
    for load in loads:
        load.start()

    barrier = pltpu.get_barrier_semaphore()

    def greet(device):
        pl.semaphore_signal(barrier, inc=1, device_id=device, device_id_type=MESH)

    partners = back + ahead + (sibling, pair)
    partners += tuple(d for _, d, _ in ones + twos + ys) + tuple(d for d, _ in zs)
    for device in partners:
        greet(device)

    def rim_copies(snd, rcv, devices, base):
        return [
            remote(
                snd.at[f, pl.ds(at, size)], rcv.at[f, pl.ds(at, size)],
                halo_sem.at[0, base + f * 3 + k], halo_sem.at[1, base + f * 3 + k], devices[k],
            )
            for f in range(2)
            for k, (at, size) in enumerate(RIMS)
        ]

    rims_in = rim_copies(rim_snd, rim_in, back, 0)
    rims_out = rim_copies(rim_osnd, rim_out, ahead, 6)
    slab[...] = jnp.zeros_like(slab)
    for f, src in enumerate((cells_v, cot_v)):
        loads[2 * f].wait()
        for s in range(SLABS):
            slab[f, s * PITCH:s * PITCH + COLS, :] = src[s // WH, s % WH]
        if f == 0:
            loads[1].wait()
        rim_snd[f] = nn(send_ref[...], slab[f]).astype(BF16)
        if f == 0:
            pl.semaphore_wait(barrier, len(partners))
        for copy in rims_in[3 * f:3 * f + 3]:
            copy.start()

    for load in loads[3:6]:
        load.wait()
    last = (lat == lat_size - 1).astype(F32)
    for z2 in range(LEV):
        table = r_ref[z2]
        hi = table.astype(BF16)
        rest = table - hi.astype(F32)
        mid = rest.astype(BF16)
        lo = (rest - mid.astype(F32)).astype(BF16)
        spread = spread_ref[...]
        u = nt(spread, hi) + nt(spread, mid) + nt(spread, lo)
        for g in range(groups):
            rows = jnp.concatenate(
                [u[j * half:(j + 1) * half, g * blk:(g + 1) * blk] for j in range(WW)], axis=1
            )
            keep = pl.ds(z2 * half, half)
            bt[g, keep, :] = rows + cross_ref[keep, :] * last
    row = lax.broadcasted_iota(jnp.int32, (c, c), 0)
    col = lax.broadcasted_iota(jnp.int32, (c, c), 1)
    eye = (row == col).astype(F32).astype(BF16)
    head_row = lax.broadcasted_iota(jnp.int32, (gw, LANES), 0) // HEAD
    head_lane = lax.broadcasted_iota(jnp.int32, (gw, LANES), 1) % GROUP
    mine = (head_row == head_lane).astype(F32)
    for load in loads[6:]:
        load.wait()
    for part in range(3):
        wt[part * c:(part + 1) * c, :] = nt(eye, wqkv_ref[:, part * c:(part + 1) * c]).astype(BF16)
    pick = pick_ref[...]

    def arrive(f, ref):
        for copy in rims_in[3 * f:3 * f + 3]:
            copy.wait()
        ref[...] = (nn(own_ref[...], slab[f]) + nn(rim_ref[...], rim_in[f])).astype(BF16)

    arrive(0, x_w)
    cells = x_w[...].astype(F32)
    average = jnp.mean(cells, axis=-1, keepdims=True)
    centred = cells - average
    variance = jnp.mean(centred * centred, axis=-1, keepdims=True)
    rstd = lax.rsqrt(variance + 1e-05)
    normed[...] = (centred * rstd).astype(BF16)
    normed_t[...] = nt(eye, normed[...]).astype(BF16)

    kv[...] = nn(normed[...], wqkv_ref[:, c:]).astype(BF16)

    def at_of(w):
        return slice(w * TOK, (w + 1) * TOK)

    def g_of(g, part=0):
        return slice(part * c + g * gw, part * c + (g + 1) * gw)

    def forward(w):
        at = at_of(w)
        turned = nt(wt[...], normed[at, :]).astype(BF16)
        q_all = nn(turned[:c], pick)
        k_ts[w] = turned[c:2 * c]
        for g in range(groups):
            q_wide = (q_all[g_of(g)] * mine).astype(BF16)
            q_ws[w, g] = q_wide
            s = nn(kv[at, g_of(g)], q_wide) * scale + bt[g]
            top = jnp.max(s, axis=0, keepdims=True)
            e = jnp.exp(s - top)
            soft = e * (1.0 / jnp.sum(e, axis=0, keepdims=True))
            soft_s[w, g] = soft
            m_ts[g_of(g), :] = (nn(turned[g_of(g, 2)], soft.astype(BF16)) * mine).astype(BF16)
        mix[at, :] = nt(pick, m_ts[...]).astype(BF16)

    def widen(w):
        dm_t = nt(wout_ref[...], dy_w[at_of(w), :]).astype(BF16)
        dm_all = nn(dm_t, pick)
        for g in range(groups):
            dm_ws[w, g] = (dm_all[g_of(g)] * mine).astype(BF16)

    def backward(g, w):
        at = at_of(w)
        soft = soft_s[w, g]
        dm_wide = dm_ws[w, g]
        da = nn(kv[at, g_of(g, 1)], dm_wide)
        ds = soft * (da - jnp.sum(soft * da, axis=0, keepdims=True))
        if w == 0:
            db[g] = ds
        else:
            db[g] += ds
        ds = ds.astype(BF16)
        dq_ts[w * gw:(w + 1) * gw, :] = (nn(k_ts[w, g_of(g), :], ds) * (mine * scale)).astype(BF16)
        dproj[at, g_of(g, 1)] = (nt(ds, q_ws[w, g]) * scale).astype(BF16)
        dproj[at, g_of(g, 2)] = nt(soft.astype(BF16), dm_wide).astype(BF16)

    def tile_at(t):
        i = 0
        while t >= CHUNKS[i]:
            t -= CHUNKS[i]
            i += 1
        half_tiles = CHUNKS[i] // 2
        share = half_tiles // (n * n)
        return i, (t // half_tiles, t % half_tiles // (n * share), t % (n * share) // share, t % share)

    def put(t, value):
        i, at = tile_at(t)
        chunk_refs[i][0][at] = value.astype(BF16)

    def out_grads():
        grad = nn(nt(eye, mix[...]).astype(BF16), dy_w[...]) * grad_scale
        for k in range(3):
            for r in range(24):
                put(k * 24 + r, grad[r * 16:(r + 1) * 16, k * 128:(k + 1) * 128])

    def qkv_grads(g):
        dq = nt(pick, dq_ts[...]).astype(BF16)
        for w in range(WINDOWS):
            dproj[at_of(w), g_of(g)] = dq[:, w * gw:(w + 1) * gw]
        for part in range(3):
            grad = nn(normed_t[...], dproj[:, g_of(g, part)]) * grad_scale
            for r in range(24):
                put(72 + 72 * g + part * 24 + r, grad[r * 16:(r + 1) * 16])

    class Chain:
        def __init__(self, refs):
            (self.gb, self.crecv, self.xs, self.arecv, self.ys, self.brecv, self.zbuf, self.fin,
             self.sem, self.zsem) = refs

        def copy(self, k, src, dst, device):
            return remote(src, dst, self.sem.at[0, k], self.sem.at[1, k], device)

        def core_copy(self):
            return self.copy(0, self.gb.at[other], self.crecv, sibling)

        def one_copies(self):
            return [self.copy(1 + o, self.xs.at[q], self.arecv.at[o], d) for o, (q, d, _) in enumerate(ones)]

        def two_copies(self):
            return [self.copy(4 + o, self.ys.at[q], self.brecv.at[o], d) for o, (q, d, _) in enumerate(twos)]

        def z_copies(self, here=True):
            at = [z if here else q for _, q in zs]
            return [
                remote(self.zbuf.at[at[o]], self.zbuf.at[at[o]], self.zsem.at[0, o], self.zsem.at[1, o], d)
                for o, (d, _) in enumerate(zs)
            ]

        def back_two(self, here=True):
            at = [two if here else q for _, _, q in twos]
            return [
                self.copy(7 + o, self.fin.at[core, one, at[o]], self.fin.at[core, one, at[o]], d)
                for o, (_, d, _) in enumerate(twos)
            ]

        def back_one(self, here=True):
            at = [one if here else q for _, _, q in ones]
            return [
                self.copy(10 + o, self.fin.at[core, at[o]], self.fin.at[core, at[o]], d)
                for o, (_, d, _) in enumerate(ones)
            ]

        def back_core(self, o, half_at):
            at = one if o == 0 else ones[o - 1][2]
            return self.copy(13 + o, self.fin.at[half_at, at], self.fin.at[half_at, at], sibling)

        def start(self):
            self.core_copy().start()

        def first(self):
            self.core_copy().wait()
            self.xs[...] = (self.gb[core].astype(F32) + self.crecv[...].astype(F32)).astype(BF16)
            for copy in self.one_copies():
                copy.start()

        def second(self):
            for copy in self.one_copies():
                copy.wait()
            total = self.xs[one].astype(F32)
            for o in range(n - 1):
                total += self.arecv[o].astype(F32)
            self.ys[...] = total.astype(BF16)
            for copy in self.two_copies():
                copy.start()

        def third(self):
            for copy in self.two_copies():
                copy.wait()
            total = self.ys[two].astype(F32)
            for o in range(n - 1):
                total += self.brecv[o].astype(F32)
            self.zbuf[z] = total.astype(BF16)
            for copy in self.z_copies():
                copy.start()

        def fourth(self):
            for copy in self.z_copies():
                copy.wait_send()
            for copy in self.z_copies(False):
                copy.wait_recv()
            total = self.zbuf[0].astype(F32)
            for k in range(1, nz):
                total += self.zbuf[k].astype(F32)
            self.fin[core, one, two] = total.astype(BF16)
            for copy in self.back_two():
                copy.start()

        def fifth(self):
            for copy in self.back_two():
                copy.wait_send()
            for copy in self.back_two(False):
                copy.wait_recv()
            for copy in self.back_one():
                copy.start()
            self.back_core(0, core).start()

        def sixth(self):
            for o, copy in enumerate(self.back_one(False)):
                copy.wait_recv()
                self.back_core(o + 1, core).start()

        def last(self):
            for copy in self.back_one():
                copy.wait_send()
            for o in range(n):
                self.back_core(o, core).wait_send()
                self.back_core(o, other).wait_recv()

    chains = [Chain(r) for r in chunk_refs]

    def unpack(first, end):
        for t in range(first, end):
            i, at = tile_at(t)
            value = chains[i].fin[at].astype(F32)
            r, k = t % 24, t // 24
            rows = slice(r * 16, (r + 1) * 16)
            if k < 3:
                gout_ref[rows, k * 128:(k + 1) * 128] = value
            else:
                g, part = (k - 3) // 3, (k - 3) % 3
                gqkv_ref[rows, g_of(g, part)] = value

    bshare = BIAS_TILES // (4 * n)

    def bcopy(k, src, dst, device):
        return remote(src, dst, b_sem.at[0, k], b_sem.at[1, k], device)

    def bcore_copy():
        return bcopy(0, bb.at[other], bcrecv, sibling)

    def bx_copy():
        return bcopy(1, bs.at[1 - x_lo], bxrecv, pair)

    def by_copies():
        return [bcopy(2 + o, by.at[q], byrecv.at[o], d) for o, (q, d, _) in enumerate(ys)]

    def by_back(here=True):
        at = [y if here else q for _, _, q in ys]
        return [
            bcopy(5 + o, bfin.at[core, x_lo, at[o]], bfin.at[core, x_lo, at[o]], d)
            for o, (_, d, _) in enumerate(ys)
        ]

    def bx_back(x_at):
        return bcopy(8, bfin.at[core, x_at], bfin.at[core, x_at], pair)

    def bcore_back(half_at):
        return bcopy(9, bfin.at[half_at], bfin.at[half_at], sibling)

    def bias_core():
        rows = jnp.concatenate(
            [
                jnp.concatenate(
                    [
                        db[g, z2 * half:(z2 + 1) * half, j * blk:(j + 1) * blk]
                        for z2 in range(LEV)
                        for g in range(groups)
                    ]
                    + [jnp.zeros((half, 96), F32)],
                    axis=1,
                )
                for j in range(WW)
            ],
            axis=0,
        ).astype(BF16)
        dr = nn(gather_ref[...], rows).astype(BF16)
        for t in range(BIAS_TILES):
            k, r = t // 9, t % 9
            tile = dr[r * 16:(r + 1) * 16, k * 128:(k + 1) * 128] if k < 3 else jnp.zeros((16, 128), BF16)
            bb[bias_at(t)] = tile
        bcore_copy().start()

    def bias_at(t):
        return t // 16, t % 16 // (n * bshare), t % (n * bshare) // bshare, t % bshare

    def bias_x():
        bcore_copy().wait()
        bs[...] = (bb[core].astype(F32) + bcrecv[...].astype(F32)).astype(BF16)
        bx_copy().start()

    def bias_y():
        bx_copy().wait()
        by[...] = (bs[x_lo].astype(F32) + bxrecv[...].astype(F32)).astype(BF16)
        for copy in by_copies():
            copy.start()

    def bias_back_y():
        for copy in by_copies():
            copy.wait()
        total = by[y].astype(F32)
        for o in range(n - 1):
            total += byrecv[o].astype(F32)
        bfin[core, x_lo, y] = total.astype(BF16)
        for copy in by_back():
            copy.start()

    def bias_back_x():
        for copy in by_back():
            copy.wait_send()
        for copy in by_back(False):
            copy.wait_recv()
        bx_back(x_lo).start()

    def bias_back_core():
        bx_back(x_lo).wait_send()
        bx_back(1 - x_lo).wait_recv()
        bcore_back(core).start()

    def bias_end():
        bcore_back(core).wait_send()
        bcore_back(other).wait_recv()
        for t in range(27):
            k, r = t // 9, t % 9
            dr_ref[r * 16:(r + 1) * 16, k * 128:(k + 1) * 128] = bfin[bias_at(t)].astype(F32)

    def finish(f, ref):
        for copy in rims_out[3 * f:3 * f + 3]:
            copy.wait()
        full = (nn(ownt_ref[...], ow[f]) + nn(sendt_ref[...], rim_out[f])).astype(BF16)
        for s in range(SLABS):
            ref[s // WH, s % WH] = full[s * PITCH:s * PITCH + COLS]

    c0, c1, c2 = chains
    for w in range(WINDOWS):
        forward(w)
    ow[0] = (cells + nn(mix[...], wout_ref[...])).astype(BF16)
    rim_osnd[0] = nn(rimt_ref[...], ow[0]).astype(BF16)
    for copy in rims_out[:3]:
        copy.start()
    arrive(1, dy_w)
    out_grads()
    c0.start()
    for w in range(WINDOWS):
        widen(w)
    backward(0, 0)
    c0.first()
    backward(0, 1)
    backward(0, 2)
    qkv_grads(0)
    c0.second()
    for w in range(WINDOWS):
        backward(1, w)
    qkv_grads(1)
    c1.start()
    c0.third()
    backward(2, 0)
    backward(2, 1)
    c1.first()
    backward(2, 2)
    qkv_grads(2)
    c2.start()
    dn = nt(dproj[...], wqkv_ref[...])
    n_w = centred * rstd
    dx = (dn - jnp.mean(dn, axis=-1, keepdims=True) - n_w * jnp.mean(dn * n_w, axis=-1, keepdims=True)) * rstd
    ow[1] = (dx + dy_w[...].astype(F32)).astype(BF16)
    c2.first()
    rim_osnd[1] = nn(rimt_ref[...], ow[1]).astype(BF16)
    for copy in rims_out[3:]:
        copy.start()
    c0.fourth()
    bias_core()
    c1.second()
    c2.second()
    bias_x()
    c1.third()
    c2.third()
    c0.fifth()
    bias_y()
    finish(0, out_ref)
    c1.fourth()
    c2.fourth()
    bias_back_y()
    c0.sixth()
    c1.fifth()
    c2.fifth()
    bias_back_x()
    finish(1, dx_ref)
    c1.sixth()
    c2.sixth()
    bias_back_core()
    c0.last()
    unpack(0, CHUNKS[0])
    c1.last()
    unpack(CHUNKS[0], CHUNKS[0] + CHUNKS[1])
    bias_end()
    c2.last()
    unpack(CHUNKS[0] + CHUNKS[1], sum(CHUNKS))


def fused(cells, cot, qkv_weight, out_weight, table, lon_size, lat_size, cells_total):
    c = out_weight.shape[0]
    heads = table.shape[0]
    groups = heads // GROUP
    consts = constants()
    table = table.reshape(groups, GROUP, LEV, LEV, WH, WH * SPAN)
    table = table.transpose(3, 0, 2, 4, 1, 5).reshape(LEV, heads * SLABS, WH * SPAN)
    ins = (cells, cot, qkv_weight, out_weight, table) + consts
    n, nz = lon_size // 4, lat_size // X_HI
    bshare = BIAS_TILES // (4 * n)
    gw = GROUP * HEAD
    vm = pltpu.VMEM
    dma = pltpu.SemaphoreType.DMA
    scratch = [vm(a.shape, a.dtype) for a in ins] + [
        dma((len(ins),)),
        vm((2, SLABS * PITCH, c), BF16),
        vm((2, RIM, c), BF16),
        vm((2, RIM, c), BF16),
        vm((groups, TOK, LANES), F32),
        vm((groups, TOK, LANES), F32),
        vm((ROWS, c), BF16),
        vm((ROWS, c), BF16),
        vm((ROWS, c), BF16),
        vm((c, ROWS), BF16),
        vm((ROWS, c), BF16),
        vm((ROWS, 3 * c), BF16),
        vm((3 * c, c), BF16),
        vm((2, ROWS, c), BF16),
        vm((2, RIM, c), BF16),
        vm((2, RIM, c), BF16),
        vm((ROWS, 2 * c), BF16),
        vm((WINDOWS, c, TOK), BF16),
        vm((WINDOWS, groups, gw, LANES), BF16),
        vm((WINDOWS, groups, TOK, LANES), F32),
        vm((c, LANES), BF16),
        vm((WINDOWS, groups, gw, LANES), BF16),
        vm((WINDOWS * gw, LANES), BF16),
        dma((2, 12)),
    ]
    tile = (16, 128)
    for tiles in CHUNKS:
        share = tiles // (2 * n * n)
        scratch += [
            vm((2, n, n, share) + tile, BF16),
            vm((n, n, share) + tile, BF16),
            vm((n, n, share) + tile, BF16),
            vm((n - 1, n, share) + tile, BF16),
            vm((n, share) + tile, BF16),
            vm((n - 1, share) + tile, BF16),
            vm((nz, share) + tile, BF16),
            vm((2, n, n, share) + tile, BF16),
            dma((2, 17)),
            dma((2, nz)),
        ]
    scratch += [
        vm((2, 2, n, bshare) + tile, BF16),
        vm((2, n, bshare) + tile, BF16),
        vm((2, n, bshare) + tile, BF16),
        vm((n, bshare) + tile, BF16),
        vm((n, bshare) + tile, BF16),
        vm((n - 1, bshare) + tile, BF16),
        vm((2, 2, n, bshare) + tile, BF16),
        dma((2, 10)),
    ]
    kernel = functools.partial(
        body, lon_size, lat_size, groups, (c // heads) ** -0.5, cells_total ** -0.5
    )
    out_shape = (
        jax.ShapeDtypeStruct(cells.shape, BF16),
        jax.ShapeDtypeStruct(cells.shape, BF16),
        jax.ShapeDtypeStruct((c, 3 * c), F32),
        jax.ShapeDtypeStruct((c, c), F32),
        jax.ShapeDtypeStruct((144, 384), F32),
    )
    return pl.pallas_call(
        kernel,
        out_shape=out_shape,
        in_specs=[pl.BlockSpec(memory_space=pl.ANY)] * len(ins),
        out_specs=(pl.BlockSpec(memory_space=pltpu.VMEM),) * len(out_shape),
        scratch_shapes=scratch,
        compiler_params=pltpu.CompilerParams(
            vmem_limit_bytes=60 * 1024 * 1024, collective_id=0, has_side_effects=True
        ),
        cost_estimate=pl.CostEstimate(flops=6_000_000_000, bytes_accessed=10_000_000, transcendentals=800_000),
    )(*ins)


def on_device(cells, qkv_weight, out_weight, earth_bias, cotangent):
    lon_size, lat_size = lax.axis_size("lon"), lax.axis_size("lat")
    heads = earth_bias.shape[1]
    cells_total = LEV * cells.shape[1] * cells.shape[2] * lon_size * lat_size
    out, dx, gqkv, gout, dr = fused(
        cells, cotangent, qkv_weight, out_weight, earth_bias[0], lon_size, lat_size, cells_total
    )
    dr = dr[: WH * SPAN, : 2 * heads * SLABS].reshape(WH * SPAN, LEV, heads // GROUP, LEV, WH, GROUP)
    dr = dr.transpose(2, 5, 3, 1, 4, 0).reshape(earth_bias.shape)
    return out, dx, gqkv, gout, dr


def solution(mesh):
    grid = P(None, "lat", "lon", None)
    return jax.shard_map(
        on_device,
        mesh=mesh,
        in_specs=(grid, P(), P(), P("lat", None, None), grid),
        out_specs=(grid, grid, P(), P(), P("lat", None, None)),
        check_vma=False,
    )
```

```python
import functools

import numpy as np
import jax
import jax.numpy as jnp
from jax import lax
from jax.experimental import pallas as pl
from jax.experimental.pallas import tpu as pltpu
from jax.sharding import PartitionSpec as P

LEV = 2
WH = 6
WW = 12
TOK = LEV * WH * WW
SLABS = LEV * WH
SPAN = 2 * WW - 1
GROUP = 4
HEAD = 32
LANES = GROUP * TOK
WINDOWS = 3
ROWS = WINDOWS * TOK
COLS = WINDOWS * WW
PITCH = 80
RIMS = ((0, 208), (208, 48), (256, 48))
RIM = 304
BIAS_TILES = 32
CHUNKS = (64, 128, 96)
X_HI = 2
F32 = jnp.float32
BF16 = jnp.bfloat16
MESH = pl.DeviceIdType.MESH


def nn(a, b):
    return lax.dot_general(a, b, (((1,), (0,)), ((), ())), preferred_element_type=F32)


def nt(a, b):
    return lax.dot_general(a, b, (((1,), (1,)), ((), ())), preferred_element_type=F32)


def constants():
    j1, i2, j2 = np.meshgrid(np.arange(WW), np.arange(WH), np.arange(WW), indexing="ij")
    spot = (i2 * SPAN + j1 - j2 + WW - 1).reshape(-1)
    spread = (spot[:, None] == np.arange(WH * SPAN)[None, :]).astype(np.float32)
    gather = np.zeros((144, spread.shape[0]), np.float32)
    gather[: WH * SPAN] = spread.T
    lane = np.arange(LANES)
    lane_col, lane_slab = lane // (SLABS * GROUP), lane // GROUP % SLABS
    token_of_lane = lane_slab * WW + lane_col
    pick = (np.arange(TOK)[:, None] == token_of_lane[None, :]).astype(np.float32)
    row_half = np.arange(TOK) // WW % WH >= WH - WH // 2
    lane_half = lane_slab % WH >= WH - WH // 2
    cross = np.where(row_half[:, None] != lane_half[None, :], -1e9, 0.0).astype(np.float32)
    own = np.zeros((ROWS, WH * PITCH), np.float32)
    rim = np.zeros((ROWS, RIM), np.float32)
    send = np.zeros((RIM, WH * PITCH), np.float32)
    h = WH // 2
    for w in range(WINDOWS):
        for z in range(LEV):
            for i in range(WH):
                for j in range(WW):
                    t = w * TOK + (z * WH + i) * WW + j
                    col = WW // 2 + w * WW + j
                    below, beside = i >= h, col >= COLS
                    row, k = ((i - h) if below else (i + h)), i % h
                    slab = row * PITCH + col % COLS * LEV + z
                    if not below and not beside:
                        own[t, slab] = 1
                        continue
                    if beside:
                        at = (256 if below else 208) + z * 18 + k * 6 + j - 6
                    elif w == WINDOWS - 1:
                        at = 160 + z * 18 + k * 6 + j
                    else:
                        at = 80 * w + z * 36 + k * 12 + j
                    rim[t, at] = 1
                    send[at, slab] = 1
    bf = lambda a: jnp.asarray(np.ascontiguousarray(a), BF16)
    return (
        bf(spread), bf(gather), bf(pick), jnp.asarray(cross, F32),
        bf(own), bf(rim), bf(send), bf(own.T), bf(rim.T), bf(send.T),
    )


N_IN = 15


def body(lon_size, lat_size, groups, scale, grad_scale, *refs):
    (cells_h, cot_h, wqkv_h, wout_h, r_h) = refs[:5]
    consts_h = refs[5:N_IN]
    (out_ref, dx_ref, gqkv_ref, gout_ref, dr_ref) = refs[N_IN:N_IN + 5]
    (cells_v, cot_v, wqkv_ref, wout_ref, r_ref,
     spread_ref, gather_ref, pick_ref, cross_ref, own_ref, rim_ref, send_ref, ownt_ref, rimt_ref, sendt_ref,
     load_sem, slab, rim_snd, rim_in, bt, db, x_w, dy_w, normed, normed_t, mix, dproj, wt, ow, rim_osnd, rim_out,
     kv, k_ts, q_ws, soft_s, m_ts, dm_ws, dq_ts, tab, rows_of, turned,
     halo_sem, *comm) = refs[N_IN + 5:]
    chunk_refs = [comm[i * 9:i * 9 + 9] for i in range(len(CHUNKS))]
    (bb, bcrecv, bs, bxrecv, by, byrecv, bfin, b_sem) = comm[len(CHUNKS) * 9:]
    c = wout_ref.shape[0]
    n, nz = lon_size // 4, lat_size // X_HI
    half = WH * WW
    blk = SLABS * GROUP
    gw = GROUP * HEAD

    lon, lat = lax.axis_index("lon"), lax.axis_index("lat")
    core, x_lo, y = lon % 2, lon // 2 % 2, lon // 4
    x_hi, z = lat // nz, lat % nz
    x = x_hi * 2 + x_lo
    other = 1 - core
    one = jnp.where(core == 0, x, y)
    two = jnp.where(core == 0, y, x)

    def dev(lon_at, lat_at):
        return {"lon": lon_at, "lat": lat_at}

    def chip(x_at, y_at):
        return dev((y_at * 2 + x_at % 2) * 2 + core, x_at // 2 * nz + z)

    sibling = dev(lon + 1 - 2 * core, lat)
    ones, twos, zs, ys = [], [], [], []
    for o in range(1, n):
        q = (one + o) % n
        ones.append((q, chip(jnp.where(core == 0, q, x), jnp.where(core == 0, y, q)), (one + n - o) % n))
        q = (two + o) % n
        twos.append((q, chip(jnp.where(core == 0, x, q), jnp.where(core == 0, q, y)), (two + n - o) % n))
        q = (y + o) % n
        ys.append((q, chip(x, q), (y + n - o) % n))
    for o in range(1, nz):
        zs.append((dev(lon, x_hi * nz + (z + o) % nz), (z + nz - o) % nz))
    pair = dev((y * 2 + 1 - x_lo) * 2 + core, lat)

    lon_prev, lon_next = (lon + lon_size - 1) % lon_size, (lon + 1) % lon_size
    lat_prev, lat_next = (lat + lat_size - 1) % lat_size, (lat + 1) % lat_size
    back = (dev(lon, lat_prev), dev(lon_prev, lat), dev(lon_prev, lat_prev))
    ahead = (dev(lon, lat_next), dev(lon_next, lat), dev(lon_next, lat_next))

    def remote(src, dst, send_sem, recv_sem, device):
        return pltpu.make_async_remote_copy(
            src_ref=src, dst_ref=dst, send_sem=send_sem, recv_sem=recv_sem, device_id=device, device_id_type=MESH
        )

    order = (
        (cells_h, cells_v), (consts_h[6], send_ref), (cot_h, cot_v), (r_h, r_ref), (consts_h[0], spread_ref),
        (consts_h[3], cross_ref), (wqkv_h, wqkv_ref), (consts_h[4], own_ref), (consts_h[5], rim_ref),
        (consts_h[2], pick_ref), (wout_h, wout_ref), (consts_h[8], rimt_ref), (consts_h[7], ownt_ref),
        (consts_h[9], sendt_ref), (consts_h[1], gather_ref),
    )
    loads = [pltpu.make_async_copy(s, d, load_sem.at[i]) for i, (s, d) in enumerate(order)]
    for load in loads:
        load.start()

    barrier = pltpu.get_barrier_semaphore()

    def greet(device):
        pl.semaphore_signal(barrier, inc=1, device_id=device, device_id_type=MESH)

    partners = back + ahead + (sibling, pair)
    partners += tuple(d for _, d, _ in ones + twos + ys) + tuple(d for d, _ in zs)
    for device in partners:
        greet(device)

    def rim_copies(snd, rcv, devices, base):
        return [
            remote(
                snd.at[f, pl.ds(at, size)], rcv.at[f, pl.ds(at, size)],
                halo_sem.at[0, base + f * 3 + k], halo_sem.at[1, base + f * 3 + k], devices[k],
            )
            for f in range(2)
            for k, (at, size) in enumerate(RIMS)
        ]

    rims_in = rim_copies(rim_snd, rim_in, back, 0)
    rims_out = rim_copies(rim_osnd, rim_out, ahead, 6)
    for f, src in enumerate((cells_v, cot_v)):
        loads[2 * f].wait()
        for s in range(WH):
            slab[f, s * PITCH:(s + 1) * PITCH, :] = jnp.concatenate(
                [src[s].reshape(COLS * LEV, c), jnp.zeros((PITCH - COLS * LEV, c), BF16)], axis=0
            )
        if f == 0:
            loads[1].wait()
        rim_snd[f] = nn(send_ref[...], slab[f]).astype(BF16)
        if f == 0:
            pl.semaphore_wait(barrier, len(partners))
        for copy in rims_in[3 * f:3 * f + 3]:
            copy.start()

    for load in loads[3:6]:
        load.wait()
    last = (lat == lat_size - 1).astype(F32)
    tab[...] = r_ref[:, 0, :]
    width = WH * SPAN

    def segment(z1, z2, i1):
        return pl.ds(((z1 * LEV + z2) * WH + i1) * width, width)

    for z2 in range(LEV):
        for z1 in range(LEV):
            for i1 in range(WH):
                piece = tab[:, segment(z1, z2, i1)]
                for g in range(groups):
                    at = g * blk + (z1 * WH + i1) * GROUP
                    rows_of[at:at + GROUP, :] = piece[g * GROUP:(g + 1) * GROUP]
        table = rows_of[...]
        hi = table.astype(BF16)
        rest = table - hi.astype(F32)
        mid = rest.astype(BF16)
        lo = (rest - mid.astype(F32)).astype(BF16)
        spread = spread_ref[...]
        u = nt(spread, hi) + nt(spread, mid) + nt(spread, lo)
        for g in range(groups):
            rows = jnp.concatenate(
                [u[j * half:(j + 1) * half, g * blk:(g + 1) * blk] for j in range(WW)], axis=1
            )
            keep = pl.ds(z2 * half, half)
            bt[g, keep, :] = rows + cross_ref[keep, :] * last
    row = lax.broadcasted_iota(jnp.int32, (c, c), 0)
    col = lax.broadcasted_iota(jnp.int32, (c, c), 1)
    eye = (row == col).astype(F32).astype(BF16)
    head_row = lax.broadcasted_iota(jnp.int32, (gw, LANES), 0) // HEAD
    head_lane = lax.broadcasted_iota(jnp.int32, (gw, LANES), 1) % GROUP
    mine = (head_row == head_lane).astype(F32)
    for load in loads[6:]:
        load.wait()
    for part in range(3):
        wt[part * c:(part + 1) * c, :] = nt(eye, wqkv_ref[:, part * c:(part + 1) * c]).astype(BF16)
    pick = pick_ref[...]

    def arrive(f, ref):
        for copy in rims_in[3 * f:3 * f + 3]:
            copy.wait()
        ref[...] = (nn(own_ref[...], slab[f]) + nn(rim_ref[...], rim_in[f])).astype(BF16)

    arrive(0, x_w)
    cells = x_w[...].astype(F32)
    average = jnp.mean(cells, axis=-1, keepdims=True)
    centred = cells - average
    variance = jnp.mean(centred * centred, axis=-1, keepdims=True)
    rstd = lax.rsqrt(variance + 1e-05)
    normed[...] = (centred * rstd).astype(BF16)
    normed_t[...] = nt(eye, normed[...]).astype(BF16)

    kv[...] = nn(normed[...], wqkv_ref[:, c:]).astype(BF16)

    def at_of(w):
        return slice(w * TOK, (w + 1) * TOK)

    def g_of(g, part=0):
        return slice(part * c + g * gw, part * c + (g + 1) * gw)

    def forward(w):
        at = at_of(w)
        qkv_t = nt(wt[...], normed[at, :]).astype(BF16)
        q_all = nn(qkv_t[:c], pick)
        k_ts[w] = qkv_t[c:2 * c]
        for g in range(groups):
            q_wide = (q_all[g_of(g)] * mine).astype(BF16)
            q_ws[w, g] = q_wide
            s = nn(kv[at, g_of(g)], q_wide) * scale + bt[g]
            top = jnp.max(s, axis=0, keepdims=True)
            e = jnp.exp(s - top)
            soft = e * (1.0 / jnp.sum(e, axis=0, keepdims=True))
            soft_s[w, g] = soft
            m_ts[g_of(g), :] = (nn(qkv_t[g_of(g, 2)], soft.astype(BF16)) * mine).astype(BF16)
        mix[at, :] = nt(pick, m_ts[...]).astype(BF16)

    def widen(w):
        dm_t = nt(wout_ref[...], dy_w[at_of(w), :]).astype(BF16)
        dm_all = nn(dm_t, pick)
        for g in range(groups):
            dm_ws[w, g] = (dm_all[g_of(g)] * mine).astype(BF16)

    def backward(g, w):
        at = at_of(w)
        soft = soft_s[w, g]
        dm_wide = dm_ws[w, g]
        da = nn(kv[at, g_of(g, 1)], dm_wide)
        ds = soft * (da - jnp.sum(soft * da, axis=0, keepdims=True))
        if w == 0:
            db[g] = ds
        else:
            db[g] += ds
        ds = ds.astype(BF16)
        dq_ts[w * gw:(w + 1) * gw, :] = (nn(k_ts[w, g_of(g), :], ds) * (mine * scale)).astype(BF16)
        dproj[at, g_of(g, 1)] = (nt(ds, q_ws[w, g]) * scale).astype(BF16)
        dproj[at, g_of(g, 2)] = nt(soft.astype(BF16), dm_wide).astype(BF16)

    def tile_at(t):
        i = 0
        while t >= CHUNKS[i]:
            t -= CHUNKS[i]
            i += 1
        half_tiles = CHUNKS[i] // 2
        share = half_tiles // (n * n)
        return i, (t // half_tiles, t % half_tiles // (n * share), t % (n * share) // share, t % share)

    def put(t, value):
        i, at = tile_at(t)
        chunk_refs[i][0][at] = value.astype(BF16)

    def out_grads():
        grad = nn(nt(eye, mix[...]).astype(BF16), dy_w[...]) * grad_scale
        for k in range(3):
            for r in range(24):
                put(k * 24 + r, grad[r * 16:(r + 1) * 16, k * 128:(k + 1) * 128])

    def qkv_grads(g):
        dq = nt(pick, dq_ts[...]).astype(BF16)
        for w in range(WINDOWS):
            dproj[at_of(w), g_of(g)] = dq[:, w * gw:(w + 1) * gw]
        for part in range(3):
            grad = nn(normed_t[...], dproj[:, g_of(g, part)]) * grad_scale
            for r in range(24):
                put(72 + 72 * g + part * 24 + r, grad[r * 16:(r + 1) * 16])

    class Chain:
        def __init__(self, refs):
            (self.gb, self.crecv, self.xs, self.arecv, self.ys, self.brecv, self.zbuf, self.fin, self.sem) = refs

        def send(self, stage, src, dst, device):
            remote(src, dst, self.sem.at[0, stage], self.sem.at[1, stage], device).start()

        def wait(self, side, stage, like):
            pltpu.make_async_copy(like, like, self.sem.at[side, stage]).wait()

        def start(self):
            self.send(0, self.gb.at[other], self.crecv, sibling)

        def first(self):
            self.wait(1, 0, self.crecv)
            self.xs[...] = (self.gb[core].astype(F32) + self.crecv[...].astype(F32)).astype(BF16)
            for o, (q, d, _) in enumerate(ones):
                self.send(1, self.xs.at[q], self.arecv.at[o], d)

        def second(self):
            self.wait(1, 1, self.arecv)
            total = self.xs[one].astype(F32)
            for o in range(n - 1):
                total += self.arecv[o].astype(F32)
            self.ys[...] = total.astype(BF16)
            for o, (q, d, _) in enumerate(twos):
                self.send(2, self.ys.at[q], self.brecv.at[o], d)

        def third(self):
            self.wait(1, 2, self.brecv)
            total = self.ys[two].astype(F32)
            for o in range(n - 1):
                total += self.brecv[o].astype(F32)
            self.zbuf[0] = total.astype(BF16)
            for o, (d, _) in enumerate(zs):
                self.send(3, self.zbuf.at[0], self.zbuf.at[o + 1], d)

        def fourth(self):
            if nz > 1:
                self.wait(1, 3, self.zbuf.at[pl.ds(1, nz - 1)])
            total = self.zbuf[z].astype(F32)
            for k in range(1, nz):
                total += self.zbuf[(z + nz - k) % nz].astype(F32)
            mine_at = self.fin.at[core, one, two]
            mine_at[...] = total.astype(BF16)
            for _, d, _ in twos:
                self.send(4, mine_at, mine_at, d)

        def fifth(self):
            self.wait(1, 4, self.fin.at[core, one, pl.ds(0, n - 1)])
            mine_at = self.fin.at[core, one]
            for _, d, _ in ones:
                self.send(5, mine_at, mine_at, d)

        def sixth(self):
            self.wait(1, 5, self.fin.at[core, pl.ds(0, n - 1)])
            self.send(6, self.fin.at[core], self.fin.at[core], sibling)

        def last(self):
            self.wait(1, 6, self.fin.at[other])

        def drain(self):
            self.wait(0, 0, self.crecv)
            self.wait(0, 1, self.arecv)
            self.wait(0, 2, self.brecv)
            if nz > 1:
                self.wait(0, 3, self.zbuf.at[pl.ds(1, nz - 1)])
            self.wait(0, 4, self.brecv)
            self.wait(0, 5, self.arecv)
            self.wait(0, 6, self.crecv)

    chains = [Chain(r) for r in chunk_refs]

    def unpack(first, end):
        for t in range(first, end):
            i, at = tile_at(t)
            value = chains[i].fin[at]
            r, k = t % 24, t // 24
            rows = slice(r * 16, (r + 1) * 16)
            if k < 3:
                gout_ref[rows, k * 128:(k + 1) * 128] = value
            else:
                g, part = (k - 3) // 3, (k - 3) % 3
                gqkv_ref[rows, g_of(g, part)] = value

    bshare = BIAS_TILES // (4 * n)

    def bcopy(k, src, dst, device):
        return remote(src, dst, b_sem.at[0, k], b_sem.at[1, k], device)

    def bcore_copy():
        return bcopy(0, bb.at[other], bcrecv, sibling)

    def bx_copy():
        return bcopy(1, bs.at[1 - x_lo], bxrecv, pair)

    def by_copies():
        return [bcopy(2 + o, by.at[q], byrecv.at[o], d) for o, (q, d, _) in enumerate(ys)]

    def by_back(here=True):
        at = [y if here else q for _, _, q in ys]
        return [
            bcopy(5 + o, bfin.at[core, x_lo, at[o]], bfin.at[core, x_lo, at[o]], d)
            for o, (_, d, _) in enumerate(ys)
        ]

    def bx_back(x_at):
        return bcopy(8, bfin.at[core, x_at], bfin.at[core, x_at], pair)

    def bcore_back(half_at):
        return bcopy(9, bfin.at[half_at], bfin.at[half_at], sibling)

    def bias_core():
        rows = jnp.concatenate(
            [
                jnp.concatenate(
                    [
                        db[g, z2 * half:(z2 + 1) * half, j * blk:(j + 1) * blk]
                        for z2 in range(LEV)
                        for g in range(groups)
                    ]
                    + [jnp.zeros((half, 96), F32)],
                    axis=1,
                )
                for j in range(WW)
            ],
            axis=0,
        ).astype(BF16)
        dr = nn(gather_ref[...], rows).astype(BF16)
        for t in range(BIAS_TILES):
            k, r = t // 9, t % 9
            tile = dr[r * 16:(r + 1) * 16, k * 128:(k + 1) * 128] if k < 3 else jnp.zeros((16, 128), BF16)
            bb[bias_at(t)] = tile
        bcore_copy().start()

    def bias_at(t):
        return t // 16, t % 16 // (n * bshare), t % (n * bshare) // bshare, t % bshare

    def bias_x():
        bcore_copy().wait()
        bs[...] = (bb[core].astype(F32) + bcrecv[...].astype(F32)).astype(BF16)
        bx_copy().start()

    def bias_y():
        bx_copy().wait()
        by[...] = (bs[x_lo].astype(F32) + bxrecv[...].astype(F32)).astype(BF16)
        for copy in by_copies():
            copy.start()

    def bias_back_y():
        for copy in by_copies():
            copy.wait()
        total = by[y].astype(F32)
        for o in range(n - 1):
            total += byrecv[o].astype(F32)
        bfin[core, x_lo, y] = total.astype(BF16)
        for copy in by_back():
            copy.start()

    def bias_back_x():
        for copy in by_back():
            copy.wait_send()
        for copy in by_back(False):
            copy.wait_recv()
        bx_back(x_lo).start()

    def bias_back_core():
        bx_back(x_lo).wait_send()
        bx_back(1 - x_lo).wait_recv()
        bcore_back(core).start()

    def bias_end():
        bcore_back(core).wait_send()
        bcore_back(other).wait_recv()
        turned[144:, :] = jnp.zeros((256 - 144, 384), F32)
        for t in range(27):
            k, r = t // 9, t % 9
            turned[r * 16:(r + 1) * 16, k * 128:(k + 1) * 128] = bfin[bias_at(t)].astype(F32)
        flat = turned[...].T
        for z2 in range(LEV):
            for z1 in range(LEV):
                for i1 in range(WH):
                    for g in range(groups):
                        at = z2 * groups * blk + g * blk + (z1 * WH + i1) * GROUP
                        tab[g * GROUP:(g + 1) * GROUP, segment(z1, z2, i1)] = flat[at:at + GROUP, :width]
        dr_ref[:, 0, :] = tab[...]

    def finish(f, ref):
        for copy in rims_out[3 * f:3 * f + 3]:
            copy.wait()
        full = (nn(ownt_ref[...], ow[f]) + nn(sendt_ref[...], rim_out[f])).astype(BF16)
        for s in range(WH):
            ref[s] = full[s * PITCH:s * PITCH + COLS * LEV].reshape(COLS, LEV, c)

    c0, c1, c2 = chains
    for w in range(WINDOWS):
        forward(w)
    ow[0] = (cells + nn(mix[...], wout_ref[...])).astype(BF16)
    rim_osnd[0] = nn(rimt_ref[...], ow[0]).astype(BF16)
    for copy in rims_out[:3]:
        copy.start()
    arrive(1, dy_w)
    out_grads()
    c0.start()
    for w in range(WINDOWS):
        widen(w)
    backward(0, 0)
    c0.first()
    backward(0, 1)
    backward(0, 2)
    qkv_grads(0)
    c0.second()
    for w in range(WINDOWS):
        backward(1, w)
    qkv_grads(1)
    c1.start()
    c0.third()
    backward(2, 0)
    backward(2, 1)
    c1.first()
    backward(2, 2)
    qkv_grads(2)
    c2.start()
    dn = nt(dproj[...], wqkv_ref[...])
    n_w = centred * rstd
    dx = (dn - jnp.mean(dn, axis=-1, keepdims=True) - n_w * jnp.mean(dn * n_w, axis=-1, keepdims=True)) * rstd
    ow[1] = (dx + dy_w[...].astype(F32)).astype(BF16)
    c2.first()
    rim_osnd[1] = nn(rimt_ref[...], ow[1]).astype(BF16)
    c0.fourth()
    c1.second()
    c2.second()
    bias_core()
    c1.third()
    c2.third()
    for copy in rims_out[3:]:
        copy.start()
    bias_x()
    c0.fifth()
    finish(0, out_ref)
    bias_y()
    c1.fourth()
    c2.fourth()
    c0.sixth()
    bias_back_y()
    c1.fifth()
    c2.fifth()
    bias_back_x()
    c0.last()
    unpack(0, CHUNKS[0])
    c1.sixth()
    c2.sixth()
    bias_back_core()
    finish(1, dx_ref)
    c1.last()
    unpack(CHUNKS[0], CHUNKS[0] + CHUNKS[1])
    bias_end()
    c2.last()
    unpack(CHUNKS[0] + CHUNKS[1], sum(CHUNKS))
    for chain in chains:
        chain.drain()


def fused(cells, cot, qkv_weight, out_weight, table, lon_size, lat_size, cells_total):
    c = out_weight.shape[0]
    heads, _, entries = table.shape
    groups = heads // GROUP
    consts = constants()
    ins = (cells, cot, qkv_weight, out_weight, table) + consts
    n, nz = lon_size // 4, lat_size // X_HI
    bshare = BIAS_TILES // (4 * n)
    gw = GROUP * HEAD
    vm = pltpu.VMEM
    dma = pltpu.SemaphoreType.DMA
    scratch = [vm(a.shape, a.dtype) for a in ins] + [
        dma((len(ins),)),
        vm((2, WH * PITCH, c), BF16),
        vm((2, RIM, c), BF16),
        vm((2, RIM, c), BF16),
        vm((groups, TOK, LANES), F32),
        vm((groups, TOK, LANES), F32),
        vm((ROWS, c), BF16),
        vm((ROWS, c), BF16),
        vm((ROWS, c), BF16),
        vm((c, ROWS), BF16),
        vm((ROWS, c), BF16),
        vm((ROWS, 3 * c), BF16),
        vm((3 * c, c), BF16),
        vm((2, ROWS, c), BF16),
        vm((2, RIM, c), BF16),
        vm((2, RIM, c), BF16),
        vm((ROWS, 2 * c), BF16),
        vm((WINDOWS, c, TOK), BF16),
        vm((WINDOWS, groups, gw, LANES), BF16),
        vm((WINDOWS, groups, TOK, LANES), F32),
        vm((c, LANES), BF16),
        vm((WINDOWS, groups, gw, LANES), BF16),
        vm((WINDOWS * gw, LANES), BF16),
        vm((heads, entries), F32),
        vm((heads * SLABS, WH * SPAN), F32),
        vm((256, 384), F32),
        dma((2, 12)),
    ]
    tile = (16, 128)
    for tiles in CHUNKS:
        share = tiles // (2 * n * n)
        scratch += [
            vm((2, n, n, share) + tile, BF16),
            vm((n, n, share) + tile, BF16),
            vm((n, n, share) + tile, BF16),
            vm((n - 1, n, share) + tile, BF16),
            vm((n, share) + tile, BF16),
            vm((n - 1, share) + tile, BF16),
            vm((nz, share) + tile, BF16),
            vm((2, n, n, share) + tile, BF16),
            dma((2, 7)),
        ]
    scratch += [
        vm((2, 2, n, bshare) + tile, BF16),
        vm((2, n, bshare) + tile, BF16),
        vm((2, n, bshare) + tile, BF16),
        vm((n, bshare) + tile, BF16),
        vm((n, bshare) + tile, BF16),
        vm((n - 1, bshare) + tile, BF16),
        vm((2, 2, n, bshare) + tile, BF16),
        dma((2, 10)),
    ]
    kernel = functools.partial(
        body, lon_size, lat_size, groups, (c // heads) ** -0.5, cells_total ** -0.5
    )
    out_shape = (
        jax.ShapeDtypeStruct(cells.shape, BF16),
        jax.ShapeDtypeStruct(cells.shape, BF16),
        jax.ShapeDtypeStruct((c, 3 * c), BF16),
        jax.ShapeDtypeStruct((c, c), BF16),
        jax.ShapeDtypeStruct(table.shape, F32),
    )
    return pl.pallas_call(
        kernel,
        out_shape=out_shape,
        in_specs=[pl.BlockSpec(memory_space=pl.ANY)] * len(ins),
        out_specs=(pl.BlockSpec(memory_space=pltpu.VMEM),) * len(out_shape),
        scratch_shapes=scratch,
        compiler_params=pltpu.CompilerParams(
            vmem_limit_bytes=60 * 1024 * 1024, collective_id=0, has_side_effects=True
        ),
        cost_estimate=pl.CostEstimate(flops=6_000_000_000, bytes_accessed=10_000_000, transcendentals=800_000),
    )(*ins)


def on_device(cells, qkv_weight, out_weight, earth_bias, cotangent):
    lon_size, lat_size = lax.axis_size("lon"), lax.axis_size("lat")
    heads = earth_bias.shape[1]
    cells_total = LEV * cells.shape[1] * cells.shape[2] * lon_size * lat_size
    out, dx, gqkv, gout, dr = fused(
        cells.transpose(1, 2, 0, 3), cotangent.transpose(1, 2, 0, 3), qkv_weight, out_weight, earth_bias.transpose(1, 0, 2),
        lon_size, lat_size, cells_total
    )
    out, dx = out.transpose(2, 0, 1, 3), dx.transpose(2, 0, 1, 3)
    return out, dx, gqkv.astype(F32), gout.astype(F32), dr.transpose(1, 0, 2)


def solution(mesh):
    grid = P(None, "lat", "lon", None)
    return jax.shard_map(
        on_device,
        mesh=mesh,
        in_specs=(grid, P(), P(), P("lat", None, None), grid),
        out_specs=(grid, grid, P(), P(), P("lat", None, None)),
        check_vma=False,
    )
```

```python
import functools

import numpy as np
import jax
import jax.numpy as jnp
from jax import lax
from jax.experimental import pallas as pl
from jax.experimental.pallas import tpu as pltpu
from jax.sharding import PartitionSpec as P

LEV = 2
WH = 6
WW = 12
TOK = LEV * WH * WW
SLABS = LEV * WH
SPAN = 2 * WW - 1
GROUP = 4
HEAD = 32
LANES = GROUP * TOK
WINDOWS = 3
ROWS = WINDOWS * TOK
COLS = WINDOWS * WW
PITCH = 80
FINE_RIMS = ((0, 80, 0), (80, 80, 0), (160, 48, 0), (208, 48, 1), (256, 48, 2))
RIMS = ((0, 208, 0), (208, 48, 1), (256, 48, 2))
RIM_OF = ((0, 80), (80, 80), (160, 144))
RIM = 304
BIAS_TILES = 32
CHUNKS = (128, 160)
X_HI = 2
F32 = jnp.float32
BF16 = jnp.bfloat16
MESH = pl.DeviceIdType.MESH


def nn(a, b):
    return lax.dot_general(a, b, (((1,), (0,)), ((), ())), preferred_element_type=F32)


def nt(a, b):
    return lax.dot_general(a, b, (((1,), (1,)), ((), ())), preferred_element_type=F32)


def constants():
    j1, i2, j2 = np.meshgrid(np.arange(WW), np.arange(WH), np.arange(WW), indexing="ij")
    spot = (i2 * SPAN + j1 - j2 + WW - 1).reshape(-1)
    spread = (spot[:, None] == np.arange(WH * SPAN)[None, :]).astype(np.float32)
    gather = np.zeros((144, spread.shape[0]), np.float32)
    gather[: WH * SPAN] = spread.T
    lane = np.arange(LANES)
    lane_col, lane_slab = lane // (SLABS * GROUP), lane // GROUP % SLABS
    token_of_lane = lane_slab * WW + lane_col
    pick = (np.arange(TOK)[:, None] == token_of_lane[None, :]).astype(np.float32)
    row_half = np.arange(TOK) // WW % WH >= WH - WH // 2
    lane_half = lane_slab % WH >= WH - WH // 2
    cross = np.where(row_half[:, None] != lane_half[None, :], -1e9, 0.0).astype(np.float32)
    own = np.zeros((ROWS, WH * PITCH), np.float32)
    rim = np.zeros((ROWS, RIM), np.float32)
    send = np.zeros((RIM, WH * PITCH), np.float32)
    h = WH // 2
    for w in range(WINDOWS):
        for z in range(LEV):
            for i in range(WH):
                for j in range(WW):
                    t = w * TOK + (z * WH + i) * WW + j
                    col = WW // 2 + w * WW + j
                    below, beside = i >= h, col >= COLS
                    row, k = ((i - h) if below else (i + h)), i % h
                    slab = row * PITCH + col % COLS * LEV + z
                    if not below and not beside:
                        own[t, slab] = 1
                        continue
                    if beside:
                        at = (256 if below else 208) + z * 18 + k * 6 + j - 6
                    elif w == WINDOWS - 1:
                        at = 160 + z * 18 + k * 6 + j
                    else:
                        at = 80 * w + z * 36 + k * 12 + j
                    rim[t, at] = 1
                    send[at, slab] = 1
    low = WH // 2 * PITCH
    rim_w = np.zeros((ROWS, 144), np.float32)
    rim_wt = np.zeros((RIM, TOK), np.float32)
    for w, (at, size) in enumerate(RIM_OF):
        block = rim[w * TOK:(w + 1) * TOK, at:at + size]
        rim_w[w * TOK:(w + 1) * TOK, :size] = block
        rim_wt[at:at + size] = block.T
    send_w = np.concatenate([send[:208, :low], send[208:256, low:], send[256:, :low]], axis=0)
    bf = lambda a: jnp.asarray(np.ascontiguousarray(a), BF16)
    return (
        bf(spread), bf(gather), bf(pick), jnp.asarray(cross, F32),
        bf(own[:, low:]), bf(rim_w), bf(send_w), bf(own[:, low:].T), bf(rim_wt), bf(send[:, :low].T),
        bf(send[208:256, low:].T),
    )


N_IN = 16


def body(lon_size, lat_size, groups, scale, grad_scale, *refs):
    (cells_h, cot_h, wqkv_h, wout_h, r_h) = refs[:5]
    consts_h = refs[5:N_IN]
    (out_ref, dx_ref, gqkv_ref, gout_ref, dr_ref) = refs[N_IN:N_IN + 5]
    (cells_v, cot_v, wqkv_ref, wout_ref, r_ref,
     spread_ref, gather_ref, pick_ref, cross_ref, own_ref, rim_ref, send_ref, ownt_ref, rimt_ref, sendt_ref,
     side_ref,
     load_sem, slab, rim_snd, rim_in, bt, db, x_w, dy_w, normed, normed_t, mix, dproj, wt, ow, rim_osnd, rim_out,
     kv, k_ts, q_ws, soft_s, m_ts, dm_ws, dq_ts, tab, rows_of, turned, n_s, rstd_s,
     halo_sem, *comm) = refs[N_IN + 5:]
    chunk_refs = [comm[i * 9:i * 9 + 9] for i in range(len(CHUNKS))]
    (bb, bcrecv, bs, bxrecv, by, byrecv, bfin, b_sem) = comm[len(CHUNKS) * 9:]
    c = wout_ref.shape[0]
    n, nz = lon_size // 4, lat_size // X_HI
    half = WH * WW
    blk = SLABS * GROUP
    gw = GROUP * HEAD

    lon, lat = lax.axis_index("lon"), lax.axis_index("lat")
    core, x_lo, y = lon % 2, lon // 2 % 2, lon // 4
    x_hi, z = lat // nz, lat % nz
    x = x_hi * 2 + x_lo
    other = 1 - core
    one = jnp.where(core == 0, x, y)
    two = jnp.where(core == 0, y, x)

    def dev(lon_at, lat_at):
        return {"lon": lon_at, "lat": lat_at}

    def chip(x_at, y_at):
        return dev((y_at * 2 + x_at % 2) * 2 + core, x_at // 2 * nz + z)

    sibling = dev(lon + 1 - 2 * core, lat)
    ones, twos, zs, ys = [], [], [], []
    for o in range(1, n):
        q = (one + o) % n
        ones.append((q, chip(jnp.where(core == 0, q, x), jnp.where(core == 0, y, q)), (one + n - o) % n))
        q = (two + o) % n
        twos.append((q, chip(jnp.where(core == 0, x, q), jnp.where(core == 0, q, y)), (two + n - o) % n))
        q = (y + o) % n
        ys.append((q, chip(x, q), (y + n - o) % n))
    for o in range(1, nz):
        zs.append((dev(lon, x_hi * nz + (z + o) % nz), (z + nz - o) % nz))
    pair = dev((y * 2 + 1 - x_lo) * 2 + core, lat)

    lon_prev, lon_next = (lon + lon_size - 1) % lon_size, (lon + 1) % lon_size
    lat_prev, lat_next = (lat + lat_size - 1) % lat_size, (lat + 1) % lat_size
    back = (dev(lon, lat_prev), dev(lon_prev, lat), dev(lon_prev, lat_prev))
    ahead = (dev(lon, lat_next), dev(lon_next, lat), dev(lon_next, lat_next))

    def remote(src, dst, send_sem, recv_sem, device):
        return pltpu.make_async_remote_copy(
            src_ref=src, dst_ref=dst, send_sem=send_sem, recv_sem=recv_sem, device_id=device, device_id_type=MESH
        )

    order = (
        (cells_h, cells_v), (consts_h[6], send_ref), (cot_h, cot_v), (r_h, r_ref), (consts_h[0], spread_ref),
        (consts_h[3], cross_ref), (wqkv_h, wqkv_ref), (consts_h[4], own_ref), (consts_h[5], rim_ref),
        (consts_h[2], pick_ref), (wout_h, wout_ref), (consts_h[8], rimt_ref), (consts_h[7], ownt_ref),
        (consts_h[9], sendt_ref), (consts_h[10], side_ref), (consts_h[1], gather_ref),
    )
    loads = [pltpu.make_async_copy(s, d, load_sem.at[i]) for i, (s, d) in enumerate(order)]
    for load in loads:
        load.start()

    barrier = pltpu.get_barrier_semaphore()

    def greet(device):
        pl.semaphore_signal(barrier, inc=1, device_id=device, device_id_type=MESH)

    partners = back + ahead + (sibling,)
    partners += tuple(d for _, d, _ in ones + twos) + tuple(d for d, _ in zs)
    for device in partners:
        greet(device)

    def rim_copies(f, snd, rcv, devices, base, parts):
        return [
            remote(
                snd.at[f, pl.ds(at, size)], rcv.at[f, pl.ds(at, size)],
                halo_sem.at[0, base + k], halo_sem.at[1, base + k], devices[to],
            )
            for k, (at, size, to) in enumerate(parts)
        ]

    rims_in = (
        rim_copies(0, rim_snd, rim_in, back, 0, FINE_RIMS),
        rim_copies(1, rim_snd, rim_in, back, 5, RIMS),
    )
    rims_out = (
        rim_copies(0, rim_osnd, rim_out, ahead, 8, RIMS),
        rim_copies(1, rim_osnd, rim_out, ahead, 11, RIMS),
    )
    low = WH // 2 * PITCH
    for f, src in enumerate((cells_v, cot_v)):
        loads[2 * f].wait()
        for s in range(WH):
            slab[f, s * PITCH:(s + 1) * PITCH, :] = jnp.concatenate(
                [src[s].reshape(COLS * LEV, c), jnp.zeros((PITCH - COLS * LEV, c), BF16)], axis=0
            )
        if f == 0:
            loads[1].wait()
        rim_snd[f, :208] = nn(send_ref[:208], slab[f, :low]).astype(BF16)
        rim_snd[f, 208:256] = nn(send_ref[208:256], slab[f, low:]).astype(BF16)
        rim_snd[f, 256:] = nn(send_ref[256:], slab[f, :low]).astype(BF16)
        if f == 0:
            pl.semaphore_wait(barrier, len(partners))
        for copy in rims_in[f]:
            copy.start()

    for load in loads[3:6]:
        load.wait()
    last = (lat == lat_size - 1).astype(F32)
    tab[...] = r_ref[:, 0, :]
    width = WH * SPAN

    def segment(z1, z2, i1):
        return pl.ds(((z1 * LEV + z2) * WH + i1) * width, width)

    for z2 in range(LEV):
        for z1 in range(LEV):
            for i1 in range(WH):
                piece = tab[:, segment(z1, z2, i1)]
                for g in range(groups):
                    at = g * blk + (z1 * WH + i1) * GROUP
                    rows_of[at:at + GROUP, :] = piece[g * GROUP:(g + 1) * GROUP]
        table = rows_of[...]
        hi = table.astype(BF16)
        rest = table - hi.astype(F32)
        mid = rest.astype(BF16)
        lo = (rest - mid.astype(F32)).astype(BF16)
        spread = spread_ref[...]
        u = nt(spread, hi) + nt(spread, mid) + nt(spread, lo)
        for g in range(groups):
            rows = jnp.concatenate(
                [u[j * half:(j + 1) * half, g * blk:(g + 1) * blk] for j in range(WW)], axis=1
            )
            keep = pl.ds(z2 * half, half)
            bt[g, keep, :] = rows + cross_ref[keep, :] * last
    row = lax.broadcasted_iota(jnp.int32, (c, c), 0)
    col = lax.broadcasted_iota(jnp.int32, (c, c), 1)
    eye = (row == col).astype(F32).astype(BF16)
    head_row = lax.broadcasted_iota(jnp.int32, (gw, LANES), 0) // HEAD
    head_lane = lax.broadcasted_iota(jnp.int32, (gw, LANES), 1) % GROUP
    mine = (head_row == head_lane).astype(F32)
    for load in loads[6:]:
        load.wait()
    for part in range(3):
        wt[part * c:(part + 1) * c, :] = nt(eye, wqkv_ref[:, part * c:(part + 1) * c]).astype(BF16)
    pick = pick_ref[...]

    def arrive(f, w, ref):
        if f == 0:
            parts = rims_in[0][w:w + 1] if w < WINDOWS - 1 else rims_in[0][w:]
        else:
            parts = rims_in[1][:1] if w == 0 else rims_in[1][1:] if w == WINDOWS - 1 else []
        for copy in parts:
            copy.wait()
        at, (first, size) = slice(w * TOK, (w + 1) * TOK), RIM_OF[w]
        ref[at, :] = (
            nn(own_ref[at, :], slab[f, low:]) + nn(rim_ref[at, :size], rim_in[f, first:first + size])
        ).astype(BF16)

    def at_of(w):
        return slice(w * TOK, (w + 1) * TOK)

    def g_of(g, part=0):
        return slice(part * c + g * gw, part * c + (g + 1) * gw)

    def forward(w):
        at = at_of(w)
        arrive(0, w, x_w)
        cells = x_w[at, :].astype(F32)
        average = jnp.mean(cells, axis=-1, keepdims=True)
        centred = cells - average
        rstd = lax.rsqrt(jnp.mean(centred * centred, axis=-1, keepdims=True) + 1e-05)
        rstd_s[at, :] = rstd
        n_w = centred * rstd
        n_s[at, :] = n_w
        here = n_w.astype(BF16)
        normed[at, :] = here
        kv[at, :] = nn(here, wqkv_ref[:, c:]).astype(BF16)
        qkv_t = nt(wt[...], here).astype(BF16)
        q_all = nn(qkv_t[:c], pick)
        k_ts[w] = qkv_t[c:2 * c]
        for g in range(groups):
            q_wide = (q_all[g_of(g)] * mine).astype(BF16)
            q_ws[w, g] = q_wide
            s = nn(kv[at, g_of(g)], q_wide) * scale + bt[g]
            top = jnp.max(s, axis=0, keepdims=True)
            e = jnp.exp(s - top)
            soft = e * (1.0 / jnp.sum(e, axis=0, keepdims=True))
            soft_s[w, g] = soft
            m_ts[g_of(g), :] = (nn(qkv_t[g_of(g, 2)], soft.astype(BF16)) * mine).astype(BF16)
        mix[at, :] = nt(pick, m_ts[...]).astype(BF16)

    def widen(w):
        dm_t = nt(wout_ref[...], dy_w[at_of(w), :]).astype(BF16)
        dm_all = nn(dm_t, pick)
        for g in range(groups):
            dm_ws[w, g] = (dm_all[g_of(g)] * mine).astype(BF16)

    def backward(g, w):
        at = at_of(w)
        soft = soft_s[w, g]
        dm_wide = dm_ws[w, g]
        da = nn(kv[at, g_of(g, 1)], dm_wide)
        ds = soft * (da - jnp.sum(soft * da, axis=0, keepdims=True))
        if w == 0:
            db[g] = ds
        else:
            db[g] += ds
        ds = ds.astype(BF16)
        dq_ts[w * gw:(w + 1) * gw, :] = (nn(k_ts[w, g_of(g), :], ds) * (mine * scale)).astype(BF16)
        dproj[at, g_of(g, 1)] = (nt(ds, q_ws[w, g]) * scale).astype(BF16)
        dproj[at, g_of(g, 2)] = nt(soft.astype(BF16), dm_wide).astype(BF16)

    def tile_at(t):
        i = 0
        while t >= CHUNKS[i]:
            t -= CHUNKS[i]
            i += 1
        half_tiles = CHUNKS[i] // 2
        share = half_tiles // (n * n)
        return i, (t // half_tiles, t % half_tiles // (n * share), t % (n * share) // share, t % share)

    def put(t, value):
        i, at = tile_at(t)
        chunk_refs[i][0][at] = value.astype(BF16)

    def out_grads():
        normed_t[...] = nt(eye, normed[...]).astype(BF16)
        grad = nn(nt(eye, mix[...]).astype(BF16), dy_w[...]) * grad_scale
        for k in range(3):
            for r in range(24):
                put(k * 24 + r, grad[r * 16:(r + 1) * 16, k * 128:(k + 1) * 128])

    def qkv_grads(g):
        dq = nt(pick, dq_ts[...]).astype(BF16)
        for w in range(WINDOWS):
            dproj[at_of(w), g_of(g)] = dq[:, w * gw:(w + 1) * gw]
        for part in range(3):
            grad = nn(normed_t[...], dproj[:, g_of(g, part)]) * grad_scale
            for r in range(24):
                put(72 + 72 * g + part * 24 + r, grad[r * 16:(r + 1) * 16])

    class Chain:
        def __init__(self, refs):
            (self.gb, self.crecv, self.xs, self.arecv, self.ys, self.brecv, self.zbuf, self.fin, self.sem) = refs

        def send(self, stage, src, dst, device):
            remote(src, dst, self.sem.at[0, stage], self.sem.at[1, stage], device).start()

        def wait(self, side, stage, like):
            pltpu.make_async_copy(like, like, self.sem.at[side, stage]).wait()

        def start(self):
            self.send(0, self.gb.at[other], self.crecv, sibling)

        def first(self):
            self.wait(1, 0, self.crecv)
            self.xs[...] = (self.gb[core].astype(F32) + self.crecv[...].astype(F32)).astype(BF16)
            for o, (q, d, _) in enumerate(ones):
                self.send(1, self.xs.at[q], self.arecv.at[o], d)

        def second(self):
            self.wait(1, 1, self.arecv)
            total = self.xs[one].astype(F32)
            for o in range(n - 1):
                total += self.arecv[o].astype(F32)
            self.ys[...] = total.astype(BF16)
            for o, (q, d, _) in enumerate(twos):
                self.send(2, self.ys.at[q], self.brecv.at[o], d)

        def third(self):
            self.wait(1, 2, self.brecv)
            total = self.ys[two].astype(F32)
            for o in range(n - 1):
                total += self.brecv[o].astype(F32)
            self.zbuf[0] = total.astype(BF16)
            for o, (d, _) in enumerate(zs):
                self.send(3, self.zbuf.at[0], self.zbuf.at[o + 1], d)

        def fourth(self):
            if nz > 1:
                self.wait(1, 3, self.zbuf.at[pl.ds(1, nz - 1)])
            total = self.zbuf[z].astype(F32)
            for k in range(1, nz):
                total += self.zbuf[(z + nz - k) % nz].astype(F32)
            mine_at = self.fin.at[core, one, two]
            mine_at[...] = total.astype(BF16)
            for _, d, _ in twos:
                self.send(4, mine_at, mine_at, d)

        def fifth(self):
            self.wait(1, 4, self.fin.at[core, one, pl.ds(0, n - 1)])
            mine_at = self.fin.at[core, one]
            for _, d, _ in ones:
                self.send(5, mine_at, mine_at, d)

        def sixth(self):
            self.wait(1, 5, self.fin.at[core, pl.ds(0, n - 1)])
            self.send(6, self.fin.at[core], self.fin.at[core], sibling)

        def last(self):
            self.wait(1, 6, self.fin.at[other])

        def drain(self):
            self.wait(0, 0, self.crecv)
            self.wait(0, 1, self.arecv)
            self.wait(0, 2, self.brecv)
            if nz > 1:
                self.wait(0, 3, self.zbuf.at[pl.ds(1, nz - 1)])
            self.wait(0, 4, self.brecv)
            self.wait(0, 5, self.arecv)
            self.wait(0, 6, self.crecv)

    chains = [Chain(r) for r in chunk_refs]

    def unpack(first, end):
        for t in range(first, end):
            i, at = tile_at(t)
            value = chains[i].fin[at].astype(F32)
            r, k = t % 24, t // 24
            rows = slice(r * 16, (r + 1) * 16)
            if k < 3:
                gout_ref[rows, k * 128:(k + 1) * 128] = value
            else:
                g, part = (k - 3) // 3, (k - 3) % 3
                gqkv_ref[rows, g_of(g, part)] = value

    bshare = BIAS_TILES // (4 * n)

    def bcopy(k, src, dst, device):
        return remote(src, dst, b_sem.at[0, k], b_sem.at[1, k], device)

    def bcore_copy():
        return bcopy(0, bb.at[other], bcrecv, sibling)

    def bx_copy():
        return bcopy(1, bs.at[1 - x_lo], bxrecv, pair)

    def by_copies():
        return [bcopy(2 + o, by.at[q], byrecv.at[o], d) for o, (q, d, _) in enumerate(ys)]

    def by_back(here=True):
        at = [y if here else q for _, _, q in ys]
        return [
            bcopy(5 + o, bfin.at[core, x_lo, at[o]], bfin.at[core, x_lo, at[o]], d)
            for o, (_, d, _) in enumerate(ys)
        ]

    def bx_back(x_at):
        return bcopy(8, bfin.at[core, x_at], bfin.at[core, x_at], pair)

    def bcore_back(half_at):
        return bcopy(9, bfin.at[half_at], bfin.at[half_at], sibling)

    def bias_core():
        rows = jnp.concatenate(
            [
                jnp.concatenate(
                    [
                        db[g, z2 * half:(z2 + 1) * half, j * blk:(j + 1) * blk]
                        for z2 in range(LEV)
                        for g in range(groups)
                    ]
                    + [jnp.zeros((half, 96), F32)],
                    axis=1,
                )
                for j in range(WW)
            ],
            axis=0,
        ).astype(BF16)
        dr = nn(gather_ref[...], rows).astype(BF16)
        for t in range(BIAS_TILES):
            k, r = t // 9, t % 9
            tile = dr[r * 16:(r + 1) * 16, k * 128:(k + 1) * 128] if k < 3 else jnp.zeros((16, 128), BF16)
            bb[bias_at(t)] = tile
        bcore_copy().start()

    def bias_at(t):
        return t // 16, t % 16 // (n * bshare), t % (n * bshare) // bshare, t % bshare

    def bias_x():
        bcore_copy().wait()
        bs[...] = (bb[core].astype(F32) + bcrecv[...].astype(F32)).astype(BF16)
        bx_copy().start()

    def bias_y():
        bx_copy().wait()
        by[...] = (bs[x_lo].astype(F32) + bxrecv[...].astype(F32)).astype(BF16)
        for copy in by_copies():
            copy.start()

    def bias_back_y():
        for copy in by_copies():
            copy.wait()
        total = by[y].astype(F32)
        for o in range(n - 1):
            total += byrecv[o].astype(F32)
        bfin[core, x_lo, y] = total.astype(BF16)
        for copy in by_back():
            copy.start()

    def bias_back_x():
        for copy in by_back():
            copy.wait_send()
        for copy in by_back(False):
            copy.wait_recv()
        bx_back(x_lo).start()

    def bias_back_core():
        bx_back(x_lo).wait_send()
        bx_back(1 - x_lo).wait_recv()
        bcore_back(core).start()

    def bias_end():
        bcore_back(core).wait_send()
        bcore_back(other).wait_recv()
        turned[144:, :] = jnp.zeros((256 - 144, 384), F32)
        for t in range(27):
            k, r = t // 9, t % 9
            turned[r * 16:(r + 1) * 16, k * 128:(k + 1) * 128] = bfin[bias_at(t)].astype(F32)
        flat = turned[...].T
        for z2 in range(LEV):
            for z1 in range(LEV):
                for i1 in range(WH):
                    for g in range(groups):
                        at = z2 * groups * blk + g * blk + (z1 * WH + i1) * GROUP
                        tab[g * GROUP:(g + 1) * GROUP, segment(z1, z2, i1)] = flat[at:at + GROUP, :width]
        dr_ref[:, 0, :] = tab[...]

    def pack_out(f):
        for w, (first, size) in enumerate(RIM_OF):
            rim_osnd[f, first:first + size] = nn(rimt_ref[first:first + size], ow[f, at_of(w)]).astype(BF16)

    def finish(f, ref):
        for copy in rims_out[f]:
            copy.wait()
        upper = nn(sendt_ref[...], rim_out[f]).astype(BF16)
        lower = (nn(ownt_ref[...], ow[f]) + nn(side_ref[...], rim_out[f, 208:256])).astype(BF16)
        for s in range(WH):
            full, r = (upper, s) if s < WH // 2 else (lower, s - WH // 2)
            ref[s] = full[r * PITCH:r * PITCH + COLS * LEV].reshape(COLS, LEV, c)

    c0, c1 = chains
    for w in range(WINDOWS):
        forward(w)
    ow[0] = (x_w[...].astype(F32) + nn(mix[...], wout_ref[...])).astype(BF16)
    pack_out(0)
    for copy in rims_out[0]:
        copy.start()
    for w in range(WINDOWS):
        arrive(1, w, dy_w)
    out_grads()
    for w in range(WINDOWS):
        widen(w)
    for w in range(WINDOWS):
        backward(0, w)
    qkv_grads(0)
    c0.start()
    backward(1, 0)
    backward(1, 1)
    c0.first()
    backward(1, 2)
    qkv_grads(1)
    backward(2, 0)
    c0.second()
    backward(2, 1)
    backward(2, 2)
    qkv_grads(2)
    c1.start()
    c0.third()
    dn = nt(dproj[...], wqkv_ref[...])
    n_w = n_s[...]
    dx = dn - jnp.mean(dn, axis=-1, keepdims=True) - n_w * jnp.mean(dn * n_w, axis=-1, keepdims=True)
    ow[1] = (dx * rstd_s[...] + dy_w[...].astype(F32)).astype(BF16)
    c1.first()
    pack_out(1)
    bias_core()
    c0.fourth()
    c1.second()
    bias_x()
    c0.fifth()
    c1.third()
    for copy in rims_out[1]:
        copy.start()
    bias_y()
    finish(0, out_ref)
    c0.sixth()
    c1.fourth()
    bias_back_y()
    c0.last()
    unpack(0, CHUNKS[0])
    c1.fifth()
    bias_back_x()
    finish(1, dx_ref)
    bias_back_core()
    c1.sixth()
    bias_end()
    c1.last()
    unpack(CHUNKS[0], sum(CHUNKS))
    for chain in chains:
        chain.drain()


def fused(cells, cot, qkv_weight, out_weight, table, lon_size, lat_size, cells_total):
    c = out_weight.shape[0]
    heads, _, entries = table.shape
    groups = heads // GROUP
    consts = constants()
    ins = (cells, cot, qkv_weight, out_weight, table) + consts
    n, nz = lon_size // 4, lat_size // X_HI
    bshare = BIAS_TILES // (4 * n)
    gw = GROUP * HEAD
    vm = pltpu.VMEM
    dma = pltpu.SemaphoreType.DMA
    scratch = [vm(a.shape, a.dtype) for a in ins] + [
        dma((len(ins),)),
        vm((2, WH * PITCH, c), BF16),
        vm((2, RIM, c), BF16),
        vm((2, RIM, c), BF16),
        vm((groups, TOK, LANES), F32),
        vm((groups, TOK, LANES), F32),
        vm((ROWS, c), BF16),
        vm((ROWS, c), BF16),
        vm((ROWS, c), BF16),
        vm((c, ROWS), BF16),
        vm((ROWS, c), BF16),
        vm((ROWS, 3 * c), BF16),
        vm((3 * c, c), BF16),
        vm((2, ROWS, c), BF16),
        vm((2, RIM, c), BF16),
        vm((2, RIM, c), BF16),
        vm((ROWS, 2 * c), BF16),
        vm((WINDOWS, c, TOK), BF16),
        vm((WINDOWS, groups, gw, LANES), BF16),
        vm((WINDOWS, groups, TOK, LANES), F32),
        vm((c, LANES), BF16),
        vm((WINDOWS, groups, gw, LANES), BF16),
        vm((WINDOWS * gw, LANES), BF16),
        vm((heads, entries), F32),
        vm((heads * SLABS, WH * SPAN), F32),
        vm((256, 384), F32),
        vm((ROWS, c), F32),
        vm((ROWS, 1), F32),
        dma((2, 14)),
    ]
    tile = (16, 128)
    for tiles in CHUNKS:
        share = tiles // (2 * n * n)
        scratch += [
            vm((2, n, n, share) + tile, BF16),
            vm((n, n, share) + tile, BF16),
            vm((n, n, share) + tile, BF16),
            vm((n - 1, n, share) + tile, BF16),
            vm((n, share) + tile, BF16),
            vm((n - 1, share) + tile, BF16),
            vm((nz, share) + tile, BF16),
            vm((2, n, n, share) + tile, BF16),
            dma((2, 7)),
        ]
    scratch += [
        vm((2, 2, n, bshare) + tile, BF16),
        vm((2, n, bshare) + tile, BF16),
        vm((2, n, bshare) + tile, BF16),
        vm((n, bshare) + tile, BF16),
        vm((n, bshare) + tile, BF16),
        vm((n - 1, bshare) + tile, BF16),
        vm((2, 2, n, bshare) + tile, BF16),
        dma((2, 10)),
    ]
    kernel = functools.partial(
        body, lon_size, lat_size, groups, (c // heads) ** -0.5, cells_total ** -0.5
    )
    out_shape = (
        jax.ShapeDtypeStruct(cells.shape, BF16),
        jax.ShapeDtypeStruct(cells.shape, BF16),
        jax.ShapeDtypeStruct((c, 3 * c), F32),
        jax.ShapeDtypeStruct((c, c), F32),
        jax.ShapeDtypeStruct(table.shape, F32),
    )
    results = pl.pallas_call(
        kernel,
        out_shape=out_shape,
        in_specs=[pl.BlockSpec(memory_space=pl.ANY)] * len(ins),
        out_specs=(pl.BlockSpec(memory_space=pltpu.VMEM),) * len(out_shape),
        scratch_shapes=scratch,
        compiler_params=pltpu.CompilerParams(
            vmem_limit_bytes=60 * 1024 * 1024, collective_id=0, has_side_effects=True
        ),
        cost_estimate=pl.CostEstimate(flops=6_000_000_000, bytes_accessed=10_000_000, transcendentals=800_000),
    )(*ins)
    return handed_out(results)


def handed_out(arrays):
    cuts = [(i, k) for i, a in enumerate(arrays) for k in range(6 if i == 2 else 2 if i == 3 else 1)]

    def move(*refs):
        ins, outs, (sem, *held) = refs[:len(arrays)], refs[len(arrays):2 * len(arrays)], refs[2 * len(arrays):]
        into, out_of = [], []
        for j, (i, k) in enumerate(cuts):
            parts = sum(1 for at, _ in cuts if at == i)
            rows = arrays[i].shape[0] // parts
            at = pl.ds(k * rows, rows)
            into.append(pltpu.make_async_copy(ins[i].at[at], held[i].at[at], sem.at[0, j]))
            out_of.append(pltpu.make_async_copy(held[i].at[at], outs[i].at[at], sem.at[1, j]))
        for copy in into:
            copy.start()
        for first, second in zip(into, out_of):
            first.wait()
            second.start()
        for copy in out_of:
            copy.wait()

    return pl.pallas_call(
        move,
        out_shape=tuple(jax.ShapeDtypeStruct(a.shape, a.dtype) for a in arrays),
        in_specs=[pl.BlockSpec(memory_space=pl.ANY)] * len(arrays),
        out_specs=(pl.BlockSpec(memory_space=pl.ANY),) * len(arrays),
        scratch_shapes=[pltpu.SemaphoreType.DMA((2, len(cuts)))] + [pltpu.VMEM(a.shape, a.dtype) for a in arrays],
        compiler_params=pltpu.CompilerParams(vmem_limit_bytes=60 * 1024 * 1024),
    )(*arrays)


def on_device(cells, qkv_weight, out_weight, earth_bias, cotangent):
    lon_size, lat_size = lax.axis_size("lon"), lax.axis_size("lat")
    heads = earth_bias.shape[1]
    cells_total = LEV * cells.shape[1] * cells.shape[2] * lon_size * lat_size
    out, dx, gqkv, gout, dr = fused(
        cells.transpose(1, 2, 0, 3), cotangent.transpose(1, 2, 0, 3), qkv_weight, out_weight, earth_bias.transpose(1, 0, 2),
        lon_size, lat_size, cells_total
    )
    out, dx = out.transpose(2, 0, 1, 3), dx.transpose(2, 0, 1, 3)
    return out, dx, gqkv, gout, dr.transpose(1, 0, 2)


def solution(mesh):
    grid = P(None, "lat", "lon", None)
    return jax.shard_map(
        on_device,
        mesh=mesh,
        in_specs=(grid, P(), P(), P("lat", None, None), grid),
        out_specs=(grid, grid, P(), P(), P("lat", None, None)),
        check_vma=False,
    )
```

```python
import functools

import numpy as np
import jax
import jax.numpy as jnp
from jax import lax
from jax.experimental import pallas as pl
from jax.experimental.pallas import tpu as pltpu
from jax.sharding import PartitionSpec as P

LEV = 2
WH = 6
WW = 12
TOK = LEV * WH * WW
SLABS = LEV * WH
SPAN = 2 * WW - 1
GROUP = 4
HEAD = 32
LANES = GROUP * TOK
WINDOWS = 3
ROWS = WINDOWS * TOK
COLS = WINDOWS * WW
PITCH = 80
FINE_RIMS = ((0, 80, 0), (80, 80, 0), (160, 48, 0), (208, 48, 1), (256, 48, 2))
RIMS = ((0, 208, 0), (208, 48, 1), (256, 48, 2))
RIM_OF = ((0, 80), (80, 80), (160, 144))
RIM = 304
BIAS_TILES = 32
CHUNKS = (96, 96, 96)
X_HI = 2
F32 = jnp.float32
BF16 = jnp.bfloat16
MESH = pl.DeviceIdType.MESH


def nn(a, b):
    return lax.dot_general(a, b, (((1,), (0,)), ((), ())), preferred_element_type=F32)


def nt(a, b):
    return lax.dot_general(a, b, (((1,), (1,)), ((), ())), preferred_element_type=F32)


def constants():
    j1, i2, j2 = np.meshgrid(np.arange(WW), np.arange(WH), np.arange(WW), indexing="ij")
    spot = (i2 * SPAN + j1 - j2 + WW - 1).reshape(-1)
    spread = (spot[:, None] == np.arange(WH * SPAN)[None, :]).astype(np.float32)
    gather = np.zeros((144, spread.shape[0]), np.float32)
    gather[: WH * SPAN] = spread.T
    lane = np.arange(LANES)
    lane_col, lane_slab = lane // (SLABS * GROUP), lane // GROUP % SLABS
    token_of_lane = lane_slab * WW + lane_col
    pick = (np.arange(TOK)[:, None] == token_of_lane[None, :]).astype(np.float32)
    row_half = np.arange(TOK) // WW % WH >= WH - WH // 2
    lane_half = lane_slab % WH >= WH - WH // 2
    cross = np.where(row_half[:, None] != lane_half[None, :], -1e9, 0.0).astype(np.float32)
    own = np.zeros((ROWS, WH * PITCH), np.float32)
    rim = np.zeros((ROWS, RIM), np.float32)
    send = np.zeros((RIM, WH * PITCH), np.float32)
    h = WH // 2
    for w in range(WINDOWS):
        for z in range(LEV):
            for i in range(WH):
                for j in range(WW):
                    t = w * TOK + (z * WH + i) * WW + j
                    col = WW // 2 + w * WW + j
                    below, beside = i >= h, col >= COLS
                    row, k = ((i - h) if below else (i + h)), i % h
                    slab = row * PITCH + col % COLS * LEV + z
                    if not below and not beside:
                        own[t, slab] = 1
                        continue
                    if beside:
                        at = (256 if below else 208) + z * 18 + k * 6 + j - 6
                    elif w == WINDOWS - 1:
                        at = 160 + z * 18 + k * 6 + j
                    else:
                        at = 80 * w + z * 36 + k * 12 + j
                    rim[t, at] = 1
                    send[at, slab] = 1
    low = WH // 2 * PITCH
    rim_w = np.zeros((ROWS, 144), np.float32)
    rim_wt = np.zeros((RIM, TOK), np.float32)
    for w, (at, size) in enumerate(RIM_OF):
        block = rim[w * TOK:(w + 1) * TOK, at:at + size]
        rim_w[w * TOK:(w + 1) * TOK, :size] = block
        rim_wt[at:at + size] = block.T
    send_w = np.concatenate([send[:208, :low], send[208:256, low:], send[256:, :low]], axis=0)
    bf = lambda a: jnp.asarray(np.ascontiguousarray(a), BF16)
    return (
        bf(spread), bf(gather), bf(pick), jnp.asarray(cross, F32),
        bf(own[:, low:]), bf(rim_w), bf(send_w), bf(own[:, low:].T), bf(rim_wt), bf(send[:, :low].T),
        bf(send[208:256, low:].T),
    )


N_IN = 16


def body(lon_size, lat_size, groups, scale, grad_scale, *refs):
    (cells_h, cot_h, wqkv_h, wout_h, r_h) = refs[:5]
    consts_h = refs[5:N_IN]
    (out_ref, dx_ref, gqkv_ref, gout_ref, dr_ref) = refs[N_IN:N_IN + 5]
    (cells_v, cot_v, wqkv_ref, wout_ref, r_ref,
     spread_ref, gather_ref, pick_ref, cross_ref, own_ref, rim_ref, send_ref, ownt_ref, rimt_ref, sendt_ref,
     side_ref,
     load_sem, slab, rim_snd, rim_in, bt, db, x_w, dy_w, normed, normed_t, mix, dproj, wt, ow, rim_osnd, rim_out,
     kv, k_ts, q_ws, soft_s, m_ts, dm_ws, dq_ts, tab, rows_of, turned, n_s, rstd_s,
     halo_sem, *comm) = refs[N_IN + 5:]
    chunk_refs = [comm[i * 7:i * 7 + 7] for i in range(len(CHUNKS))]
    (bb, bcrecv, bs, bxrecv, by, byrecv, bfin, b_sem) = comm[len(CHUNKS) * 7:]
    c = wout_ref.shape[0]
    n, nz = lon_size // 4, lat_size // X_HI
    half = WH * WW
    blk = SLABS * GROUP
    gw = GROUP * HEAD

    lon, lat = lax.axis_index("lon"), lax.axis_index("lat")
    core, x_lo, y = lon % 2, lon // 2 % 2, lon // 4
    x_hi, z = lat // nz, lat % nz
    x = x_hi * 2 + x_lo
    other = 1 - core
    nxy = n * n
    p = y * n + x

    def dev(lon_at, lat_at):
        return {"lon": lon_at, "lat": lat_at}

    def chip(x_at, y_at):
        return dev((y_at * 2 + x_at % 2) * 2 + core, x_at // 2 * nz + z)

    sibling = dev(lon + 1 - 2 * core, lat)
    plane, zs, ys = [], [], []
    for o in range(1, nxy):
        q = (p + o) % nxy
        plane.append((q, chip(q % n, q // n)))
    for o in range(1, n):
        q = (y + o) % n
        ys.append((q, chip(x, q), (y + n - o) % n))
    for o in range(1, nz):
        zs.append((dev(lon, x_hi * nz + (z + o) % nz), (z + nz - o) % nz))
    pair = dev((y * 2 + 1 - x_lo) * 2 + core, lat)

    lon_prev, lon_next = (lon + lon_size - 1) % lon_size, (lon + 1) % lon_size
    lat_prev, lat_next = (lat + lat_size - 1) % lat_size, (lat + 1) % lat_size
    back = (dev(lon, lat_prev), dev(lon_prev, lat), dev(lon_prev, lat_prev))
    ahead = (dev(lon, lat_next), dev(lon_next, lat), dev(lon_next, lat_next))

    def remote(src, dst, send_sem, recv_sem, device):
        return pltpu.make_async_remote_copy(
            src_ref=src, dst_ref=dst, send_sem=send_sem, recv_sem=recv_sem, device_id=device, device_id_type=MESH
        )

    order = (
        (cells_h, cells_v), (consts_h[6], send_ref), (cot_h, cot_v), (r_h, r_ref), (consts_h[0], spread_ref),
        (consts_h[3], cross_ref), (wqkv_h, wqkv_ref), (consts_h[4], own_ref), (consts_h[5], rim_ref),
        (consts_h[2], pick_ref), (wout_h, wout_ref), (consts_h[8], rimt_ref), (consts_h[7], ownt_ref),
        (consts_h[9], sendt_ref), (consts_h[10], side_ref), (consts_h[1], gather_ref),
    )
    loads = [pltpu.make_async_copy(s, d, load_sem.at[i]) for i, (s, d) in enumerate(order)]
    for load in loads:
        load.start()

    barrier = pltpu.get_barrier_semaphore()

    def greet(device):
        pl.semaphore_signal(barrier, inc=1, device_id=device, device_id_type=MESH)

    partners = back + ahead + (sibling,)
    partners += tuple(d for _, d in plane) + tuple(d for d, _ in zs)
    for device in partners:
        greet(device)

    def rim_copies(f, snd, rcv, devices, base, parts):
        return [
            remote(
                snd.at[f, pl.ds(at, size)], rcv.at[f, pl.ds(at, size)],
                halo_sem.at[0, base + k], halo_sem.at[1, base + k], devices[to],
            )
            for k, (at, size, to) in enumerate(parts)
        ]

    rims_in = (
        rim_copies(0, rim_snd, rim_in, back, 0, FINE_RIMS),
        rim_copies(1, rim_snd, rim_in, back, 5, RIMS),
    )
    rims_out = (
        rim_copies(0, rim_osnd, rim_out, ahead, 8, RIMS),
        rim_copies(1, rim_osnd, rim_out, ahead, 11, RIMS),
    )
    low = WH // 2 * PITCH
    for f, src in enumerate((cells_v, cot_v)):
        loads[2 * f].wait()
        for s in range(WH):
            slab[f, s * PITCH:(s + 1) * PITCH, :] = jnp.concatenate(
                [src[s].reshape(COLS * LEV, c), jnp.zeros((PITCH - COLS * LEV, c), BF16)], axis=0
            )
        if f == 0:
            loads[1].wait()
        rim_snd[f, :208] = nn(send_ref[:208], slab[f, :low]).astype(BF16)
        rim_snd[f, 208:256] = nn(send_ref[208:256], slab[f, low:]).astype(BF16)
        rim_snd[f, 256:] = nn(send_ref[256:], slab[f, :low]).astype(BF16)
        if f == 0:
            pl.semaphore_wait(barrier, len(partners))
        for copy in rims_in[f]:
            copy.start()

    for load in loads[3:6]:
        load.wait()
    last = (lat == lat_size - 1).astype(F32)
    tab[...] = r_ref[:, 0, :]
    width = WH * SPAN

    def segment(z1, z2, i1):
        return pl.ds(((z1 * LEV + z2) * WH + i1) * width, width)

    for z2 in range(LEV):
        for z1 in range(LEV):
            for i1 in range(WH):
                piece = tab[:, segment(z1, z2, i1)]
                for g in range(groups):
                    at = g * blk + (z1 * WH + i1) * GROUP
                    rows_of[at:at + GROUP, :] = piece[g * GROUP:(g + 1) * GROUP]
        table = rows_of[...]
        hi = table.astype(BF16)
        rest = table - hi.astype(F32)
        mid = rest.astype(BF16)
        lo = (rest - mid.astype(F32)).astype(BF16)
        spread = spread_ref[...]
        u = nt(spread, hi) + nt(spread, mid) + nt(spread, lo)
        for g in range(groups):
            rows = jnp.concatenate(
                [u[j * half:(j + 1) * half, g * blk:(g + 1) * blk] for j in range(WW)], axis=1
            )
            keep = pl.ds(z2 * half, half)
            bt[g, keep, :] = rows + cross_ref[keep, :] * last
    row = lax.broadcasted_iota(jnp.int32, (c, c), 0)
    col = lax.broadcasted_iota(jnp.int32, (c, c), 1)
    eye = (row == col).astype(F32).astype(BF16)
    head_row = lax.broadcasted_iota(jnp.int32, (gw, LANES), 0) // HEAD
    head_lane = lax.broadcasted_iota(jnp.int32, (gw, LANES), 1) % GROUP
    mine = (head_row == head_lane).astype(F32)
    for load in loads[6:]:
        load.wait()
    for part in range(3):
        wt[part * c:(part + 1) * c, :] = nt(eye, wqkv_ref[:, part * c:(part + 1) * c]).astype(BF16)
    pick = pick_ref[...]

    def arrive(f, w, ref):
        if f == 0:
            parts = rims_in[0][w:w + 1] if w < WINDOWS - 1 else rims_in[0][w:]
        else:
            parts = rims_in[1][:1] if w == 0 else rims_in[1][1:] if w == WINDOWS - 1 else []
        for copy in parts:
            copy.wait()
        at, (first, size) = slice(w * TOK, (w + 1) * TOK), RIM_OF[w]
        ref[at, :] = (
            nn(own_ref[at, :], slab[f, low:]) + nn(rim_ref[at, :size], rim_in[f, first:first + size])
        ).astype(BF16)

    def at_of(w):
        return slice(w * TOK, (w + 1) * TOK)

    def g_of(g, part=0):
        return slice(part * c + g * gw, part * c + (g + 1) * gw)

    def forward(w):
        at = at_of(w)
        arrive(0, w, x_w)
        cells = x_w[at, :].astype(F32)
        average = jnp.mean(cells, axis=-1, keepdims=True)
        centred = cells - average
        rstd = lax.rsqrt(jnp.mean(centred * centred, axis=-1, keepdims=True) + 1e-05)
        rstd_s[at, :] = rstd
        n_w = centred * rstd
        n_s[at, :] = n_w
        here = n_w.astype(BF16)
        normed[at, :] = here
        kv[at, :] = nn(here, wqkv_ref[:, c:]).astype(BF16)
        qkv_t = nt(wt[...], here).astype(BF16)
        q_all = nn(qkv_t[:c], pick)
        k_ts[w] = qkv_t[c:2 * c]
        for g in range(groups):
            q_wide = (q_all[g_of(g)] * mine).astype(BF16)
            q_ws[w, g] = q_wide
            s = nn(kv[at, g_of(g)], q_wide) * scale + bt[g]
            top = jnp.max(s, axis=0, keepdims=True)
            e = jnp.exp(s - top)
            soft = e * (1.0 / jnp.sum(e, axis=0, keepdims=True))
            soft_s[w, g] = soft
            m_ts[g_of(g), :] = (nn(qkv_t[g_of(g, 2)], soft.astype(BF16)) * mine).astype(BF16)
        mix[at, :] = nt(pick, m_ts[...]).astype(BF16)

    def widen(w):
        dm_t = nt(wout_ref[...], dy_w[at_of(w), :]).astype(BF16)
        dm_all = nn(dm_t, pick)
        for g in range(groups):
            dm_ws[w, g] = (dm_all[g_of(g)] * mine).astype(BF16)

    def backward(g, w):
        at = at_of(w)
        soft = soft_s[w, g]
        dm_wide = dm_ws[w, g]
        da = nn(kv[at, g_of(g, 1)], dm_wide)
        ds = soft * (da - jnp.sum(soft * da, axis=0, keepdims=True))
        if w == 0:
            db[g] = ds
        else:
            db[g] += ds
        ds = ds.astype(BF16)
        dq_ts[w * gw:(w + 1) * gw, :] = (nn(k_ts[w, g_of(g), :], ds) * (mine * scale)).astype(BF16)
        dproj[at, g_of(g, 1)] = (nt(ds, q_ws[w, g]) * scale).astype(BF16)
        dproj[at, g_of(g, 2)] = nt(soft.astype(BF16), dm_wide).astype(BF16)

    def tile_at(t):
        i = 0
        while t >= CHUNKS[i]:
            t -= CHUNKS[i]
            i += 1
        half_tiles = CHUNKS[i] // 2
        share = half_tiles // nxy
        return i, (t // half_tiles, t % half_tiles // share, t % share)

    def put(t, value):
        i, at = tile_at(t)
        chunk_refs[i][0][at] = value.astype(BF16)

    def out_grads():
        normed_t[...] = nt(eye, normed[...]).astype(BF16)
        grad = nn(nt(eye, mix[...]).astype(BF16), dy_w[...]) * grad_scale
        for k in range(3):
            for r in range(24):
                put(k * 24 + r, grad[r * 16:(r + 1) * 16, k * 128:(k + 1) * 128])

    def qkv_grads(g):
        dq = nt(pick, dq_ts[...]).astype(BF16)
        for w in range(WINDOWS):
            dproj[at_of(w), g_of(g)] = dq[:, w * gw:(w + 1) * gw]
        for part in range(3):
            grad = nn(normed_t[...], dproj[:, g_of(g, part)]) * grad_scale
            for r in range(24):
                put(72 + 72 * g + part * 24 + r, grad[r * 16:(r + 1) * 16])

    class Chain:
        def __init__(self, refs):
            (self.gb, self.crecv, self.xs, self.xrecv, self.zbuf, self.fin, self.sem) = refs

        def send(self, stage, src, dst, device):
            remote(src, dst, self.sem.at[0, stage], self.sem.at[1, stage], device).start()

        def wait(self, side, stage, like):
            pltpu.make_async_copy(like, like, self.sem.at[side, stage]).wait()

        def start(self):
            self.send(0, self.gb.at[other], self.crecv, sibling)

        def first(self):
            self.wait(1, 0, self.crecv)
            self.xs[...] = (self.gb[core].astype(F32) + self.crecv[...].astype(F32)).astype(BF16)
            for o, (q, d) in enumerate(plane):
                self.send(1, self.xs.at[q], self.xrecv.at[o], d)

        def second(self):
            self.wait(1, 1, self.xrecv)
            total = self.xs[p].astype(F32)
            for o in range(nxy - 1):
                total += self.xrecv[o].astype(F32)
            self.zbuf[0] = total.astype(BF16)
            for o, (d, _) in enumerate(zs):
                self.send(2, self.zbuf.at[0], self.zbuf.at[o + 1], d)

        def third(self):
            if nz > 1:
                self.wait(1, 2, self.zbuf.at[pl.ds(1, nz - 1)])
            total = self.zbuf[z].astype(F32)
            for k in range(1, nz):
                total += self.zbuf[(z + nz - k) % nz].astype(F32)
            mine_at = self.fin.at[core, p]
            mine_at[...] = total.astype(BF16)
            for _, d in plane:
                self.send(3, mine_at, mine_at, d)

        def fourth(self):
            self.wait(1, 3, self.xrecv)
            self.send(4, self.fin.at[core], self.fin.at[core], sibling)

        def last(self):
            self.wait(1, 4, self.fin.at[other])

        def drain(self):
            self.wait(0, 0, self.crecv)
            self.wait(0, 1, self.xrecv)
            if nz > 1:
                self.wait(0, 2, self.zbuf.at[pl.ds(1, nz - 1)])
            self.wait(0, 3, self.xrecv)
            self.wait(0, 4, self.crecv)

    chains = [Chain(r) for r in chunk_refs]

    def unpack(first, end):
        for t in range(first, end):
            i, at = tile_at(t)
            value = chains[i].fin[at].astype(F32)
            r, k = t % 24, t // 24
            rows = slice(r * 16, (r + 1) * 16)
            if k < 3:
                gout_ref[rows, k * 128:(k + 1) * 128] = value
            else:
                g, part = (k - 3) // 3, (k - 3) % 3
                gqkv_ref[rows, g_of(g, part)] = value

    bshare = BIAS_TILES // (4 * n)

    def bcopy(k, src, dst, device):
        return remote(src, dst, b_sem.at[0, k], b_sem.at[1, k], device)

    def bcore_copy():
        return bcopy(0, bb.at[other], bcrecv, sibling)

    def bx_copy():
        return bcopy(1, bs.at[1 - x_lo], bxrecv, pair)

    def by_copies():
        return [bcopy(2 + o, by.at[q], byrecv.at[o], d) for o, (q, d, _) in enumerate(ys)]

    def by_back(here=True):
        at = [y if here else q for _, _, q in ys]
        return [
            bcopy(5 + o, bfin.at[core, x_lo, at[o]], bfin.at[core, x_lo, at[o]], d)
            for o, (_, d, _) in enumerate(ys)
        ]

    def bx_back(x_at):
        return bcopy(8, bfin.at[core, x_at], bfin.at[core, x_at], pair)

    def bcore_back(half_at):
        return bcopy(9, bfin.at[half_at], bfin.at[half_at], sibling)

    def bias_core():
        rows = jnp.concatenate(
            [
                jnp.concatenate(
                    [
                        db[g, z2 * half:(z2 + 1) * half, j * blk:(j + 1) * blk]
                        for z2 in range(LEV)
                        for g in range(groups)
                    ]
                    + [jnp.zeros((half, 96), F32)],
                    axis=1,
                )
                for j in range(WW)
            ],
            axis=0,
        ).astype(BF16)
        dr = nn(gather_ref[...], rows).astype(BF16)
        for t in range(BIAS_TILES):
            k, r = t // 9, t % 9
            tile = dr[r * 16:(r + 1) * 16, k * 128:(k + 1) * 128] if k < 3 else jnp.zeros((16, 128), BF16)
            bb[bias_at(t)] = tile
        bcore_copy().start()

    def bias_at(t):
        return t // 16, t % 16 // (n * bshare), t % (n * bshare) // bshare, t % bshare

    def bias_x():
        bcore_copy().wait()
        bs[...] = (bb[core].astype(F32) + bcrecv[...].astype(F32)).astype(BF16)
        bx_copy().start()

    def bias_y():
        bx_copy().wait()
        by[...] = (bs[x_lo].astype(F32) + bxrecv[...].astype(F32)).astype(BF16)
        for copy in by_copies():
            copy.start()

    def bias_back_y():
        for copy in by_copies():
            copy.wait()
        total = by[y].astype(F32)
        for o in range(n - 1):
            total += byrecv[o].astype(F32)
        bfin[core, x_lo, y] = total.astype(BF16)
        for copy in by_back():
            copy.start()

    def bias_back_x():
        for copy in by_back():
            copy.wait_send()
        for copy in by_back(False):
            copy.wait_recv()
        bx_back(x_lo).start()

    def bias_back_core():
        bx_back(x_lo).wait_send()
        bx_back(1 - x_lo).wait_recv()
        bcore_back(core).start()

    def bias_end():
        bcore_back(core).wait_send()
        bcore_back(other).wait_recv()
        turned[144:, :] = jnp.zeros((256 - 144, 384), F32)
        for t in range(27):
            k, r = t // 9, t % 9
            turned[r * 16:(r + 1) * 16, k * 128:(k + 1) * 128] = bfin[bias_at(t)].astype(F32)
        flat = turned[...].T
        for z2 in range(LEV):
            for z1 in range(LEV):
                for i1 in range(WH):
                    for g in range(groups):
                        at = z2 * groups * blk + g * blk + (z1 * WH + i1) * GROUP
                        tab[g * GROUP:(g + 1) * GROUP, segment(z1, z2, i1)] = flat[at:at + GROUP, :width]
        dr_ref[:, 0, :] = tab[...]

    def pack_out(f):
        for w, (first, size) in enumerate(RIM_OF):
            rim_osnd[f, first:first + size] = nn(rimt_ref[first:first + size], ow[f, at_of(w)]).astype(BF16)

    def finish(f, ref):
        for copy in rims_out[f]:
            copy.wait()
        upper = nn(sendt_ref[...], rim_out[f]).astype(BF16)
        lower = (nn(ownt_ref[...], ow[f]) + nn(side_ref[...], rim_out[f, 208:256])).astype(BF16)
        for s in range(WH):
            full, r = (upper, s) if s < WH // 2 else (lower, s - WH // 2)
            ref[s] = full[r * PITCH:r * PITCH + COLS * LEV].reshape(COLS, LEV, c)

    c0, c1, c2 = chains
    for w in range(WINDOWS):
        forward(w)
    ow[0] = (x_w[...].astype(F32) + nn(mix[...], wout_ref[...])).astype(BF16)
    pack_out(0)
    for copy in rims_out[0]:
        copy.start()
    for w in range(WINDOWS):
        arrive(1, w, dy_w)
    out_grads()
    for w in range(WINDOWS):
        widen(w)
    for w in range(WINDOWS):
        backward(0, w)
    qkv_grads(0)
    c0.start()
    backward(1, 0)
    backward(1, 1)
    c0.first()
    backward(1, 2)
    qkv_grads(1)
    c1.start()
    backward(2, 0)
    backward(2, 1)
    c1.first()
    backward(2, 2)
    qkv_grads(2)
    c2.start()
    c0.second()
    dn = nt(dproj[...], wqkv_ref[...])
    n_w = n_s[...]
    dx = dn - jnp.mean(dn, axis=-1, keepdims=True) - n_w * jnp.mean(dn * n_w, axis=-1, keepdims=True)
    ow[1] = (dx * rstd_s[...] + dy_w[...].astype(F32)).astype(BF16)
    c2.first()
    pack_out(1)
    c1.second()
    bias_core()
    c0.third()
    c2.second()
    for copy in rims_out[1]:
        copy.start()
    bias_x()
    c1.third()
    finish(0, out_ref)
    c0.fourth()
    c2.third()
    bias_y()
    c0.last()
    unpack(0, 96)
    c1.fourth()
    bias_back_y()
    c2.fourth()
    bias_back_x()
    c1.last()
    unpack(96, 192)
    finish(1, dx_ref)
    bias_back_core()
    bias_end()
    c2.last()
    unpack(192, 288)
    for chain in chains:
        chain.drain()


def fused(cells, cot, qkv_weight, out_weight, table, lon_size, lat_size, cells_total):
    c = out_weight.shape[0]
    heads, _, entries = table.shape
    groups = heads // GROUP
    consts = constants()
    ins = (cells, cot, qkv_weight, out_weight, table) + consts
    n, nz = lon_size // 4, lat_size // X_HI
    bshare = BIAS_TILES // (4 * n)
    gw = GROUP * HEAD
    vm = pltpu.VMEM
    dma = pltpu.SemaphoreType.DMA
    scratch = [vm(a.shape, a.dtype) for a in ins] + [
        dma((len(ins),)),
        vm((2, WH * PITCH, c), BF16),
        vm((2, RIM, c), BF16),
        vm((2, RIM, c), BF16),
        vm((groups, TOK, LANES), F32),
        vm((groups, TOK, LANES), F32),
        vm((ROWS, c), BF16),
        vm((ROWS, c), BF16),
        vm((ROWS, c), BF16),
        vm((c, ROWS), BF16),
        vm((ROWS, c), BF16),
        vm((ROWS, 3 * c), BF16),
        vm((3 * c, c), BF16),
        vm((2, ROWS, c), BF16),
        vm((2, RIM, c), BF16),
        vm((2, RIM, c), BF16),
        vm((ROWS, 2 * c), BF16),
        vm((WINDOWS, c, TOK), BF16),
        vm((WINDOWS, groups, gw, LANES), BF16),
        vm((WINDOWS, groups, TOK, LANES), F32),
        vm((c, LANES), BF16),
        vm((WINDOWS, groups, gw, LANES), BF16),
        vm((WINDOWS * gw, LANES), BF16),
        vm((heads, entries), F32),
        vm((heads * SLABS, WH * SPAN), F32),
        vm((256, 384), F32),
        vm((ROWS, c), F32),
        vm((ROWS, 1), F32),
        dma((2, 14)),
    ]
    tile = (16, 128)
    for tiles in CHUNKS:
        share = tiles // (2 * n * n)
        scratch += [
            vm((2, n * n, share) + tile, BF16),
            vm((n * n, share) + tile, BF16),
            vm((n * n, share) + tile, BF16),
            vm((n * n - 1, share) + tile, BF16),
            vm((nz, share) + tile, BF16),
            vm((2, n * n, share) + tile, BF16),
            dma((2, 5)),
        ]
    scratch += [
        vm((2, 2, n, bshare) + tile, BF16),
        vm((2, n, bshare) + tile, BF16),
        vm((2, n, bshare) + tile, BF16),
        vm((n, bshare) + tile, BF16),
        vm((n, bshare) + tile, BF16),
        vm((n - 1, bshare) + tile, BF16),
        vm((2, 2, n, bshare) + tile, BF16),
        dma((2, 10)),
    ]
    kernel = functools.partial(
        body, lon_size, lat_size, groups, (c // heads) ** -0.5, cells_total ** -0.5
    )
    out_shape = (
        jax.ShapeDtypeStruct(cells.shape, BF16),
        jax.ShapeDtypeStruct(cells.shape, BF16),
        jax.ShapeDtypeStruct((c, 3 * c), F32),
        jax.ShapeDtypeStruct((c, c), F32),
        jax.ShapeDtypeStruct(table.shape, F32),
    )
    results = pl.pallas_call(
        kernel,
        out_shape=out_shape,
        in_specs=[pl.BlockSpec(memory_space=pl.ANY)] * len(ins),
        out_specs=(pl.BlockSpec(memory_space=pltpu.VMEM),) * len(out_shape),
        scratch_shapes=scratch,
        compiler_params=pltpu.CompilerParams(
            vmem_limit_bytes=60 * 1024 * 1024, collective_id=0, has_side_effects=True
        ),
        cost_estimate=pl.CostEstimate(flops=6_000_000_000, bytes_accessed=10_000_000, transcendentals=800_000),
    )(*ins)
    return handed_out(results)


def handed_out(arrays):
    cuts = [(i, k) for i, a in enumerate(arrays) for k in range(6 if i == 2 else 2 if i == 3 else 1)]

    def move(*refs):
        ins, outs, (sem, *held) = refs[:len(arrays)], refs[len(arrays):2 * len(arrays)], refs[2 * len(arrays):]
        into, out_of = [], []
        for j, (i, k) in enumerate(cuts):
            parts = sum(1 for at, _ in cuts if at == i)
            rows = arrays[i].shape[0] // parts
            at = pl.ds(k * rows, rows)
            into.append(pltpu.make_async_copy(ins[i].at[at], held[i].at[at], sem.at[0, j]))
            out_of.append(pltpu.make_async_copy(held[i].at[at], outs[i].at[at], sem.at[1, j]))
        for copy in into:
            copy.start()
        for first, second in zip(into, out_of):
            first.wait()
            second.start()
        for copy in out_of:
            copy.wait()

    return pl.pallas_call(
        move,
        out_shape=tuple(jax.ShapeDtypeStruct(a.shape, a.dtype) for a in arrays),
        in_specs=[pl.BlockSpec(memory_space=pl.ANY)] * len(arrays),
        out_specs=(pl.BlockSpec(memory_space=pl.ANY),) * len(arrays),
        scratch_shapes=[pltpu.SemaphoreType.DMA((2, len(cuts)))] + [pltpu.VMEM(a.shape, a.dtype) for a in arrays],
        compiler_params=pltpu.CompilerParams(vmem_limit_bytes=60 * 1024 * 1024),
    )(*arrays)


def on_device(cells, qkv_weight, out_weight, earth_bias, cotangent):
    lon_size, lat_size = lax.axis_size("lon"), lax.axis_size("lat")
    heads = earth_bias.shape[1]
    cells_total = LEV * cells.shape[1] * cells.shape[2] * lon_size * lat_size
    out, dx, gqkv, gout, dr = fused(
        cells.transpose(1, 2, 0, 3), cotangent.transpose(1, 2, 0, 3), qkv_weight, out_weight, earth_bias.transpose(1, 0, 2),
        lon_size, lat_size, cells_total
    )
    out, dx = out.transpose(2, 0, 1, 3), dx.transpose(2, 0, 1, 3)
    return out, dx, gqkv, gout, dr.transpose(1, 0, 2)


def solution(mesh):
    grid = P(None, "lat", "lon", None)
    return jax.shard_map(
        on_device,
        mesh=mesh,
        in_specs=(grid, P(), P(), P("lat", None, None), grid),
        out_specs=(grid, grid, P(), P(), P("lat", None, None)),
        check_vma=False,
    )
```

```python
import functools

import numpy as np
import jax
import jax.numpy as jnp
from jax import lax
from jax.experimental import pallas as pl
from jax.experimental.pallas import tpu as pltpu
from jax.sharding import PartitionSpec as P

LEV = 2
WH = 6
WW = 12
TOK = LEV * WH * WW
SLABS = LEV * WH
SPAN = 2 * WW - 1
GROUP = 4
HEAD = 32
LANES = GROUP * TOK
WINDOWS = 3
ROWS = WINDOWS * TOK
COLS = WINDOWS * WW
PITCH = 80
FINE_RIMS = ((0, 80, 0), (80, 80, 0), (160, 48, 0), (208, 48, 1), (256, 48, 2))
RIMS = ((0, 208, 0), (208, 48, 1), (256, 48, 2))
RIM_OF = ((0, 80), (80, 80), (160, 144))
RIM = 304
BIAS_TILES = 32
CHUNKS = (96, 96, 96)
X_HI = 2
F32 = jnp.float32
BF16 = jnp.bfloat16
MESH = pl.DeviceIdType.MESH


def nn(a, b):
    return lax.dot_general(a, b, (((1,), (0,)), ((), ())), preferred_element_type=F32)


def nt(a, b):
    return lax.dot_general(a, b, (((1,), (1,)), ((), ())), preferred_element_type=F32)


def constants():
    j1, i2, j2 = np.meshgrid(np.arange(WW), np.arange(WH), np.arange(WW), indexing="ij")
    spot = (i2 * SPAN + j1 - j2 + WW - 1).reshape(-1)
    spread = (spot[:, None] == np.arange(WH * SPAN)[None, :]).astype(np.float32)
    gather = np.zeros((144, spread.shape[0]), np.float32)
    gather[: WH * SPAN] = spread.T
    lane = np.arange(LANES)
    lane_col, lane_slab = lane // (SLABS * GROUP), lane // GROUP % SLABS
    token_of_lane = lane_slab * WW + lane_col
    pick = (np.arange(TOK)[:, None] == token_of_lane[None, :]).astype(np.float32)
    row_half = np.arange(TOK) // WW % WH >= WH - WH // 2
    lane_half = lane_slab % WH >= WH - WH // 2
    cross = np.where(row_half[:, None] != lane_half[None, :], -1e9, 0.0).astype(np.float32)
    own = np.zeros((ROWS, WH * PITCH), np.float32)
    rim = np.zeros((ROWS, RIM), np.float32)
    send = np.zeros((RIM, WH * PITCH), np.float32)
    h = WH // 2
    for w in range(WINDOWS):
        for z in range(LEV):
            for i in range(WH):
                for j in range(WW):
                    t = w * TOK + (z * WH + i) * WW + j
                    col = WW // 2 + w * WW + j
                    below, beside = i >= h, col >= COLS
                    row, k = ((i - h) if below else (i + h)), i % h
                    slab = row * PITCH + col % COLS * LEV + z
                    if not below and not beside:
                        own[t, slab] = 1
                        continue
                    if beside:
                        at = (256 if below else 208) + z * 18 + k * 6 + j - 6
                    elif w == WINDOWS - 1:
                        at = 160 + z * 18 + k * 6 + j
                    else:
                        at = 80 * w + z * 36 + k * 12 + j
                    rim[t, at] = 1
                    send[at, slab] = 1
    low = WH // 2 * PITCH
    rim_w = np.zeros((ROWS, 144), np.float32)
    rim_wt = np.zeros((RIM, TOK), np.float32)
    for w, (at, size) in enumerate(RIM_OF):
        block = rim[w * TOK:(w + 1) * TOK, at:at + size]
        rim_w[w * TOK:(w + 1) * TOK, :size] = block
        rim_wt[at:at + size] = block.T
    send_w = np.concatenate([send[:208, :low], send[208:256, low:], send[256:, :low]], axis=0)
    bf = lambda a: jnp.asarray(np.ascontiguousarray(a), BF16)
    return (
        bf(spread), bf(gather), bf(pick), jnp.asarray(cross, F32),
        bf(own[:, low:]), bf(rim_w), bf(send_w), bf(own[:, low:].T), bf(rim_wt), bf(send[:, :low].T),
        bf(send[208:256, low:].T),
    )


N_IN = 16


def body(lon_size, lat_size, groups, scale, grad_scale, *refs):
    (cells_h, cot_h, wqkv_h, wout_h, r_h) = refs[:5]
    consts_h = refs[5:N_IN]
    outs_h = refs[N_IN:N_IN + 5]
    (cells_v, cot_v, wqkv_ref, wout_ref, r_ref,
     spread_ref, gather_ref, pick_ref, cross_ref, own_ref, rim_ref, send_ref, ownt_ref, rimt_ref, sendt_ref,
     side_ref,
     load_sem, slab, rim_snd, rim_in, bt, db, x_w, dy_w, normed, normed_t, mix, dproj, wt, ow, rim_osnd, rim_out,
     kv, k_ts, q_ws, soft_s, m_ts, dm_ws, dq_ts, tab, rows_of, turned, n_s, rstd_s,
     halo_sem, *comm) = refs[N_IN + 5:]
    (out_ref, dx_ref, gqkv_ref, gout_ref, dr_ref, out_sem) = comm[-6:]
    chunk_refs = [comm[i * 7:i * 7 + 7] for i in range(len(CHUNKS))]
    (bb, brecv, bfin, b_sem) = comm[len(CHUNKS) * 7:-6]
    c = wout_ref.shape[0]
    n, nz = lon_size // 4, lat_size // X_HI
    half = WH * WW
    blk = SLABS * GROUP
    gw = GROUP * HEAD

    lon, lat = lax.axis_index("lon"), lax.axis_index("lat")
    core, x_lo, y = lon % 2, lon // 2 % 2, lon // 4
    x_hi, z = lat // nz, lat % nz
    x = x_hi * 2 + x_lo
    other = 1 - core
    nxy = n * n
    p = y * n + x

    def dev(lon_at, lat_at):
        return {"lon": lon_at, "lat": lat_at}

    def chip(x_at, y_at):
        return dev((y_at * 2 + x_at % 2) * 2 + core, x_at // 2 * nz + z)

    sibling = dev(lon + 1 - 2 * core, lat)
    plane, zs, line = [], [], []
    for o in range(1, nxy):
        q = (p + o) % nxy
        plane.append((q, chip(q % n, q // n)))
    for o in range(1, lon_size):
        q = (lon + o) % lon_size
        line.append((q, dev(q, lat)))
    for o in range(1, nz):
        zs.append((dev(lon, x_hi * nz + (z + o) % nz), (z + nz - o) % nz))

    lon_prev, lon_next = (lon + lon_size - 1) % lon_size, (lon + 1) % lon_size
    lat_prev, lat_next = (lat + lat_size - 1) % lat_size, (lat + 1) % lat_size
    back = (dev(lon, lat_prev), dev(lon_prev, lat), dev(lon_prev, lat_prev))
    ahead = (dev(lon, lat_next), dev(lon_next, lat), dev(lon_next, lat_next))

    def remote(src, dst, send_sem, recv_sem, device):
        return pltpu.make_async_remote_copy(
            src_ref=src, dst_ref=dst, send_sem=send_sem, recv_sem=recv_sem, device_id=device, device_id_type=MESH
        )

    order = (
        (cells_h, cells_v), (consts_h[6], send_ref), (cot_h, cot_v), (r_h, r_ref), (consts_h[0], spread_ref),
        (consts_h[3], cross_ref), (wqkv_h, wqkv_ref), (consts_h[4], own_ref), (consts_h[5], rim_ref),
        (consts_h[2], pick_ref), (wout_h, wout_ref), (consts_h[8], rimt_ref), (consts_h[7], ownt_ref),
        (consts_h[9], sendt_ref), (consts_h[10], side_ref), (consts_h[1], gather_ref),
    )
    loads = [pltpu.make_async_copy(s, d, load_sem.at[i]) for i, (s, d) in enumerate(order)]
    for load in loads:
        load.start()

    barrier = pltpu.get_barrier_semaphore()

    def greet(device):
        pl.semaphore_signal(barrier, inc=1, device_id=device, device_id_type=MESH)

    partners = back + ahead
    partners += tuple(d for _, d in plane + line) + tuple(d for d, _ in zs)
    for device in partners:
        greet(device)

    def rim_copies(f, snd, rcv, devices, base, parts):
        return [
            remote(
                snd.at[f, pl.ds(at, size)], rcv.at[f, pl.ds(at, size)],
                halo_sem.at[0, base + k], halo_sem.at[1, base + k], devices[to],
            )
            for k, (at, size, to) in enumerate(parts)
        ]

    rims_in = (
        rim_copies(0, rim_snd, rim_in, back, 0, FINE_RIMS),
        rim_copies(1, rim_snd, rim_in, back, 5, RIMS),
    )
    rims_out = (
        rim_copies(0, rim_osnd, rim_out, ahead, 8, RIMS),
        rim_copies(1, rim_osnd, rim_out, ahead, 11, RIMS),
    )
    low = WH // 2 * PITCH
    for f, src in enumerate((cells_v, cot_v)):
        loads[2 * f].wait()
        for s in range(WH):
            slab[f, s * PITCH:(s + 1) * PITCH, :] = jnp.concatenate(
                [src[s].reshape(COLS * LEV, c), jnp.zeros((PITCH - COLS * LEV, c), BF16)], axis=0
            )
        if f == 0:
            loads[1].wait()
        rim_snd[f, :208] = nn(send_ref[:208], slab[f, :low]).astype(BF16)
        rim_snd[f, 208:256] = nn(send_ref[208:256], slab[f, low:]).astype(BF16)
        rim_snd[f, 256:] = nn(send_ref[256:], slab[f, :low]).astype(BF16)
        if f == 0:
            pl.semaphore_wait(barrier, len(partners))
        for copy in rims_in[f]:
            copy.start()

    for load in loads[3:6]:
        load.wait()
    last = (lat == lat_size - 1).astype(F32)
    tab[...] = r_ref[:, 0, :]
    width = WH * SPAN

    def segment(z1, z2, i1):
        return pl.ds(((z1 * LEV + z2) * WH + i1) * width, width)

    for z2 in range(LEV):
        for z1 in range(LEV):
            for i1 in range(WH):
                piece = tab[:, segment(z1, z2, i1)]
                for g in range(groups):
                    at = g * blk + (z1 * WH + i1) * GROUP
                    rows_of[at:at + GROUP, :] = piece[g * GROUP:(g + 1) * GROUP]
        table = rows_of[...]
        hi = table.astype(BF16)
        rest = table - hi.astype(F32)
        mid = rest.astype(BF16)
        lo = (rest - mid.astype(F32)).astype(BF16)
        spread = spread_ref[...]
        u = nt(spread, hi) + nt(spread, mid) + nt(spread, lo)
        for g in range(groups):
            rows = jnp.concatenate(
                [u[j * half:(j + 1) * half, g * blk:(g + 1) * blk] for j in range(WW)], axis=1
            )
            keep = pl.ds(z2 * half, half)
            bt[g, keep, :] = rows + cross_ref[keep, :] * last
    row = lax.broadcasted_iota(jnp.int32, (c, c), 0)
    col = lax.broadcasted_iota(jnp.int32, (c, c), 1)
    eye = (row == col).astype(F32).astype(BF16)
    head_row = lax.broadcasted_iota(jnp.int32, (gw, LANES), 0) // HEAD
    head_lane = lax.broadcasted_iota(jnp.int32, (gw, LANES), 1) % GROUP
    mine = (head_row == head_lane).astype(F32)
    for load in loads[6:]:
        load.wait()
    for part in range(3):
        wt[part * c:(part + 1) * c, :] = nt(eye, wqkv_ref[:, part * c:(part + 1) * c]).astype(BF16)
    pick = pick_ref[...]

    def arrive(f, w, ref):
        if f == 0:
            parts = rims_in[0][w:w + 1] if w < WINDOWS - 1 else rims_in[0][w:]
        else:
            parts = rims_in[1][:1] if w == 0 else rims_in[1][1:] if w == WINDOWS - 1 else []
        for copy in parts:
            copy.wait()
        at, (first, size) = slice(w * TOK, (w + 1) * TOK), RIM_OF[w]
        ref[at, :] = (
            nn(own_ref[at, :], slab[f, low:]) + nn(rim_ref[at, :size], rim_in[f, first:first + size])
        ).astype(BF16)

    def at_of(w):
        return slice(w * TOK, (w + 1) * TOK)

    def g_of(g, part=0):
        return slice(part * c + g * gw, part * c + (g + 1) * gw)

    def forward(w):
        at = at_of(w)
        arrive(0, w, x_w)
        cells = x_w[at, :].astype(F32)
        average = jnp.mean(cells, axis=-1, keepdims=True)
        centred = cells - average
        rstd = lax.rsqrt(jnp.mean(centred * centred, axis=-1, keepdims=True) + 1e-05)
        rstd_s[at, :] = rstd
        n_w = centred * rstd
        n_s[at, :] = n_w
        here = n_w.astype(BF16)
        normed[at, :] = here
        kv[at, :] = nn(here, wqkv_ref[:, c:]).astype(BF16)
        qkv_t = nt(wt[...], here).astype(BF16)
        q_all = nn(qkv_t[:c], pick)
        k_ts[w] = qkv_t[c:2 * c]
        for g in range(groups):
            q_wide = (q_all[g_of(g)] * mine).astype(BF16)
            q_ws[w, g] = q_wide
            s = nn(kv[at, g_of(g)], q_wide) * scale + bt[g]
            top = jnp.max(s, axis=0, keepdims=True)
            e = jnp.exp(s - top)
            soft = e * (1.0 / jnp.sum(e, axis=0, keepdims=True))
            soft_s[w, g] = soft
            m_ts[g_of(g), :] = (nn(qkv_t[g_of(g, 2)], soft.astype(BF16)) * mine).astype(BF16)
        mix[at, :] = nt(pick, m_ts[...]).astype(BF16)

    def widen(w):
        dm_t = nt(wout_ref[...], dy_w[at_of(w), :]).astype(BF16)
        dm_all = nn(dm_t, pick)
        for g in range(groups):
            dm_ws[w, g] = (dm_all[g_of(g)] * mine).astype(BF16)

    def backward(g, w):
        at = at_of(w)
        soft = soft_s[w, g]
        dm_wide = dm_ws[w, g]
        da = nn(kv[at, g_of(g, 1)], dm_wide)
        ds = soft * (da - jnp.sum(soft * da, axis=0, keepdims=True))
        if w == 0:
            db[g] = ds
        else:
            db[g] += ds
        ds = ds.astype(BF16)
        dq_ts[w * gw:(w + 1) * gw, :] = (nn(k_ts[w, g_of(g), :], ds) * (mine * scale)).astype(BF16)
        dproj[at, g_of(g, 1)] = (nt(ds, q_ws[w, g]) * scale).astype(BF16)
        dproj[at, g_of(g, 2)] = nt(soft.astype(BF16), dm_wide).astype(BF16)

    def tile_at(t):
        i = 0
        while t >= CHUNKS[i]:
            t -= CHUNKS[i]
            i += 1
        half_tiles = CHUNKS[i] // 2
        share = half_tiles // nxy
        return i, (t // half_tiles, t % half_tiles // share, t % share)

    def put(t, value):
        i, at = tile_at(t)
        chunk_refs[i][0][at] = value.astype(BF16)

    def out_grads():
        normed_t[...] = nt(eye, normed[...]).astype(BF16)
        grad = nn(nt(eye, mix[...]).astype(BF16), dy_w[...]) * grad_scale
        for k in range(3):
            for r in range(24):
                put(k * 24 + r, grad[r * 16:(r + 1) * 16, k * 128:(k + 1) * 128])

    def qkv_grads(g):
        dq = nt(pick, dq_ts[...]).astype(BF16)
        for w in range(WINDOWS):
            dproj[at_of(w), g_of(g)] = dq[:, w * gw:(w + 1) * gw]
        for part in range(3):
            grad = nn(normed_t[...], dproj[:, g_of(g, part)]) * grad_scale
            for r in range(24):
                put(72 + 72 * g + part * 24 + r, grad[r * 16:(r + 1) * 16])

    class Chain:
        def __init__(self, refs):
            (self.gb, self.crecv, self.xs, self.xrecv, self.zbuf, self.fin, self.sem) = refs

        def send(self, stage, src, dst, device):
            remote(src, dst, self.sem.at[0, stage], self.sem.at[1, stage], device).start()

        def wait(self, side, stage, like):
            pltpu.make_async_copy(like, like, self.sem.at[side, stage]).wait()

        def start(self):
            self.send(0, self.gb.at[other], self.crecv, sibling)

        def first(self):
            self.wait(1, 0, self.crecv)
            self.xs[...] = (self.gb[core].astype(F32) + self.crecv[...].astype(F32)).astype(BF16)
            for o, (q, d) in enumerate(plane):
                self.send(1, self.xs.at[q], self.xrecv.at[o], d)

        def second(self):
            self.wait(1, 1, self.xrecv)
            total = self.xs[p].astype(F32)
            for o in range(nxy - 1):
                total += self.xrecv[o].astype(F32)
            self.zbuf[0] = total.astype(BF16)
            for o, (d, _) in enumerate(zs):
                self.send(2, self.zbuf.at[0], self.zbuf.at[o + 1], d)

        def third(self):
            if nz > 1:
                self.wait(1, 2, self.zbuf.at[pl.ds(1, nz - 1)])
            total = self.zbuf[z].astype(F32)
            for k in range(1, nz):
                total += self.zbuf[(z + nz - k) % nz].astype(F32)
            mine_at = self.fin.at[core, p]
            mine_at[...] = total.astype(BF16)
            for _, d in plane:
                self.send(3, mine_at, mine_at, d)

        def fourth(self):
            self.wait(1, 3, self.xrecv)
            self.send(4, self.fin.at[core], self.fin.at[core], sibling)

        def last(self):
            self.wait(1, 4, self.fin.at[other])

        def drain(self):
            self.wait(0, 0, self.crecv)
            self.wait(0, 1, self.xrecv)
            if nz > 1:
                self.wait(0, 2, self.zbuf.at[pl.ds(1, nz - 1)])
            self.wait(0, 3, self.xrecv)
            self.wait(0, 4, self.crecv)

    chains = [Chain(r) for r in chunk_refs]

    def unpack(first, end):
        for t in range(first, end):
            i, at = tile_at(t)
            value = chains[i].fin[at].astype(F32)
            r, k = t % 24, t // 24
            rows = slice(r * 16, (r + 1) * 16)
            if k < 3:
                gout_ref[rows, k * 128:(k + 1) * 128] = value
            else:
                g, part = (k - 3) // 3, (k - 3) % 3
                gqkv_ref[rows, g_of(g, part)] = value

    bshare = BIAS_TILES // lon_size

    def bias_wait(side, stage):
        pltpu.make_async_copy(brecv, brecv, b_sem.at[side, stage]).wait()

    def bias_core():
        rows = jnp.concatenate(
            [
                jnp.concatenate(
                    [
                        db[g, z2 * half:(z2 + 1) * half, j * blk:(j + 1) * blk]
                        for z2 in range(LEV)
                        for g in range(groups)
                    ]
                    + [jnp.zeros((half, 96), F32)],
                    axis=1,
                )
                for j in range(WW)
            ],
            axis=0,
        ).astype(BF16)
        dr = nn(gather_ref[...], rows).astype(BF16)
        for t in range(BIAS_TILES):
            k, r = t // 9, t % 9
            tile = dr[r * 16:(r + 1) * 16, k * 128:(k + 1) * 128] if k < 3 else jnp.zeros((16, 128), BF16)
            bb[bias_at(t)] = tile
        for o, (q, d) in enumerate(line):
            remote(bb.at[q], brecv.at[o], b_sem.at[0, 0], b_sem.at[1, 0], d).start()

    def bias_at(t):
        return t // bshare, t % bshare

    def bias_back():
        bias_wait(1, 0)
        total = bb[lon].astype(F32)
        for o in range(lon_size - 1):
            total += brecv[o].astype(F32)
        mine_at = bfin.at[lon]
        mine_at[...] = total.astype(BF16)
        for _, d in line:
            remote(mine_at, mine_at, b_sem.at[0, 1], b_sem.at[1, 1], d).start()

    def bias_end():
        bias_wait(1, 1)
        turned[144:, :] = jnp.zeros((256 - 144, 384), F32)
        for t in range(27):
            k, r = t // 9, t % 9
            turned[r * 16:(r + 1) * 16, k * 128:(k + 1) * 128] = bfin[bias_at(t)].astype(F32)
        flat = turned[...].T
        for z2 in range(LEV):
            for z1 in range(LEV):
                for i1 in range(WH):
                    for g in range(groups):
                        at = z2 * groups * blk + g * blk + (z1 * WH + i1) * GROUP
                        tab[g * GROUP:(g + 1) * GROUP, segment(z1, z2, i1)] = flat[at:at + GROUP, :width]
        dr_ref[:, 0, :] = tab[...]

    def pack_out(f):
        for w, (first, size) in enumerate(RIM_OF):
            rim_osnd[f, first:first + size] = nn(rimt_ref[first:first + size], ow[f, at_of(w)]).astype(BF16)

    def finish(f, ref):
        for copy in rims_out[f]:
            copy.wait()
        upper = nn(sendt_ref[...], rim_out[f]).astype(BF16)
        lower = (nn(ownt_ref[...], ow[f]) + nn(side_ref[...], rim_out[f, 208:256])).astype(BF16)
        for s in range(WH):
            full, r = (upper, s) if s < WH // 2 else (lower, s - WH // 2)
            ref[s] = full[r * PITCH:r * PITCH + COLS * LEV].reshape(COLS, LEV, c)

    stores = []

    def store(src, dst):
        stores.append(pltpu.make_async_copy(src, dst, out_sem.at[len(stores)]))
        stores[-1].start()

    def store_columns(first, end):
        for k in range(first, end):
            at = (slice(None), g_of(k // 3, k % 3))
            store(gqkv_ref.at[at], outs_h[2].at[at])

    c0, c1, c2 = chains
    for w in range(WINDOWS):
        forward(w)
    ow[0] = (x_w[...].astype(F32) + nn(mix[...], wout_ref[...])).astype(BF16)
    pack_out(0)
    for copy in rims_out[0]:
        copy.start()
    for w in range(WINDOWS):
        arrive(1, w, dy_w)
    out_grads()
    for w in range(WINDOWS):
        widen(w)
    for w in range(WINDOWS):
        backward(0, w)
    qkv_grads(0)
    c0.start()
    backward(1, 0)
    backward(1, 1)
    c0.first()
    backward(1, 2)
    qkv_grads(1)
    c1.start()
    backward(2, 0)
    backward(2, 1)
    c1.first()
    backward(2, 2)
    qkv_grads(2)
    c2.start()
    c0.second()
    dn = nt(dproj[...], wqkv_ref[...])
    n_w = n_s[...]
    dx = dn - jnp.mean(dn, axis=-1, keepdims=True) - n_w * jnp.mean(dn * n_w, axis=-1, keepdims=True)
    ow[1] = (dx * rstd_s[...] + dy_w[...].astype(F32)).astype(BF16)
    c2.first()
    pack_out(1)
    c1.second()
    bias_core()
    c0.third()
    c2.second()
    for copy in rims_out[1]:
        copy.start()
    finish(0, out_ref)
    store(out_ref, outs_h[0])
    c1.third()
    c0.fourth()
    bias_back()
    c2.third()
    c0.last()
    unpack(0, 96)
    store(gout_ref, outs_h[3])
    c1.fourth()
    bias_end()
    store(dr_ref, outs_h[4])
    finish(1, dx_ref)
    store(dx_ref, outs_h[1])
    c1.last()
    unpack(96, 192)
    store_columns(0, 5)
    c2.fourth()
    c2.last()
    unpack(192, 288)
    store_columns(5, 9)
    for copy in stores:
        copy.wait()
    for chain in chains:
        chain.drain()
    bias_wait(0, 0)
    bias_wait(0, 1)


def fused(cells, cot, qkv_weight, out_weight, table, lon_size, lat_size, cells_total):
    c = out_weight.shape[0]
    heads, _, entries = table.shape
    groups = heads // GROUP
    consts = constants()
    ins = (cells, cot, qkv_weight, out_weight, table) + consts
    n, nz = lon_size // 4, lat_size // X_HI
    bshare = BIAS_TILES // lon_size
    gw = GROUP * HEAD
    vm = pltpu.VMEM
    dma = pltpu.SemaphoreType.DMA
    out_shape = (
        jax.ShapeDtypeStruct(cells.shape, BF16),
        jax.ShapeDtypeStruct(cells.shape, BF16),
        jax.ShapeDtypeStruct((c, 3 * c), F32),
        jax.ShapeDtypeStruct((c, c), F32),
        jax.ShapeDtypeStruct(table.shape, F32),
    )
    scratch = [vm(a.shape, a.dtype) for a in ins] + [
        dma((len(ins),)),
        vm((2, WH * PITCH, c), BF16),
        vm((2, RIM, c), BF16),
        vm((2, RIM, c), BF16),
        vm((groups, TOK, LANES), F32),
        vm((groups, TOK, LANES), F32),
        vm((ROWS, c), BF16),
        vm((ROWS, c), BF16),
        vm((ROWS, c), BF16),
        vm((c, ROWS), BF16),
        vm((ROWS, c), BF16),
        vm((ROWS, 3 * c), BF16),
        vm((3 * c, c), BF16),
        vm((2, ROWS, c), BF16),
        vm((2, RIM, c), BF16),
        vm((2, RIM, c), BF16),
        vm((ROWS, 2 * c), BF16),
        vm((WINDOWS, c, TOK), BF16),
        vm((WINDOWS, groups, gw, LANES), BF16),
        vm((WINDOWS, groups, TOK, LANES), F32),
        vm((c, LANES), BF16),
        vm((WINDOWS, groups, gw, LANES), BF16),
        vm((WINDOWS * gw, LANES), BF16),
        vm((heads, entries), F32),
        vm((heads * SLABS, WH * SPAN), F32),
        vm((256, 384), F32),
        vm((ROWS, c), F32),
        vm((ROWS, 1), F32),
        dma((2, 14)),
    ]
    tile = (16, 128)
    for tiles in CHUNKS:
        share = tiles // (2 * n * n)
        scratch += [
            vm((2, n * n, share) + tile, BF16),
            vm((n * n, share) + tile, BF16),
            vm((n * n, share) + tile, BF16),
            vm((n * n - 1, share) + tile, BF16),
            vm((nz, share) + tile, BF16),
            vm((2, n * n, share) + tile, BF16),
            dma((2, 5)),
        ]
    scratch += [
        vm((lon_size, bshare) + tile, BF16),
        vm((lon_size - 1, bshare) + tile, BF16),
        vm((lon_size, bshare) + tile, BF16),
        dma((2, 2)),
    ]
    scratch += [vm(a.shape, a.dtype) for a in out_shape] + [dma((13,))]
    kernel = functools.partial(
        body, lon_size, lat_size, groups, (c // heads) ** -0.5, cells_total ** -0.5
    )
    results = pl.pallas_call(
        kernel,
        out_shape=out_shape,
        in_specs=[pl.BlockSpec(memory_space=pl.ANY)] * len(ins),
        out_specs=(pl.BlockSpec(memory_space=pl.ANY),) * len(out_shape),
        scratch_shapes=scratch,
        compiler_params=pltpu.CompilerParams(
            vmem_limit_bytes=60 * 1024 * 1024, collective_id=0, has_side_effects=True
        ),
        cost_estimate=pl.CostEstimate(flops=6_000_000_000, bytes_accessed=10_000_000, transcendentals=800_000),
    )(*ins)
    return handed_out(results)


def handed_out(arrays):
    cuts = [(i, k) for i, a in enumerate(arrays) for k in range(6 if i == 2 else 2 if i == 3 else 1)]

    def move(*refs):
        ins, outs, (sem, *held) = refs[:len(arrays)], refs[len(arrays):2 * len(arrays)], refs[2 * len(arrays):]
        into, out_of = [], []
        for j, (i, k) in enumerate(cuts):
            parts = sum(1 for at, _ in cuts if at == i)
            rows = arrays[i].shape[0] // parts
            at = pl.ds(k * rows, rows)
            into.append(pltpu.make_async_copy(ins[i].at[at], held[i].at[at], sem.at[0, j]))
            out_of.append(pltpu.make_async_copy(held[i].at[at], outs[i].at[at], sem.at[1, j]))
        for copy in into:
            copy.start()
        for first, second in zip(into, out_of):
            first.wait()
            second.start()
        for copy in out_of:
            copy.wait()

    return pl.pallas_call(
        move,
        out_shape=tuple(jax.ShapeDtypeStruct(a.shape, a.dtype) for a in arrays),
        in_specs=[pl.BlockSpec(memory_space=pl.ANY)] * len(arrays),
        out_specs=(pl.BlockSpec(memory_space=pl.ANY),) * len(arrays),
        scratch_shapes=[pltpu.SemaphoreType.DMA((2, len(cuts)))] + [pltpu.VMEM(a.shape, a.dtype) for a in arrays],
        compiler_params=pltpu.CompilerParams(vmem_limit_bytes=60 * 1024 * 1024),
    )(*arrays)


def on_device(cells, qkv_weight, out_weight, earth_bias, cotangent):
    lon_size, lat_size = lax.axis_size("lon"), lax.axis_size("lat")
    heads = earth_bias.shape[1]
    cells_total = LEV * cells.shape[1] * cells.shape[2] * lon_size * lat_size
    out, dx, gqkv, gout, dr = fused(
        cells.transpose(1, 2, 0, 3), cotangent.transpose(1, 2, 0, 3), qkv_weight, out_weight, earth_bias.transpose(1, 0, 2),
        lon_size, lat_size, cells_total
    )
    out, dx = out.transpose(2, 0, 1, 3), dx.transpose(2, 0, 1, 3)
    return out, dx, gqkv, gout, dr.transpose(1, 0, 2)


def solution(mesh):
    grid = P(None, "lat", "lon", None)
    return jax.shard_map(
        on_device,
        mesh=mesh,
        in_specs=(grid, P(), P(), P("lat", None, None), grid),
        out_specs=(grid, grid, P(), P(), P("lat", None, None)),
        check_vma=False,
    )
```

```python
import functools

import numpy as np
import jax
import jax.numpy as jnp
from jax import lax
from jax.experimental import pallas as pl
from jax.experimental.pallas import tpu as pltpu
from jax.sharding import PartitionSpec as P

LEV = 2
WH = 6
WW = 12
TOK = LEV * WH * WW
SLABS = LEV * WH
SPAN = 2 * WW - 1
GROUP = 4
HEAD = 32
LANES = GROUP * TOK
WINDOWS = 3
ROWS = WINDOWS * TOK
COLS = WINDOWS * WW
PITCH = 80
FINE_RIMS = ((0, 80, 0), (80, 80, 0), (160, 48, 0), (208, 48, 1), (256, 48, 2))
RIMS = ((0, 208, 0), (208, 48, 1), (256, 48, 2))
RIM_OF = ((0, 80), (80, 80), (160, 144))
RIM = 304
BIAS_TILES = 32
CHUNKS = (128, 96, 64)
X_HI = 2
F32 = jnp.float32
BF16 = jnp.bfloat16
MESH = pl.DeviceIdType.MESH


def nn(a, b):
    return lax.dot_general(a, b, (((1,), (0,)), ((), ())), preferred_element_type=F32)


def nt(a, b):
    return lax.dot_general(a, b, (((1,), (1,)), ((), ())), preferred_element_type=F32)


def constants():
    j1, i2, j2 = np.meshgrid(np.arange(WW), np.arange(WH), np.arange(WW), indexing="ij")
    spot = (i2 * SPAN + j1 - j2 + WW - 1).reshape(-1)
    spread = (spot[:, None] == np.arange(WH * SPAN)[None, :]).astype(np.float32)
    gather = np.zeros((144, spread.shape[0]), np.float32)
    gather[: WH * SPAN] = spread.T
    lane = np.arange(LANES)
    lane_col, lane_slab = lane // (SLABS * GROUP), lane // GROUP % SLABS
    token_of_lane = lane_slab * WW + lane_col
    pick = (np.arange(TOK)[:, None] == token_of_lane[None, :]).astype(np.float32)
    row_half = np.arange(TOK) // WW % WH >= WH - WH // 2
    lane_half = lane_slab % WH >= WH - WH // 2
    cross = np.where(row_half[:, None] != lane_half[None, :], -1e9, 0.0).astype(np.float32)
    own = np.zeros((ROWS, WH * PITCH), np.float32)
    rim = np.zeros((ROWS, RIM), np.float32)
    send = np.zeros((RIM, WH * PITCH), np.float32)
    h = WH // 2
    for w in range(WINDOWS):
        for z in range(LEV):
            for i in range(WH):
                for j in range(WW):
                    t = w * TOK + (z * WH + i) * WW + j
                    col = WW // 2 + w * WW + j
                    below, beside = i >= h, col >= COLS
                    row, k = ((i - h) if below else (i + h)), i % h
                    slab = row * PITCH + col % COLS * LEV + z
                    if not below and not beside:
                        own[t, slab] = 1
                        continue
                    if beside:
                        at = (256 if below else 208) + z * 18 + k * 6 + j - 6
                    elif w == WINDOWS - 1:
                        at = 160 + z * 18 + k * 6 + j
                    else:
                        at = 80 * w + z * 36 + k * 12 + j
                    rim[t, at] = 1
                    send[at, slab] = 1
    low = WH // 2 * PITCH
    rim_w = np.zeros((ROWS, 144), np.float32)
    rim_wt = np.zeros((RIM, TOK), np.float32)
    for w, (at, size) in enumerate(RIM_OF):
        block = rim[w * TOK:(w + 1) * TOK, at:at + size]
        rim_w[w * TOK:(w + 1) * TOK, :size] = block
        rim_wt[at:at + size] = block.T
    send_w = np.concatenate([send[:208, :low], send[208:256, low:], send[256:, :low]], axis=0)
    bf = lambda a: jnp.asarray(np.ascontiguousarray(a), BF16)
    return (
        bf(spread), bf(gather), bf(pick), jnp.asarray(cross, F32),
        bf(own[:, low:]), bf(rim_w), bf(send_w), bf(own[:, low:].T), bf(rim_wt), bf(send[:, :low].T),
        bf(send[208:256, low:].T),
    )


N_IN = 16


def body(lon_size, lat_size, groups, scale, grad_scale, *refs):
    (cells_h, cot_h, wqkv_h, wout_h, r_h) = refs[:5]
    consts_h = refs[5:N_IN]
    outs_h = refs[N_IN:N_IN + 5]
    (cells_v, cot_v, wqkv_ref, wout_ref, r_ref,
     spread_ref, gather_ref, pick_ref, cross_ref, own_ref, rim_ref, send_ref, ownt_ref, rimt_ref, sendt_ref,
     side_ref,
     load_sem, slab, rim_snd, rim_in, bt, db, x_w, dy_w, normed, normed_t, mix, dproj, wt, ow, rim_osnd, rim_out,
     kv, k_ts, q_ws, soft_s, m_ts, dm_ws, dq_ts, tab, rows_of, turned, n_s, rstd_s,
     halo_sem, *comm) = refs[N_IN + 5:]
    (out_ref, dx_ref, gqkv_ref, gout_ref, dr_ref, out_sem) = comm[-6:]
    chunk_refs = [comm[i * 7:i * 7 + 7] for i in range(len(CHUNKS))]
    (bb, brecv, bfin, b_sem) = comm[len(CHUNKS) * 7:-6]
    c = wout_ref.shape[0]
    n, nz = lon_size // 4, lat_size // X_HI
    half = WH * WW
    blk = SLABS * GROUP
    gw = GROUP * HEAD

    lon, lat = lax.axis_index("lon"), lax.axis_index("lat")
    core, x_lo, y = lon % 2, lon // 2 % 2, lon // 4
    x_hi, z = lat // nz, lat % nz
    x = x_hi * 2 + x_lo
    other = 1 - core
    nxy = n * n
    p = y * n + x

    def dev(lon_at, lat_at):
        return {"lon": lon_at, "lat": lat_at}

    def chip(x_at, y_at):
        return dev((y_at * 2 + x_at % 2) * 2 + core, x_at // 2 * nz + z)

    sibling = dev(lon + 1 - 2 * core, lat)
    plane, zs, line = [], [], []
    for o in range(1, nxy):
        q = (p + o) % nxy
        plane.append((q, chip(q % n, q // n)))
    for o in range(1, lon_size):
        q = (lon + o) % lon_size
        line.append((q, dev(q, lat)))
    for o in range(1, nz):
        zs.append((dev(lon, x_hi * nz + (z + o) % nz), (z + nz - o) % nz))

    lon_prev, lon_next = (lon + lon_size - 1) % lon_size, (lon + 1) % lon_size
    lat_prev, lat_next = (lat + lat_size - 1) % lat_size, (lat + 1) % lat_size
    back = (dev(lon, lat_prev), dev(lon_prev, lat), dev(lon_prev, lat_prev))
    ahead = (dev(lon, lat_next), dev(lon_next, lat), dev(lon_next, lat_next))

    def remote(src, dst, send_sem, recv_sem, device):
        return pltpu.make_async_remote_copy(
            src_ref=src, dst_ref=dst, send_sem=send_sem, recv_sem=recv_sem, device_id=device, device_id_type=MESH
        )

    order = (
        (cells_h, cells_v), (consts_h[6], send_ref), (cot_h, cot_v), (r_h, r_ref), (consts_h[0], spread_ref),
        (consts_h[3], cross_ref), (wqkv_h, wqkv_ref), (consts_h[4], own_ref), (consts_h[5], rim_ref),
        (consts_h[2], pick_ref), (wout_h, wout_ref), (consts_h[8], rimt_ref), (consts_h[7], ownt_ref),
        (consts_h[9], sendt_ref), (consts_h[10], side_ref), (consts_h[1], gather_ref),
    )
    loads = [pltpu.make_async_copy(s, d, load_sem.at[i]) for i, (s, d) in enumerate(order)]
    for load in loads:
        load.start()

    barrier = pltpu.get_barrier_semaphore()

    def greet(device):
        pl.semaphore_signal(barrier, inc=1, device_id=device, device_id_type=MESH)

    partners = back + ahead
    partners += tuple(d for _, d in plane + line) + tuple(d for d, _ in zs)
    for device in partners:
        greet(device)

    def rim_copies(f, snd, rcv, devices, base, parts):
        return [
            remote(
                snd.at[f, pl.ds(at, size)], rcv.at[f, pl.ds(at, size)],
                halo_sem.at[0, base + k], halo_sem.at[1, base + k], devices[to],
            )
            for k, (at, size, to) in enumerate(parts)
        ]

    rims_in = (
        rim_copies(0, rim_snd, rim_in, back, 0, FINE_RIMS),
        rim_copies(1, rim_snd, rim_in, back, 5, RIMS),
    )
    rims_out = (
        rim_copies(0, rim_osnd, rim_out, ahead, 8, RIMS),
        rim_copies(1, rim_osnd, rim_out, ahead, 11, RIMS),
    )
    low = WH // 2 * PITCH
    for f, src in enumerate((cells_v, cot_v)):
        loads[2 * f].wait()
        for s in range(WH):
            slab[f, s * PITCH:(s + 1) * PITCH, :] = jnp.concatenate(
                [src[s].reshape(COLS * LEV, c), jnp.zeros((PITCH - COLS * LEV, c), BF16)], axis=0
            )
        if f == 0:
            loads[1].wait()
        rim_snd[f, :208] = nn(send_ref[:208], slab[f, :low]).astype(BF16)
        rim_snd[f, 208:256] = nn(send_ref[208:256], slab[f, low:]).astype(BF16)
        rim_snd[f, 256:] = nn(send_ref[256:], slab[f, :low]).astype(BF16)
        if f == 0:
            pl.semaphore_wait(barrier, len(partners))
        for copy in rims_in[f]:
            copy.start()

    for load in loads[3:6]:
        load.wait()
    last = (lat == lat_size - 1).astype(F32)
    tab[...] = r_ref[:, 0, :]
    width = WH * SPAN

    def segment(z1, z2, i1):
        return pl.ds(((z1 * LEV + z2) * WH + i1) * width, width)

    for z2 in range(LEV):
        for z1 in range(LEV):
            for i1 in range(WH):
                piece = tab[:, segment(z1, z2, i1)]
                for g in range(groups):
                    at = g * blk + (z1 * WH + i1) * GROUP
                    rows_of[at:at + GROUP, :] = piece[g * GROUP:(g + 1) * GROUP]
        table = rows_of[...]
        hi = table.astype(BF16)
        rest = table - hi.astype(F32)
        mid = rest.astype(BF16)
        lo = (rest - mid.astype(F32)).astype(BF16)
        spread = spread_ref[...]
        u = nt(spread, hi) + nt(spread, mid) + nt(spread, lo)
        for g in range(groups):
            rows = jnp.concatenate(
                [u[j * half:(j + 1) * half, g * blk:(g + 1) * blk] for j in range(WW)], axis=1
            )
            keep = pl.ds(z2 * half, half)
            bt[g, keep, :] = rows + cross_ref[keep, :] * last
    row = lax.broadcasted_iota(jnp.int32, (c, c), 0)
    col = lax.broadcasted_iota(jnp.int32, (c, c), 1)
    eye = (row == col).astype(F32).astype(BF16)
    head_row = lax.broadcasted_iota(jnp.int32, (gw, LANES), 0) // HEAD
    head_lane = lax.broadcasted_iota(jnp.int32, (gw, LANES), 1) % GROUP
    mine = (head_row == head_lane).astype(F32)
    for load in loads[6:]:
        load.wait()
    for part in range(3):
        wt[part * c:(part + 1) * c, :] = nt(eye, wqkv_ref[:, part * c:(part + 1) * c]).astype(BF16)
    pick = pick_ref[...]

    def arrive(f, w, ref):
        if f == 0:
            parts = rims_in[0][w:w + 1] if w < WINDOWS - 1 else rims_in[0][w:]
        else:
            parts = rims_in[1][:1] if w == 0 else rims_in[1][1:] if w == WINDOWS - 1 else []
        for copy in parts:
            copy.wait()
        at, (first, size) = slice(w * TOK, (w + 1) * TOK), RIM_OF[w]
        ref[at, :] = (
            nn(own_ref[at, :], slab[f, low:]) + nn(rim_ref[at, :size], rim_in[f, first:first + size])
        ).astype(BF16)

    def at_of(w):
        return slice(w * TOK, (w + 1) * TOK)

    def g_of(g, part=0):
        return slice(part * c + g * gw, part * c + (g + 1) * gw)

    def forward(w):
        at = at_of(w)
        arrive(0, w, x_w)
        cells = x_w[at, :].astype(F32)
        average = jnp.mean(cells, axis=-1, keepdims=True)
        centred = cells - average
        rstd = lax.rsqrt(jnp.mean(centred * centred, axis=-1, keepdims=True) + 1e-05)
        rstd_s[at, :] = rstd
        n_w = centred * rstd
        n_s[at, :] = n_w
        here = n_w.astype(BF16)
        normed[at, :] = here
        kv[at, :] = nn(here, wqkv_ref[:, c:]).astype(BF16)
        qkv_t = nt(wt[...], here).astype(BF16)
        q_all = nn(qkv_t[:c], pick)
        k_ts[w] = qkv_t[c:2 * c]
        for g in range(groups):
            q_wide = (q_all[g_of(g)] * mine).astype(BF16)
            q_ws[w, g] = q_wide
            s = nn(kv[at, g_of(g)], q_wide) * scale + bt[g]
            top = jnp.max(s, axis=0, keepdims=True)
            e = jnp.exp(s - top)
            soft = e * (1.0 / jnp.sum(e, axis=0, keepdims=True))
            soft_s[w, g] = soft
            m_ts[g_of(g), :] = (nn(qkv_t[g_of(g, 2)], soft.astype(BF16)) * mine).astype(BF16)
        mix[at, :] = nt(pick, m_ts[...]).astype(BF16)

    def widen(w):
        dm_t = nt(wout_ref[...], dy_w[at_of(w), :]).astype(BF16)
        dm_all = nn(dm_t, pick)
        for g in range(groups):
            dm_ws[w, g] = (dm_all[g_of(g)] * mine).astype(BF16)

    def backward(g, w):
        at = at_of(w)
        soft = soft_s[w, g]
        dm_wide = dm_ws[w, g]
        da = nn(kv[at, g_of(g, 1)], dm_wide)
        ds = soft * (da - jnp.sum(soft * da, axis=0, keepdims=True))
        if w == 0:
            db[g] = ds
        else:
            db[g] += ds
        ds = ds.astype(BF16)
        dq_ts[w * gw:(w + 1) * gw, :] = (nn(k_ts[w, g_of(g), :], ds) * (mine * scale)).astype(BF16)
        dproj[at, g_of(g, 1)] = (nt(ds, q_ws[w, g]) * scale).astype(BF16)

    def values(g, w):
        dproj[at_of(w), g_of(g, 2)] = nt(soft_s[w, g].astype(BF16), dm_ws[w, g]).astype(BF16)

    def tile_at(t):
        i = 0
        while t >= CHUNKS[i]:
            t -= CHUNKS[i]
            i += 1
        half_tiles = CHUNKS[i] // 2
        share = half_tiles // nxy
        return i, (t // half_tiles, t % half_tiles // share, t % share)

    def put(t, value):
        i, at = tile_at(t)
        chunk_refs[i][0][at] = value.astype(BF16)

    def out_grads():
        normed_t[...] = nt(eye, normed[...]).astype(BF16)
        grad = nn(nt(eye, mix[...]).astype(BF16), dy_w[...]) * grad_scale
        for k in range(3):
            for r in range(24):
                put(k * 24 + r, grad[r * 16:(r + 1) * 16, k * 128:(k + 1) * 128])

    def column_grad(k, g, part):
        grad = nn(normed_t[...], dproj[:, g_of(g, part)]) * grad_scale
        for r in range(24):
            put(24 * k + r, grad[r * 16:(r + 1) * 16])

    def qk_grads(g):
        dq = nt(pick, dq_ts[...]).astype(BF16)
        for w in range(WINDOWS):
            dproj[at_of(w), g_of(g)] = dq[:, w * gw:(w + 1) * gw]
        for part in range(2):
            column_grad(6 + 2 * g + part, g, part)

    def columns_of(k):
        return g_of(k - 3, 2) if k < 6 else g_of((k - 6) // 2, (k - 6) % 2)

    class Chain:
        def __init__(self, refs):
            (self.gb, self.crecv, self.xs, self.xrecv, self.zbuf, self.fin, self.sem) = refs

        def send(self, stage, src, dst, device):
            remote(src, dst, self.sem.at[0, stage], self.sem.at[1, stage], device).start()

        def wait(self, side, stage, like):
            pltpu.make_async_copy(like, like, self.sem.at[side, stage]).wait()

        def start(self):
            self.send(0, self.gb.at[other], self.crecv, sibling)

        def first(self):
            self.wait(1, 0, self.crecv)
            self.xs[...] = (self.gb[core].astype(F32) + self.crecv[...].astype(F32)).astype(BF16)
            for o, (q, d) in enumerate(plane):
                self.send(1, self.xs.at[q], self.xrecv.at[o], d)

        def second(self):
            self.wait(1, 1, self.xrecv)
            total = self.xs[p].astype(F32)
            for o in range(nxy - 1):
                total += self.xrecv[o].astype(F32)
            self.zbuf[0] = total.astype(BF16)
            for o, (d, _) in enumerate(zs):
                self.send(2, self.zbuf.at[0], self.zbuf.at[o + 1], d)

        def third(self):
            if nz > 1:
                self.wait(1, 2, self.zbuf.at[pl.ds(1, nz - 1)])
            total = self.zbuf[z].astype(F32)
            for k in range(1, nz):
                total += self.zbuf[(z + nz - k) % nz].astype(F32)
            mine_at = self.fin.at[core, p]
            mine_at[...] = total.astype(BF16)
            for _, d in plane:
                self.send(3, mine_at, mine_at, d)

        def fourth(self):
            self.wait(1, 3, self.xrecv)
            self.send(4, self.fin.at[core], self.fin.at[core], sibling)

        def last(self):
            self.wait(1, 4, self.fin.at[other])

        def drain(self):
            self.wait(0, 0, self.crecv)
            self.wait(0, 1, self.xrecv)
            if nz > 1:
                self.wait(0, 2, self.zbuf.at[pl.ds(1, nz - 1)])
            self.wait(0, 3, self.xrecv)
            self.wait(0, 4, self.crecv)

    chains = [Chain(r) for r in chunk_refs]

    def unpack(first, end):
        for t in range(first, end):
            i, at = tile_at(t)
            value = chains[i].fin[at].astype(F32)
            r, k = t % 24, t // 24
            rows = slice(r * 16, (r + 1) * 16)
            if k < 3:
                gout_ref[rows, k * 128:(k + 1) * 128] = value
            else:
                gqkv_ref[rows, columns_of(k)] = value

    bshare = BIAS_TILES // lon_size

    def bias_wait(side, stage):
        pltpu.make_async_copy(brecv, brecv, b_sem.at[side, stage]).wait()

    def bias_core():
        rows = jnp.concatenate(
            [
                jnp.concatenate(
                    [
                        db[g, z2 * half:(z2 + 1) * half, j * blk:(j + 1) * blk]
                        for z2 in range(LEV)
                        for g in range(groups)
                    ]
                    + [jnp.zeros((half, 96), F32)],
                    axis=1,
                )
                for j in range(WW)
            ],
            axis=0,
        ).astype(BF16)
        dr = nn(gather_ref[...], rows).astype(BF16)
        for t in range(BIAS_TILES):
            k, r = t // 9, t % 9
            tile = dr[r * 16:(r + 1) * 16, k * 128:(k + 1) * 128] if k < 3 else jnp.zeros((16, 128), BF16)
            bb[bias_at(t)] = tile
        for o, (q, d) in enumerate(line):
            remote(bb.at[q], brecv.at[o], b_sem.at[0, 0], b_sem.at[1, 0], d).start()

    def bias_at(t):
        return t // bshare, t % bshare

    def bias_back():
        bias_wait(1, 0)
        total = bb[lon].astype(F32)
        for o in range(lon_size - 1):
            total += brecv[o].astype(F32)
        mine_at = bfin.at[lon]
        mine_at[...] = total.astype(BF16)
        for _, d in line:
            remote(mine_at, mine_at, b_sem.at[0, 1], b_sem.at[1, 1], d).start()

    def bias_end():
        bias_wait(1, 1)
        turned[144:, :] = jnp.zeros((256 - 144, 384), F32)
        for t in range(27):
            k, r = t // 9, t % 9
            turned[r * 16:(r + 1) * 16, k * 128:(k + 1) * 128] = bfin[bias_at(t)].astype(F32)
        flat = turned[...].T
        for z2 in range(LEV):
            for z1 in range(LEV):
                for i1 in range(WH):
                    for g in range(groups):
                        at = z2 * groups * blk + g * blk + (z1 * WH + i1) * GROUP
                        tab[g * GROUP:(g + 1) * GROUP, segment(z1, z2, i1)] = flat[at:at + GROUP, :width]
        dr_ref[:, 0, :] = tab[...]

    def pack_out(f):
        for w, (first, size) in enumerate(RIM_OF):
            rim_osnd[f, first:first + size] = nn(rimt_ref[first:first + size], ow[f, at_of(w)]).astype(BF16)

    def finish(f, ref):
        for copy in rims_out[f]:
            copy.wait()
        upper = nn(sendt_ref[...], rim_out[f]).astype(BF16)
        lower = (nn(ownt_ref[...], ow[f]) + nn(side_ref[...], rim_out[f, 208:256])).astype(BF16)
        for s in range(WH):
            full, r = (upper, s) if s < WH // 2 else (lower, s - WH // 2)
            ref[s] = full[r * PITCH:r * PITCH + COLS * LEV].reshape(COLS, LEV, c)

    stores = []

    def store(src, dst):
        stores.append(pltpu.make_async_copy(src, dst, out_sem.at[len(stores)]))
        stores[-1].start()

    def store_columns(first, end):
        for k in range(first, end):
            at = (slice(None), columns_of(k))
            store(gqkv_ref.at[at], outs_h[2].at[at])

    c0, c1, c2 = chains
    for w in range(WINDOWS):
        forward(w)
    ow[0] = (x_w[...].astype(F32) + nn(mix[...], wout_ref[...])).astype(BF16)
    pack_out(0)
    for copy in rims_out[0]:
        copy.start()
    for w in range(WINDOWS):
        arrive(1, w, dy_w)
    out_grads()
    for w in range(WINDOWS):
        widen(w)
    for g in range(groups):
        for w in range(WINDOWS):
            values(g, w)
        column_grad(3 + g, g, 2)
    c0.start()
    for w in range(WINDOWS):
        backward(0, w)
    c0.first()
    qk_grads(0)
    for w in range(WINDOWS):
        backward(1, w)
    qk_grads(1)
    c1.start()
    for w in range(WINDOWS):
        backward(2, w)
    c1.first()
    qk_grads(2)
    c2.start()
    c0.second()
    dn = nt(dproj[...], wqkv_ref[...])
    n_w = n_s[...]
    dx = dn - jnp.mean(dn, axis=-1, keepdims=True) - n_w * jnp.mean(dn * n_w, axis=-1, keepdims=True)
    ow[1] = (dx * rstd_s[...] + dy_w[...].astype(F32)).astype(BF16)
    c2.first()
    pack_out(1)
    c1.second()
    bias_core()
    c0.third()
    c2.second()
    for copy in rims_out[1]:
        copy.start()
    finish(0, out_ref)
    store(out_ref, outs_h[0])
    c1.third()
    c0.fourth()
    bias_back()
    c2.third()
    c0.last()
    unpack(0, 128)
    store(gout_ref, outs_h[3])
    store_columns(3, 5)
    c1.fourth()
    bias_end()
    store(dr_ref, outs_h[4])
    finish(1, dx_ref)
    store(dx_ref, outs_h[1])
    c1.last()
    unpack(128, 224)
    store_columns(5, 9)
    c2.fourth()
    c2.last()
    unpack(224, 288)
    store_columns(9, 12)
    for copy in stores:
        copy.wait()
    for chain in chains:
        chain.drain()
    bias_wait(0, 0)
    bias_wait(0, 1)


def fused(cells, cot, qkv_weight, out_weight, table, lon_size, lat_size, cells_total):
    c = out_weight.shape[0]
    heads, _, entries = table.shape
    groups = heads // GROUP
    consts = constants()
    ins = (cells, cot, qkv_weight, out_weight, table) + consts
    n, nz = lon_size // 4, lat_size // X_HI
    bshare = BIAS_TILES // lon_size
    gw = GROUP * HEAD
    vm = pltpu.VMEM
    dma = pltpu.SemaphoreType.DMA
    out_shape = (
        jax.ShapeDtypeStruct(cells.shape, BF16),
        jax.ShapeDtypeStruct(cells.shape, BF16),
        jax.ShapeDtypeStruct((c, 3 * c), F32),
        jax.ShapeDtypeStruct((c, c), F32),
        jax.ShapeDtypeStruct(table.shape, F32),
    )
    scratch = [vm(a.shape, a.dtype) for a in ins] + [
        dma((len(ins),)),
        vm((2, WH * PITCH, c), BF16),
        vm((2, RIM, c), BF16),
        vm((2, RIM, c), BF16),
        vm((groups, TOK, LANES), F32),
        vm((groups, TOK, LANES), F32),
        vm((ROWS, c), BF16),
        vm((ROWS, c), BF16),
        vm((ROWS, c), BF16),
        vm((c, ROWS), BF16),
        vm((ROWS, c), BF16),
        vm((ROWS, 3 * c), BF16),
        vm((3 * c, c), BF16),
        vm((2, ROWS, c), BF16),
        vm((2, RIM, c), BF16),
        vm((2, RIM, c), BF16),
        vm((ROWS, 2 * c), BF16),
        vm((WINDOWS, c, TOK), BF16),
        vm((WINDOWS, groups, gw, LANES), BF16),
        vm((WINDOWS, groups, TOK, LANES), F32),
        vm((c, LANES), BF16),
        vm((WINDOWS, groups, gw, LANES), BF16),
        vm((WINDOWS * gw, LANES), BF16),
        vm((heads, entries), F32),
        vm((heads * SLABS, WH * SPAN), F32),
        vm((256, 384), F32),
        vm((ROWS, c), F32),
        vm((ROWS, 1), F32),
        dma((2, 14)),
    ]
    tile = (16, 128)
    for tiles in CHUNKS:
        share = tiles // (2 * n * n)
        scratch += [
            vm((2, n * n, share) + tile, BF16),
            vm((n * n, share) + tile, BF16),
            vm((n * n, share) + tile, BF16),
            vm((n * n - 1, share) + tile, BF16),
            vm((nz, share) + tile, BF16),
            vm((2, n * n, share) + tile, BF16),
            dma((2, 5)),
        ]
    scratch += [
        vm((lon_size, bshare) + tile, BF16),
        vm((lon_size - 1, bshare) + tile, BF16),
        vm((lon_size, bshare) + tile, BF16),
        dma((2, 2)),
    ]
    scratch += [vm(a.shape, a.dtype) for a in out_shape] + [dma((13,))]
    kernel = functools.partial(
        body, lon_size, lat_size, groups, (c // heads) ** -0.5, cells_total ** -0.5
    )
    results = pl.pallas_call(
        kernel,
        out_shape=out_shape,
        in_specs=[pl.BlockSpec(memory_space=pl.ANY)] * len(ins),
        out_specs=(pl.BlockSpec(memory_space=pl.ANY),) * len(out_shape),
        scratch_shapes=scratch,
        compiler_params=pltpu.CompilerParams(
            vmem_limit_bytes=60 * 1024 * 1024, collective_id=0, has_side_effects=True
        ),
        cost_estimate=pl.CostEstimate(flops=6_000_000_000, bytes_accessed=10_000_000, transcendentals=800_000),
    )(*ins)
    return handed_out(results)


def handed_out(arrays):
    cuts = [(i, k) for i, a in enumerate(arrays) for k in range(6 if i == 2 else 2 if i == 3 else 1)]

    def move(*refs):
        ins, outs, (sem, *held) = refs[:len(arrays)], refs[len(arrays):2 * len(arrays)], refs[2 * len(arrays):]
        into, out_of = [], []
        for j, (i, k) in enumerate(cuts):
            parts = sum(1 for at, _ in cuts if at == i)
            rows = arrays[i].shape[0] // parts
            at = pl.ds(k * rows, rows)
            into.append(pltpu.make_async_copy(ins[i].at[at], held[i].at[at], sem.at[0, j]))
            out_of.append(pltpu.make_async_copy(held[i].at[at], outs[i].at[at], sem.at[1, j]))
        for copy in into:
            copy.start()
        for first, second in zip(into, out_of):
            first.wait()
            second.start()
        for copy in out_of:
            copy.wait()

    return pl.pallas_call(
        move,
        out_shape=tuple(jax.ShapeDtypeStruct(a.shape, a.dtype) for a in arrays),
        in_specs=[pl.BlockSpec(memory_space=pl.ANY)] * len(arrays),
        out_specs=(pl.BlockSpec(memory_space=pl.ANY),) * len(arrays),
        scratch_shapes=[pltpu.SemaphoreType.DMA((2, len(cuts)))] + [pltpu.VMEM(a.shape, a.dtype) for a in arrays],
        compiler_params=pltpu.CompilerParams(vmem_limit_bytes=60 * 1024 * 1024),
    )(*arrays)


def on_device(cells, qkv_weight, out_weight, earth_bias, cotangent):
    lon_size, lat_size = lax.axis_size("lon"), lax.axis_size("lat")
    heads = earth_bias.shape[1]
    cells_total = LEV * cells.shape[1] * cells.shape[2] * lon_size * lat_size
    out, dx, gqkv, gout, dr = fused(
        cells.transpose(1, 2, 0, 3), cotangent.transpose(1, 2, 0, 3), qkv_weight, out_weight, earth_bias.transpose(1, 0, 2),
        lon_size, lat_size, cells_total
    )
    out, dx = out.transpose(2, 0, 1, 3), dx.transpose(2, 0, 1, 3)
    return out, dx, gqkv, gout, dr.transpose(1, 0, 2)


def solution(mesh):
    grid = P(None, "lat", "lon", None)
    return jax.shard_map(
        on_device,
        mesh=mesh,
        in_specs=(grid, P(), P(), P("lat", None, None), grid),
        out_specs=(grid, grid, P(), P(), P("lat", None, None)),
        check_vma=False,
    )
```

```python
import functools

import numpy as np
import jax
import jax.numpy as jnp
from jax import lax
from jax.experimental import pallas as pl
from jax.experimental.pallas import tpu as pltpu
from jax.sharding import PartitionSpec as P

LEV = 2
WH = 6
WW = 12
TOK = LEV * WH * WW
SLABS = LEV * WH
SPAN = 2 * WW - 1
GROUP = 4
HEAD = 32
LANES = GROUP * TOK
WINDOWS = 3
ROWS = WINDOWS * TOK
COLS = WINDOWS * WW
PITCH = 80
FINE_RIMS = ((0, 80, 0), (80, 80, 0), (160, 48, 0), (208, 48, 1), (256, 48, 2))
RIMS = ((0, 208, 0), (208, 48, 1), (256, 48, 2))
RIM_OF = ((0, 80), (80, 80), (160, 144))
RIM = 304
BIAS_TILES = 32
CHUNKS = (128, 96, 64)
X_HI = 2
F32 = jnp.float32
BF16 = jnp.bfloat16
MESH = pl.DeviceIdType.MESH


def nn(a, b):
    return lax.dot_general(a, b, (((1,), (0,)), ((), ())), preferred_element_type=F32)


def nt(a, b):
    return lax.dot_general(a, b, (((1,), (1,)), ((), ())), preferred_element_type=F32)


def constants():
    j1, i2, j2 = np.meshgrid(np.arange(WW), np.arange(WH), np.arange(WW), indexing="ij")
    spot = (i2 * SPAN + j1 - j2 + WW - 1).reshape(-1)
    spread = (spot[:, None] == np.arange(WH * SPAN)[None, :]).astype(np.float32)
    gather = np.zeros((144, spread.shape[0]), np.float32)
    gather[: WH * SPAN] = spread.T
    lane = np.arange(LANES)
    lane_col, lane_slab = lane // (SLABS * GROUP), lane // GROUP % SLABS
    token_of_lane = lane_slab * WW + lane_col
    pick = (np.arange(TOK)[:, None] == token_of_lane[None, :]).astype(np.float32)
    row_half = np.arange(TOK) // WW % WH >= WH - WH // 2
    lane_half = lane_slab % WH >= WH - WH // 2
    cross = np.where(row_half[:, None] != lane_half[None, :], -1e9, 0.0).astype(np.float32)
    own = np.zeros((ROWS, WH * PITCH), np.float32)
    rim = np.zeros((ROWS, RIM), np.float32)
    send = np.zeros((RIM, WH * PITCH), np.float32)
    h = WH // 2
    for w in range(WINDOWS):
        for z in range(LEV):
            for i in range(WH):
                for j in range(WW):
                    t = w * TOK + (z * WH + i) * WW + j
                    col = WW // 2 + w * WW + j
                    below, beside = i >= h, col >= COLS
                    row, k = ((i - h) if below else (i + h)), i % h
                    slab = row * PITCH + col % COLS * LEV + z
                    if not below and not beside:
                        own[t, slab] = 1
                        continue
                    if beside:
                        at = (256 if below else 208) + z * 18 + k * 6 + j - 6
                    elif w == WINDOWS - 1:
                        at = 160 + z * 18 + k * 6 + j
                    else:
                        at = 80 * w + z * 36 + k * 12 + j
                    rim[t, at] = 1
                    send[at, slab] = 1
    low = WH // 2 * PITCH
    rim_w = np.zeros((ROWS, 144), np.float32)
    rim_wt = np.zeros((RIM, TOK), np.float32)
    for w, (at, size) in enumerate(RIM_OF):
        block = rim[w * TOK:(w + 1) * TOK, at:at + size]
        rim_w[w * TOK:(w + 1) * TOK, :size] = block
        rim_wt[at:at + size] = block.T
    send_w = np.concatenate([send[:208, :low], send[208:256, low:], send[256:, :low]], axis=0)
    bf = lambda a: jnp.asarray(np.ascontiguousarray(a), BF16)
    return (
        bf(spread), bf(gather), bf(pick), jnp.asarray(cross, F32),
        bf(own[:, low:]), bf(rim_w), bf(send_w), bf(own[:, low:].T), bf(rim_wt), bf(send[:, :low].T),
        bf(send[208:256, low:].T),
    )


N_IN = 16


def body(lon_size, lat_size, groups, scale, grad_scale, *refs):
    (cells_h, cot_h, wqkv_h, wout_h, r_h) = refs[:5]
    consts_h = refs[5:N_IN]
    outs_h = refs[N_IN:N_IN + 5]
    (cells_v, cot_v, wqkv_ref, wout_ref, r_ref,
     spread_ref, gather_ref, pick_ref, cross_ref, own_ref, rim_ref, send_ref, ownt_ref, rimt_ref, sendt_ref,
     side_ref,
     load_sem, slab, rim_snd, rim_in, bt, db, x_w, dy_w, normed, normed_t, mix, dproj, wt, ow, rim_osnd, rim_out,
     kv, k_ts, q_ws, soft_s, m_ts, dm_ws, dq_ts, tab, rows_of, turned, n_s, rstd_s,
     halo_sem, *comm) = refs[N_IN + 5:]
    (out_ref, dx_ref, gqkv_ref, gout_ref, dr_ref, out_sem) = comm[-6:]
    many = 7 * (len(CHUNKS) - 1)
    chunk_refs = [comm[i:i + 7] for i in range(0, many, 7)] + [comm[many:many + 5]]
    (bb, brecv, bfin, b_sem) = comm[many + 5:-6]
    c = wout_ref.shape[0]
    n, nz = lon_size // 4, lat_size // X_HI
    half = WH * WW
    blk = SLABS * GROUP
    gw = GROUP * HEAD

    lon, lat = lax.axis_index("lon"), lax.axis_index("lat")
    core, x_lo, y = lon % 2, lon // 2 % 2, lon // 4
    x_hi, z = lat // nz, lat % nz
    x = x_hi * 2 + x_lo
    other = 1 - core
    nxy = n * n
    p = y * n + x

    def dev(lon_at, lat_at):
        return {"lon": lon_at, "lat": lat_at}

    def chip(x_at, y_at):
        return dev((y_at * 2 + x_at % 2) * 2 + core, x_at // 2 * nz + z)

    sibling = dev(lon + 1 - 2 * core, lat)
    plane, zs, line = [], [], []
    for o in range(1, nxy):
        q = (p + o) % nxy
        plane.append((q, chip(q % n, q // n)))
    rank = core * nxy + p
    wide = []
    for o in range(1, 2 * nxy):
        q = (rank + o) % (2 * nxy)
        at = q % nxy
        wide.append((q, dev((at // n * 2 + at % n % 2) * 2 + q // nxy, at % n // 2 * nz + z)))
    for o in range(1, lon_size):
        q = (lon + o) % lon_size
        line.append((q, dev(q, lat)))
    for o in range(1, nz):
        zs.append((dev(lon, x_hi * nz + (z + o) % nz), (z + nz - o) % nz))

    lon_prev, lon_next = (lon + lon_size - 1) % lon_size, (lon + 1) % lon_size
    lat_prev, lat_next = (lat + lat_size - 1) % lat_size, (lat + 1) % lat_size
    back = (dev(lon, lat_prev), dev(lon_prev, lat), dev(lon_prev, lat_prev))
    ahead = (dev(lon, lat_next), dev(lon_next, lat), dev(lon_next, lat_next))

    def remote(src, dst, send_sem, recv_sem, device):
        return pltpu.make_async_remote_copy(
            src_ref=src, dst_ref=dst, send_sem=send_sem, recv_sem=recv_sem, device_id=device, device_id_type=MESH
        )

    order = (
        (cells_h, cells_v), (consts_h[6], send_ref), (cot_h, cot_v), (r_h, r_ref), (consts_h[0], spread_ref),
        (consts_h[3], cross_ref), (wqkv_h, wqkv_ref), (consts_h[4], own_ref), (consts_h[5], rim_ref),
        (consts_h[2], pick_ref), (wout_h, wout_ref), (consts_h[8], rimt_ref), (consts_h[7], ownt_ref),
        (consts_h[9], sendt_ref), (consts_h[10], side_ref), (consts_h[1], gather_ref),
    )
    loads = [pltpu.make_async_copy(s, d, load_sem.at[i]) for i, (s, d) in enumerate(order)]
    for load in loads:
        load.start()

    barrier = pltpu.get_barrier_semaphore()

    def greet(device):
        pl.semaphore_signal(barrier, inc=1, device_id=device, device_id_type=MESH)

    partners = back + ahead
    partners += tuple(d for _, d in wide) + tuple(d for d, _ in zs)
    for device in partners:
        greet(device)

    def rim_copies(f, snd, rcv, devices, base, parts):
        return [
            remote(
                snd.at[f, pl.ds(at, size)], rcv.at[f, pl.ds(at, size)],
                halo_sem.at[0, base + k], halo_sem.at[1, base + k], devices[to],
            )
            for k, (at, size, to) in enumerate(parts)
        ]

    rims_in = (
        rim_copies(0, rim_snd, rim_in, back, 0, FINE_RIMS),
        rim_copies(1, rim_snd, rim_in, back, 5, RIMS),
    )
    rims_out = (
        rim_copies(0, rim_osnd, rim_out, ahead, 8, RIMS),
        rim_copies(1, rim_osnd, rim_out, ahead, 11, RIMS),
    )
    low = WH // 2 * PITCH
    for f, src in enumerate((cells_v, cot_v)):
        loads[2 * f].wait()
        for s in range(WH):
            slab[f, s * PITCH:(s + 1) * PITCH, :] = jnp.concatenate(
                [src[s].reshape(COLS * LEV, c), jnp.zeros((PITCH - COLS * LEV, c), BF16)], axis=0
            )
        if f == 0:
            loads[1].wait()
        rim_snd[f, :208] = nn(send_ref[:208], slab[f, :low]).astype(BF16)
        rim_snd[f, 208:256] = nn(send_ref[208:256], slab[f, low:]).astype(BF16)
        rim_snd[f, 256:] = nn(send_ref[256:], slab[f, :low]).astype(BF16)
        if f == 0:
            pl.semaphore_wait(barrier, len(partners))
        for copy in rims_in[f]:
            copy.start()

    for load in loads[3:6]:
        load.wait()
    last = (lat == lat_size - 1).astype(F32)
    tab[...] = r_ref[:, 0, :]
    width = WH * SPAN

    def segment(z1, z2, i1):
        return pl.ds(((z1 * LEV + z2) * WH + i1) * width, width)

    for z2 in range(LEV):
        for z1 in range(LEV):
            for i1 in range(WH):
                piece = tab[:, segment(z1, z2, i1)]
                for g in range(groups):
                    at = g * blk + (z1 * WH + i1) * GROUP
                    rows_of[at:at + GROUP, :] = piece[g * GROUP:(g + 1) * GROUP]
        table = rows_of[...]
        hi = table.astype(BF16)
        rest = table - hi.astype(F32)
        mid = rest.astype(BF16)
        lo = (rest - mid.astype(F32)).astype(BF16)
        spread = spread_ref[...]
        u = nt(spread, hi) + nt(spread, mid) + nt(spread, lo)
        for g in range(groups):
            rows = jnp.concatenate(
                [u[j * half:(j + 1) * half, g * blk:(g + 1) * blk] for j in range(WW)], axis=1
            )
            keep = pl.ds(z2 * half, half)
            bt[g, keep, :] = rows + cross_ref[keep, :] * last
    row = lax.broadcasted_iota(jnp.int32, (c, c), 0)
    col = lax.broadcasted_iota(jnp.int32, (c, c), 1)
    eye = (row == col).astype(F32).astype(BF16)
    head_row = lax.broadcasted_iota(jnp.int32, (gw, LANES), 0) // HEAD
    head_lane = lax.broadcasted_iota(jnp.int32, (gw, LANES), 1) % GROUP
    mine = (head_row == head_lane).astype(F32)
    for load in loads[6:]:
        load.wait()
    for part in range(3):
        wt[part * c:(part + 1) * c, :] = nt(eye, wqkv_ref[:, part * c:(part + 1) * c]).astype(BF16)
    pick = pick_ref[...]

    def arrive(f, w, ref):
        if f == 0:
            parts = rims_in[0][w:w + 1] if w < WINDOWS - 1 else rims_in[0][w:]
        else:
            parts = rims_in[1][:1] if w == 0 else rims_in[1][1:] if w == WINDOWS - 1 else []
        for copy in parts:
            copy.wait()
        at, (first, size) = slice(w * TOK, (w + 1) * TOK), RIM_OF[w]
        ref[at, :] = (
            nn(own_ref[at, :], slab[f, low:]) + nn(rim_ref[at, :size], rim_in[f, first:first + size])
        ).astype(BF16)

    def at_of(w):
        return slice(w * TOK, (w + 1) * TOK)

    def g_of(g, part=0):
        return slice(part * c + g * gw, part * c + (g + 1) * gw)

    def forward(w):
        at = at_of(w)
        arrive(0, w, x_w)
        cells = x_w[at, :].astype(F32)
        average = jnp.mean(cells, axis=-1, keepdims=True)
        centred = cells - average
        rstd = lax.rsqrt(jnp.mean(centred * centred, axis=-1, keepdims=True) + 1e-05)
        rstd_s[at, :] = rstd
        n_w = centred * rstd
        n_s[at, :] = n_w
        here = n_w.astype(BF16)
        normed[at, :] = here
        kv[at, :] = nn(here, wqkv_ref[:, c:]).astype(BF16)
        qkv_t = nt(wt[...], here).astype(BF16)
        q_all = nn(qkv_t[:c], pick)
        k_ts[w] = qkv_t[c:2 * c]
        for g in range(groups):
            q_wide = (q_all[g_of(g)] * mine).astype(BF16)
            q_ws[w, g] = q_wide
            s = nn(kv[at, g_of(g)], q_wide) * scale + bt[g]
            top = jnp.max(s, axis=0, keepdims=True)
            e = jnp.exp(s - top)
            soft = e * (1.0 / jnp.sum(e, axis=0, keepdims=True))
            soft_s[w, g] = soft
            m_ts[g_of(g), :] = (nn(qkv_t[g_of(g, 2)], soft.astype(BF16)) * mine).astype(BF16)
        mix[at, :] = nt(pick, m_ts[...]).astype(BF16)

    def widen(w):
        dm_t = nt(wout_ref[...], dy_w[at_of(w), :]).astype(BF16)
        dm_all = nn(dm_t, pick)
        for g in range(groups):
            dm_ws[w, g] = (dm_all[g_of(g)] * mine).astype(BF16)

    def backward(g, w):
        at = at_of(w)
        soft = soft_s[w, g]
        dm_wide = dm_ws[w, g]
        da = nn(kv[at, g_of(g, 1)], dm_wide)
        ds = soft * (da - jnp.sum(soft * da, axis=0, keepdims=True))
        if w == 0:
            db[g] = ds
        else:
            db[g] += ds
        ds = ds.astype(BF16)
        dq_ts[w * gw:(w + 1) * gw, :] = (nn(k_ts[w, g_of(g), :], ds) * (mine * scale)).astype(BF16)
        dproj[at, g_of(g, 1)] = (nt(ds, q_ws[w, g]) * scale).astype(BF16)

    def values(g, w):
        dproj[at_of(w), g_of(g, 2)] = nt(soft_s[w, g].astype(BF16), dm_ws[w, g]).astype(BF16)

    def tile_at(t):
        i = 0
        while t >= CHUNKS[i]:
            t -= CHUNKS[i]
            i += 1
        if i == len(CHUNKS) - 1:
            share = CHUNKS[i] // (2 * nxy)
            return i, (t // share, t % share)
        half_tiles = CHUNKS[i] // 2
        share = half_tiles // nxy
        return i, (t // half_tiles, t % half_tiles // share, t % share)

    def put(t, value):
        i, at = tile_at(t)
        chunk_refs[i][0][at] = value.astype(BF16)

    def out_grads():
        normed_t[...] = nt(eye, normed[...]).astype(BF16)
        grad = nn(nt(eye, mix[...]).astype(BF16), dy_w[...]) * grad_scale
        for k in range(3):
            for r in range(24):
                put(k * 24 + r, grad[r * 16:(r + 1) * 16, k * 128:(k + 1) * 128])

    def column_grad(k, g, part):
        grad = nn(normed_t[...], dproj[:, g_of(g, part)]) * grad_scale
        for r in range(24):
            put(24 * k + r, grad[r * 16:(r + 1) * 16])

    def qk_grads(g):
        dq = nt(pick, dq_ts[...]).astype(BF16)
        for w in range(WINDOWS):
            dproj[at_of(w), g_of(g)] = dq[:, w * gw:(w + 1) * gw]
        for part in range(2):
            column_grad(6 + 2 * g + part, g, part)

    def columns_of(k):
        return g_of(k - 3, 2) if k < 6 else g_of((k - 6) // 2, (k - 6) % 2)

    class Chain:
        def __init__(self, refs):
            (self.gb, self.crecv, self.xs, self.xrecv, self.zbuf, self.fin, self.sem) = refs

        def send(self, stage, src, dst, device):
            remote(src, dst, self.sem.at[0, stage], self.sem.at[1, stage], device).start()

        def wait(self, side, stage, like):
            pltpu.make_async_copy(like, like, self.sem.at[side, stage]).wait()

        def start(self):
            self.send(0, self.gb.at[other], self.crecv, sibling)

        def first(self):
            self.wait(1, 0, self.crecv)
            self.xs[...] = (self.gb[core].astype(F32) + self.crecv[...].astype(F32)).astype(BF16)
            for o, (q, d) in enumerate(plane):
                self.send(1, self.xs.at[q], self.xrecv.at[o], d)

        def second(self):
            self.wait(1, 1, self.xrecv)
            total = self.xs[p].astype(F32)
            for o in range(nxy - 1):
                total += self.xrecv[o].astype(F32)
            self.zbuf[0] = total.astype(BF16)
            for o, (d, _) in enumerate(zs):
                self.send(2, self.zbuf.at[0], self.zbuf.at[o + 1], d)

        def third(self):
            if nz > 1:
                self.wait(1, 2, self.zbuf.at[pl.ds(1, nz - 1)])
            total = self.zbuf[z].astype(F32)
            for k in range(1, nz):
                total += self.zbuf[(z + nz - k) % nz].astype(F32)
            mine_at = self.fin.at[core, p]
            mine_at[...] = total.astype(BF16)
            for _, d in plane:
                self.send(3, mine_at, mine_at, d)

        def fourth(self):
            self.wait(1, 3, self.xrecv)
            self.send(4, self.fin.at[core], self.fin.at[core], sibling)

        def last(self):
            self.wait(1, 4, self.fin.at[other])

        def drain(self):
            self.wait(0, 0, self.crecv)
            self.wait(0, 1, self.xrecv)
            if nz > 1:
                self.wait(0, 2, self.zbuf.at[pl.ds(1, nz - 1)])
            self.wait(0, 3, self.xrecv)
            self.wait(0, 4, self.crecv)

    class Wide(Chain):
        def __init__(self, refs):
            (self.gb, self.xrecv, self.zbuf, self.fin, self.sem) = refs

        def start(self):
            for o, (q, d) in enumerate(wide):
                self.send(0, self.gb.at[q], self.xrecv.at[o], d)

        def second(self):
            self.wait(1, 0, self.xrecv)
            total = self.gb[rank].astype(F32)
            for o in range(2 * nxy - 1):
                total += self.xrecv[o].astype(F32)
            self.zbuf[0] = total.astype(BF16)
            for o, (d, _) in enumerate(zs):
                self.send(1, self.zbuf.at[0], self.zbuf.at[o + 1], d)

        def third(self):
            if nz > 1:
                self.wait(1, 1, self.zbuf.at[pl.ds(1, nz - 1)])
            total = self.zbuf[z].astype(F32)
            for k in range(1, nz):
                total += self.zbuf[(z + nz - k) % nz].astype(F32)
            mine_at = self.fin.at[rank]
            mine_at[...] = total.astype(BF16)
            for _, d in wide:
                self.send(2, mine_at, mine_at, d)

        def last(self):
            self.wait(1, 2, self.xrecv)

        def drain(self):
            self.wait(0, 0, self.xrecv)
            if nz > 1:
                self.wait(0, 1, self.zbuf.at[pl.ds(1, nz - 1)])
            self.wait(0, 2, self.xrecv)

    chains = [Chain(r) for r in chunk_refs[:-1]] + [Wide(chunk_refs[-1])]

    def unpack(first, end):
        for t in range(first, end):
            i, at = tile_at(t)
            value = chains[i].fin[at].astype(F32)
            r, k = t % 24, t // 24
            rows = slice(r * 16, (r + 1) * 16)
            if k < 3:
                gout_ref[rows, k * 128:(k + 1) * 128] = value
            else:
                gqkv_ref[rows, columns_of(k)] = value

    bshare = BIAS_TILES // lon_size

    def bias_wait(side, stage):
        pltpu.make_async_copy(brecv, brecv, b_sem.at[side, stage]).wait()

    def bias_core():
        rows = jnp.concatenate(
            [
                jnp.concatenate(
                    [
                        db[g, z2 * half:(z2 + 1) * half, j * blk:(j + 1) * blk]
                        for z2 in range(LEV)
                        for g in range(groups)
                    ]
                    + [jnp.zeros((half, 96), F32)],
                    axis=1,
                )
                for j in range(WW)
            ],
            axis=0,
        ).astype(BF16)
        dr = nn(gather_ref[...], rows).astype(BF16)
        for t in range(BIAS_TILES):
            k, r = t // 9, t % 9
            tile = dr[r * 16:(r + 1) * 16, k * 128:(k + 1) * 128] if k < 3 else jnp.zeros((16, 128), BF16)
            bb[bias_at(t)] = tile
        for o, (q, d) in enumerate(line):
            remote(bb.at[q], brecv.at[o], b_sem.at[0, 0], b_sem.at[1, 0], d).start()

    def bias_at(t):
        return t // bshare, t % bshare

    def bias_back():
        bias_wait(1, 0)
        total = bb[lon].astype(F32)
        for o in range(lon_size - 1):
            total += brecv[o].astype(F32)
        mine_at = bfin.at[lon]
        mine_at[...] = total.astype(BF16)
        for _, d in line:
            remote(mine_at, mine_at, b_sem.at[0, 1], b_sem.at[1, 1], d).start()

    def bias_end():
        bias_wait(1, 1)
        turned[144:, :] = jnp.zeros((256 - 144, 384), F32)
        for t in range(27):
            k, r = t // 9, t % 9
            turned[r * 16:(r + 1) * 16, k * 128:(k + 1) * 128] = bfin[bias_at(t)].astype(F32)
        flat = turned[...].T
        for z2 in range(LEV):
            for z1 in range(LEV):
                for i1 in range(WH):
                    for g in range(groups):
                        at = z2 * groups * blk + g * blk + (z1 * WH + i1) * GROUP
                        tab[g * GROUP:(g + 1) * GROUP, segment(z1, z2, i1)] = flat[at:at + GROUP, :width]
        dr_ref[:, 0, :] = tab[...]

    def pack_out(f):
        for w, (first, size) in enumerate(RIM_OF):
            rim_osnd[f, first:first + size] = nn(rimt_ref[first:first + size], ow[f, at_of(w)]).astype(BF16)

    def finish(f, ref):
        for copy in rims_out[f]:
            copy.wait()
        upper = nn(sendt_ref[...], rim_out[f]).astype(BF16)
        lower = (nn(ownt_ref[...], ow[f]) + nn(side_ref[...], rim_out[f, 208:256])).astype(BF16)
        for s in range(WH):
            full, r = (upper, s) if s < WH // 2 else (lower, s - WH // 2)
            ref[s] = full[r * PITCH:r * PITCH + COLS * LEV].reshape(COLS, LEV, c)

    stores = []

    def store(src, dst):
        stores.append(pltpu.make_async_copy(src, dst, out_sem.at[len(stores)]))
        stores[-1].start()

    def store_columns(first, end):
        for k in range(first, end):
            at = (slice(None), columns_of(k))
            store(gqkv_ref.at[at], outs_h[2].at[at])

    c0, c1, c2 = chains
    for w in range(WINDOWS):
        forward(w)
    ow[0] = (x_w[...].astype(F32) + nn(mix[...], wout_ref[...])).astype(BF16)
    pack_out(0)
    for copy in rims_out[0]:
        copy.start()
    for w in range(WINDOWS):
        arrive(1, w, dy_w)
    out_grads()
    for w in range(WINDOWS):
        widen(w)
    for g in range(groups):
        for w in range(WINDOWS):
            values(g, w)
        column_grad(3 + g, g, 2)
    c0.start()
    for w in range(WINDOWS):
        backward(0, w)
    c0.first()
    qk_grads(0)
    for w in range(WINDOWS):
        backward(1, w)
    qk_grads(1)
    c1.start()
    for w in range(WINDOWS):
        backward(2, w)
    c1.first()
    qk_grads(2)
    c2.start()
    c0.second()
    dn = nt(dproj[...], wqkv_ref[...])
    n_w = n_s[...]
    dx = dn - jnp.mean(dn, axis=-1, keepdims=True) - n_w * jnp.mean(dn * n_w, axis=-1, keepdims=True)
    ow[1] = (dx * rstd_s[...] + dy_w[...].astype(F32)).astype(BF16)
    pack_out(1)
    c1.second()
    bias_core()
    c0.third()
    c2.second()
    for copy in rims_out[1]:
        copy.start()
    finish(0, out_ref)
    store(out_ref, outs_h[0])
    c1.third()
    c0.fourth()
    bias_back()
    c2.third()
    c0.last()
    unpack(0, 128)
    store(gout_ref, outs_h[3])
    store_columns(3, 5)
    c1.fourth()
    bias_end()
    store(dr_ref, outs_h[4])
    finish(1, dx_ref)
    store(dx_ref, outs_h[1])
    c1.last()
    unpack(128, 224)
    store_columns(5, 9)
    c2.last()
    unpack(224, 288)
    store_columns(9, 12)
    for copy in stores:
        copy.wait()
    for chain in chains:
        chain.drain()
    bias_wait(0, 0)
    bias_wait(0, 1)


def fused(cells, cot, qkv_weight, out_weight, table, lon_size, lat_size, cells_total):
    c = out_weight.shape[0]
    heads, _, entries = table.shape
    groups = heads // GROUP
    consts = constants()
    ins = (cells, cot, qkv_weight, out_weight, table) + consts
    n, nz = lon_size // 4, lat_size // X_HI
    bshare = BIAS_TILES // lon_size
    gw = GROUP * HEAD
    vm = pltpu.VMEM
    dma = pltpu.SemaphoreType.DMA
    out_shape = (
        jax.ShapeDtypeStruct(cells.shape, BF16),
        jax.ShapeDtypeStruct(cells.shape, BF16),
        jax.ShapeDtypeStruct((c, 3 * c), F32),
        jax.ShapeDtypeStruct((c, c), F32),
        jax.ShapeDtypeStruct(table.shape, F32),
    )
    scratch = [vm(a.shape, a.dtype) for a in ins] + [
        dma((len(ins),)),
        vm((2, WH * PITCH, c), BF16),
        vm((2, RIM, c), BF16),
        vm((2, RIM, c), BF16),
        vm((groups, TOK, LANES), F32),
        vm((groups, TOK, LANES), F32),
        vm((ROWS, c), BF16),
        vm((ROWS, c), BF16),
        vm((ROWS, c), BF16),
        vm((c, ROWS), BF16),
        vm((ROWS, c), BF16),
        vm((ROWS, 3 * c), BF16),
        vm((3 * c, c), BF16),
        vm((2, ROWS, c), BF16),
        vm((2, RIM, c), BF16),
        vm((2, RIM, c), BF16),
        vm((ROWS, 2 * c), BF16),
        vm((WINDOWS, c, TOK), BF16),
        vm((WINDOWS, groups, gw, LANES), BF16),
        vm((WINDOWS, groups, TOK, LANES), F32),
        vm((c, LANES), BF16),
        vm((WINDOWS, groups, gw, LANES), BF16),
        vm((WINDOWS * gw, LANES), BF16),
        vm((heads, entries), F32),
        vm((heads * SLABS, WH * SPAN), F32),
        vm((256, 384), F32),
        vm((ROWS, c), F32),
        vm((ROWS, 1), F32),
        dma((2, 14)),
    ]
    tile = (16, 128)
    for tiles in CHUNKS[:-1]:
        share = tiles // (2 * n * n)
        scratch += [
            vm((2, n * n, share) + tile, BF16),
            vm((n * n, share) + tile, BF16),
            vm((n * n, share) + tile, BF16),
            vm((n * n - 1, share) + tile, BF16),
            vm((nz, share) + tile, BF16),
            vm((2, n * n, share) + tile, BF16),
            dma((2, 5)),
        ]
    share = CHUNKS[-1] // (2 * n * n)
    scratch += [
        vm((2 * n * n, share) + tile, BF16),
        vm((2 * n * n - 1, share) + tile, BF16),
        vm((nz, share) + tile, BF16),
        vm((2 * n * n, share) + tile, BF16),
        dma((2, 3)),
    ]
    scratch += [
        vm((lon_size, bshare) + tile, BF16),
        vm((lon_size - 1, bshare) + tile, BF16),
        vm((lon_size, bshare) + tile, BF16),
        dma((2, 2)),
    ]
    scratch += [vm(a.shape, a.dtype) for a in out_shape] + [dma((13,))]
    kernel = functools.partial(
        body, lon_size, lat_size, groups, (c // heads) ** -0.5, cells_total ** -0.5
    )
    results = pl.pallas_call(
        kernel,
        out_shape=out_shape,
        in_specs=[pl.BlockSpec(memory_space=pl.ANY)] * len(ins),
        out_specs=(pl.BlockSpec(memory_space=pl.ANY),) * len(out_shape),
        scratch_shapes=scratch,
        compiler_params=pltpu.CompilerParams(
            vmem_limit_bytes=60 * 1024 * 1024, collective_id=0, has_side_effects=True
        ),
        cost_estimate=pl.CostEstimate(flops=6_000_000_000, bytes_accessed=10_000_000, transcendentals=800_000),
    )(*ins)
    return handed_out(results)


def handed_out(arrays):
    cuts = [(i, k) for i, a in enumerate(arrays) for k in range(6 if i == 2 else 2 if i == 3 else 1)]

    def move(*refs):
        ins, outs, (sem, *held) = refs[:len(arrays)], refs[len(arrays):2 * len(arrays)], refs[2 * len(arrays):]
        into, out_of = [], []
        for j, (i, k) in enumerate(cuts):
            parts = sum(1 for at, _ in cuts if at == i)
            rows = arrays[i].shape[0] // parts
            at = pl.ds(k * rows, rows)
            into.append(pltpu.make_async_copy(ins[i].at[at], held[i].at[at], sem.at[0, j]))
            out_of.append(pltpu.make_async_copy(held[i].at[at], outs[i].at[at], sem.at[1, j]))
        for copy in into:
            copy.start()
        for first, second in zip(into, out_of):
            first.wait()
            second.start()
        for copy in out_of:
            copy.wait()

    return pl.pallas_call(
        move,
        out_shape=tuple(jax.ShapeDtypeStruct(a.shape, a.dtype) for a in arrays),
        in_specs=[pl.BlockSpec(memory_space=pl.ANY)] * len(arrays),
        out_specs=(pl.BlockSpec(memory_space=pl.ANY),) * len(arrays),
        scratch_shapes=[pltpu.SemaphoreType.DMA((2, len(cuts)))] + [pltpu.VMEM(a.shape, a.dtype) for a in arrays],
        compiler_params=pltpu.CompilerParams(vmem_limit_bytes=60 * 1024 * 1024),
    )(*arrays)


def on_device(cells, qkv_weight, out_weight, earth_bias, cotangent):
    lon_size, lat_size = lax.axis_size("lon"), lax.axis_size("lat")
    heads = earth_bias.shape[1]
    cells_total = LEV * cells.shape[1] * cells.shape[2] * lon_size * lat_size
    out, dx, gqkv, gout, dr = fused(
        cells.transpose(1, 2, 0, 3), cotangent.transpose(1, 2, 0, 3), qkv_weight, out_weight, earth_bias.transpose(1, 0, 2),
        lon_size, lat_size, cells_total
    )
    out, dx = out.transpose(2, 0, 1, 3), dx.transpose(2, 0, 1, 3)
    return out, dx, gqkv, gout, dr.transpose(1, 0, 2)


def solution(mesh):
    grid = P(None, "lat", "lon", None)
    return jax.shard_map(
        on_device,
        mesh=mesh,
        in_specs=(grid, P(), P(), P("lat", None, None), grid),
        out_specs=(grid, grid, P(), P(), P("lat", None, None)),
        check_vma=False,
    )
```

```python
import functools

import numpy as np
import jax
import jax.numpy as jnp
from jax import lax
from jax.experimental import pallas as pl
from jax.experimental.pallas import tpu as pltpu
from jax.sharding import PartitionSpec as P

LEV = 2
WH = 6
WW = 12
TOK = LEV * WH * WW
SLABS = LEV * WH
SPAN = 2 * WW - 1
GROUP = 4
HEAD = 32
LANES = GROUP * TOK
WINDOWS = 3
ROWS = WINDOWS * TOK
COLS = WINDOWS * WW
PITCH = 80
FINE_RIMS = ((0, 80, 0), (80, 80, 0), (160, 48, 0), (208, 48, 1), (256, 48, 2))
RIMS = ((0, 208, 0), (208, 48, 1), (256, 48, 2))
RIM_OF = ((0, 80), (80, 80), (160, 144))
RIM = 304
BIAS_TILES = 32
CHUNKS = (128, 96, 64)
X_HI = 2
F32 = jnp.float32
BF16 = jnp.bfloat16
MESH = pl.DeviceIdType.MESH


def nn(a, b):
    return lax.dot_general(a, b, (((1,), (0,)), ((), ())), preferred_element_type=F32)


def nt(a, b):
    return lax.dot_general(a, b, (((1,), (1,)), ((), ())), preferred_element_type=F32)


def constants():
    j1, i2, j2 = np.meshgrid(np.arange(WW), np.arange(WH), np.arange(WW), indexing="ij")
    spot = (i2 * SPAN + j1 - j2 + WW - 1).reshape(-1)
    spread = (spot[:, None] == np.arange(WH * SPAN)[None, :]).astype(np.float32)
    gather = np.zeros((144, spread.shape[0]), np.float32)
    gather[: WH * SPAN] = spread.T
    lane = np.arange(LANES)
    lane_col, lane_slab = lane // (SLABS * GROUP), lane // GROUP % SLABS
    token_of_lane = lane_slab * WW + lane_col
    pick = (np.arange(TOK)[:, None] == token_of_lane[None, :]).astype(np.float32)
    row_half = np.arange(TOK) // WW % WH >= WH - WH // 2
    lane_half = lane_slab % WH >= WH - WH // 2
    cross = np.where(row_half[:, None] != lane_half[None, :], -1e9, 0.0).astype(np.float32)
    own = np.zeros((ROWS, WH * PITCH), np.float32)
    rim = np.zeros((ROWS, RIM), np.float32)
    send = np.zeros((RIM, WH * PITCH), np.float32)
    h = WH // 2
    for w in range(WINDOWS):
        for z in range(LEV):
            for i in range(WH):
                for j in range(WW):
                    t = w * TOK + (z * WH + i) * WW + j
                    col = WW // 2 + w * WW + j
                    below, beside = i >= h, col >= COLS
                    row, k = ((i - h) if below else (i + h)), i % h
                    slab = row * PITCH + col % COLS * LEV + z
                    if not below and not beside:
                        own[t, slab] = 1
                        continue
                    if beside:
                        at = (256 if below else 208) + z * 18 + k * 6 + j - 6
                    elif w == WINDOWS - 1:
                        at = 160 + z * 18 + k * 6 + j
                    else:
                        at = 80 * w + z * 36 + k * 12 + j
                    rim[t, at] = 1
                    send[at, slab] = 1
    low = WH // 2 * PITCH
    rim_w = np.zeros((ROWS, 144), np.float32)
    rim_wt = np.zeros((RIM, TOK), np.float32)
    for w, (at, size) in enumerate(RIM_OF):
        block = rim[w * TOK:(w + 1) * TOK, at:at + size]
        rim_w[w * TOK:(w + 1) * TOK, :size] = block
        rim_wt[at:at + size] = block.T
    send_w = np.concatenate([send[:208, :low], send[208:256, low:], send[256:, :low]], axis=0)
    bf = lambda a: jnp.asarray(np.ascontiguousarray(a), BF16)
    return (
        bf(spread), bf(gather), bf(pick), jnp.asarray(cross, F32),
        bf(own[:, low:]), bf(rim_w), bf(send_w), bf(own[:, low:].T), bf(rim_wt), bf(send[:, :low].T),
        bf(send[208:256, low:].T),
    )


N_IN = 16


def body(lon_size, lat_size, groups, scale, grad_scale, *refs):
    (cells_h, cot_h, wqkv_h, wout_h, r_h) = refs[:5]
    consts_h = refs[5:N_IN]
    outs_h = refs[N_IN:N_IN + 5]
    (cells_v, cot_v, wqkv_ref, wout_ref, r_ref,
     spread_ref, gather_ref, pick_ref, cross_ref, own_ref, rim_ref, send_ref, ownt_ref, rimt_ref, sendt_ref,
     side_ref,
     load_sem, slab, rim_snd, rim_in, bt, db, x_w, dy_w, normed, normed_t, mix, dproj, wt, ow, rim_osnd, rim_out,
     kv, k_ts, q_ws, soft_s, m_ts, dm_ws, dq_ts, tab, rows_of, turned, n_s, rstd_s,
     halo_sem, *comm) = refs[N_IN + 5:]
    (out_ref, dx_ref, gqkv_ref, gout_ref, dr_ref, out_sem) = comm[-6:]
    many = 7 * (len(CHUNKS) - 1)
    chunk_refs = [comm[i:i + 7] for i in range(0, many, 7)] + [comm[many:many + 5]]
    (bb, brecv, bfin, b_sem) = comm[many + 5:-6]
    c = wout_ref.shape[0]
    n, nz = lon_size // 4, lat_size // X_HI
    half = WH * WW
    blk = SLABS * GROUP
    gw = GROUP * HEAD

    lon, lat = lax.axis_index("lon"), lax.axis_index("lat")
    core, x_lo, y = lon % 2, lon // 2 % 2, lon // 4
    x_hi, z = lat // nz, lat % nz
    x = x_hi * 2 + x_lo
    other = 1 - core
    nxy = n * n
    p = y * n + x

    def dev(lon_at, lat_at):
        return {"lon": lon_at, "lat": lat_at}

    def chip(x_at, y_at):
        return dev((y_at * 2 + x_at % 2) * 2 + core, x_at // 2 * nz + z)

    sibling = dev(lon + 1 - 2 * core, lat)
    plane, zs, line = [], [], []
    for o in range(1, nxy):
        q = (p + o) % nxy
        plane.append((q, chip(q % n, q // n)))
    rank = core * nxy + p
    wide = []
    for o in range(1, 2 * nxy):
        q = (rank + o) % (2 * nxy)
        at = q % nxy
        wide.append((q, dev((at // n * 2 + at % n % 2) * 2 + q // nxy, at % n // 2 * nz + z)))
    for o in range(1, lon_size):
        q = (lon + o) % lon_size
        line.append((q, dev(q, lat)))
    for o in range(1, nz):
        zs.append((dev(lon, x_hi * nz + (z + o) % nz), (z + nz - o) % nz))

    lon_prev, lon_next = (lon + lon_size - 1) % lon_size, (lon + 1) % lon_size
    lat_prev, lat_next = (lat + lat_size - 1) % lat_size, (lat + 1) % lat_size
    back = (dev(lon, lat_prev), dev(lon_prev, lat), dev(lon_prev, lat_prev))
    ahead = (dev(lon, lat_next), dev(lon_next, lat), dev(lon_next, lat_next))

    def remote(src, dst, send_sem, recv_sem, device):
        return pltpu.make_async_remote_copy(
            src_ref=src, dst_ref=dst, send_sem=send_sem, recv_sem=recv_sem, device_id=device, device_id_type=MESH
        )

    order = (
        (cells_h, cells_v), (consts_h[6], send_ref), (cot_h, cot_v), (r_h, r_ref), (consts_h[0], spread_ref),
        (consts_h[3], cross_ref), (wqkv_h, wqkv_ref), (consts_h[4], own_ref), (consts_h[5], rim_ref),
        (consts_h[2], pick_ref), (wout_h, wout_ref), (consts_h[8], rimt_ref), (consts_h[7], ownt_ref),
        (consts_h[9], sendt_ref), (consts_h[10], side_ref), (consts_h[1], gather_ref),
    )
    loads = [pltpu.make_async_copy(s, d, load_sem.at[i]) for i, (s, d) in enumerate(order)]
    for load in loads:
        load.start()

    barrier = pltpu.get_barrier_semaphore()

    def greet(device):
        pl.semaphore_signal(barrier, inc=1, device_id=device, device_id_type=MESH)

    partners = back + ahead
    partners += tuple(d for _, d in wide) + tuple(d for d, _ in zs)
    for device in partners:
        greet(device)

    def rim_copies(f, snd, rcv, devices, base, parts):
        return [
            remote(
                snd.at[f, pl.ds(at, size)], rcv.at[f, pl.ds(at, size)],
                halo_sem.at[0, base + k], halo_sem.at[1, base + k], devices[to],
            )
            for k, (at, size, to) in enumerate(parts)
        ]

    rims_in = (
        rim_copies(0, rim_snd, rim_in, back, 0, FINE_RIMS),
        rim_copies(1, rim_snd, rim_in, back, 5, RIMS),
    )
    rims_out = (
        rim_copies(0, rim_osnd, rim_out, ahead, 8, RIMS),
        rim_copies(1, rim_osnd, rim_out, ahead, 11, RIMS),
    )
    low = WH // 2 * PITCH
    for f, src in enumerate((cells_v, cot_v)):
        loads[2 * f].wait()
        for s in range(WH):
            slab[f, s * PITCH:(s + 1) * PITCH, :] = jnp.concatenate(
                [src[s].reshape(COLS * LEV, c), jnp.zeros((PITCH - COLS * LEV, c), BF16)], axis=0
            )
        if f == 0:
            loads[1].wait()
        rim_snd[f, :208] = nn(send_ref[:208], slab[f, :low]).astype(BF16)
        rim_snd[f, 208:256] = nn(send_ref[208:256], slab[f, low:]).astype(BF16)
        rim_snd[f, 256:] = nn(send_ref[256:], slab[f, :low]).astype(BF16)
        if f == 0:
            pl.semaphore_wait(barrier, len(partners))
        for copy in rims_in[f]:
            copy.start()

    for load in loads[3:6]:
        load.wait()
    last = (lat == lat_size - 1).astype(F32)
    tab[...] = r_ref[:, 0, :]
    width = WH * SPAN

    def segment(z1, z2, i1):
        return pl.ds(((z1 * LEV + z2) * WH + i1) * width, width)

    for z2 in range(LEV):
        for z1 in range(LEV):
            for i1 in range(WH):
                piece = tab[:, segment(z1, z2, i1)]
                for g in range(groups):
                    at = g * blk + (z1 * WH + i1) * GROUP
                    rows_of[at:at + GROUP, :] = piece[g * GROUP:(g + 1) * GROUP]
        table = rows_of[...]
        hi = table.astype(BF16)
        rest = table - hi.astype(F32)
        mid = rest.astype(BF16)
        lo = (rest - mid.astype(F32)).astype(BF16)
        spread = spread_ref[...]
        u = nt(spread, hi) + nt(spread, mid) + nt(spread, lo)
        for g in range(groups):
            rows = jnp.concatenate(
                [u[j * half:(j + 1) * half, g * blk:(g + 1) * blk] for j in range(WW)], axis=1
            )
            keep = pl.ds(z2 * half, half)
            bt[g, keep, :] = rows + cross_ref[keep, :] * last
    row = lax.broadcasted_iota(jnp.int32, (c, c), 0)
    col = lax.broadcasted_iota(jnp.int32, (c, c), 1)
    eye = (row == col).astype(F32).astype(BF16)
    head_row = lax.broadcasted_iota(jnp.int32, (gw, LANES), 0) // HEAD
    head_lane = lax.broadcasted_iota(jnp.int32, (gw, LANES), 1) % GROUP
    mine = (head_row == head_lane).astype(F32)
    for load in loads[6:]:
        load.wait()
    for part in range(3):
        wt[part * c:(part + 1) * c, :] = nt(eye, wqkv_ref[:, part * c:(part + 1) * c]).astype(BF16)
    pick = pick_ref[...]

    def arrive(f, w, ref):
        if f == 0:
            parts = rims_in[0][w:w + 1] if w < WINDOWS - 1 else rims_in[0][w:]
        else:
            parts = rims_in[1][:1] if w == 0 else rims_in[1][1:] if w == WINDOWS - 1 else []
        for copy in parts:
            copy.wait()
        at, (first, size) = slice(w * TOK, (w + 1) * TOK), RIM_OF[w]
        ref[at, :] = (
            nn(own_ref[at, :], slab[f, low:]) + nn(rim_ref[at, :size], rim_in[f, first:first + size])
        ).astype(BF16)

    def at_of(w):
        return slice(w * TOK, (w + 1) * TOK)

    def g_of(g, part=0):
        return slice(part * c + g * gw, part * c + (g + 1) * gw)

    def forward(w):
        at = at_of(w)
        arrive(0, w, x_w)
        cells = x_w[at, :].astype(F32)
        average = jnp.mean(cells, axis=-1, keepdims=True)
        centred = cells - average
        rstd = lax.rsqrt(jnp.mean(centred * centred, axis=-1, keepdims=True) + 1e-05)
        rstd_s[at, :] = rstd
        n_w = centred * rstd
        n_s[at, :] = n_w
        here = n_w.astype(BF16)
        normed[at, :] = here
        kv[at, :] = nn(here, wqkv_ref[:, c:]).astype(BF16)
        qkv_t = nt(wt[...], here).astype(BF16)
        q_all = nn(qkv_t[:c], pick)
        k_ts[w] = qkv_t[c:2 * c]
        for g in range(groups):
            q_wide = (q_all[g_of(g)] * mine).astype(BF16)
            q_ws[w, g] = q_wide
            s = nn(kv[at, g_of(g)], q_wide) * scale + bt[g]
            top = jnp.max(s, axis=0, keepdims=True)
            e = jnp.exp(s - top)
            soft = e * (1.0 / jnp.sum(e, axis=0, keepdims=True))
            soft_s[w, g] = soft
            m_ts[g_of(g), :] = (nn(qkv_t[g_of(g, 2)], soft.astype(BF16)) * mine).astype(BF16)
        mix[at, :] = nt(pick, m_ts[...]).astype(BF16)

    def widen(w):
        dm_t = nt(wout_ref[...], dy_w[at_of(w), :]).astype(BF16)
        dm_all = nn(dm_t, pick)
        for g in range(groups):
            dm_ws[w, g] = (dm_all[g_of(g)] * mine).astype(BF16)

    def backward(g, w):
        at = at_of(w)
        soft = soft_s[w, g]
        dm_wide = dm_ws[w, g]
        da = nn(kv[at, g_of(g, 1)], dm_wide)
        ds = soft * (da - jnp.sum(soft * da, axis=0, keepdims=True))
        if w == 0:
            db[g] = ds
        else:
            db[g] += ds
        ds = ds.astype(BF16)
        dq_ts[w * gw:(w + 1) * gw, :] = (nn(k_ts[w, g_of(g), :], ds) * (mine * scale)).astype(BF16)
        dproj[at, g_of(g, 1)] = (nt(ds, q_ws[w, g]) * scale).astype(BF16)

    def values(g, w):
        dproj[at_of(w), g_of(g, 2)] = nt(soft_s[w, g].astype(BF16), dm_ws[w, g]).astype(BF16)

    def tile_at(t):
        i = 0
        while t >= CHUNKS[i]:
            t -= CHUNKS[i]
            i += 1
        if i == len(CHUNKS) - 1:
            share = CHUNKS[i] // (2 * nxy)
            return i, (t // share, t % share)
        half_tiles = CHUNKS[i] // 2
        share = half_tiles // nxy
        return i, (t // half_tiles, t % half_tiles // share, t % share)

    def put(t, value):
        i, at = tile_at(t)
        chunk_refs[i][0][at] = value.astype(BF16)

    def out_grads():
        normed_t[...] = nt(eye, normed[...]).astype(BF16)
        grad = nn(nt(eye, mix[...]).astype(BF16), dy_w[...]) * grad_scale
        for k in range(3):
            for r in range(24):
                put(k * 24 + r, grad[r * 16:(r + 1) * 16, k * 128:(k + 1) * 128])

    def column_grad(k, g, part):
        grad = nn(normed_t[...], dproj[:, g_of(g, part)]) * grad_scale
        for r in range(24):
            put(24 * k + r, grad[r * 16:(r + 1) * 16])

    def qk_grads(g):
        dq = nt(pick, dq_ts[...]).astype(BF16)
        for w in range(WINDOWS):
            dproj[at_of(w), g_of(g)] = dq[:, w * gw:(w + 1) * gw]
        for part in range(2):
            column_grad(6 + 2 * g + part, g, part)

    def columns_of(k):
        return g_of(k - 3, 2) if k < 6 else g_of((k - 6) // 2, (k - 6) % 2)

    class Chain:
        def __init__(self, refs):
            (self.gb, self.crecv, self.xs, self.xrecv, self.zbuf, self.fin, self.sem) = refs

        def send(self, stage, src, dst, device):
            remote(src, dst, self.sem.at[0, stage], self.sem.at[1, stage], device).start()

        def wait(self, side, stage, like):
            pltpu.make_async_copy(like, like, self.sem.at[side, stage]).wait()

        def start(self):
            self.send(0, self.gb.at[other], self.crecv, sibling)

        def first(self):
            self.wait(1, 0, self.crecv)
            self.xs[...] = (self.gb[core].astype(F32) + self.crecv[...].astype(F32)).astype(BF16)
            for o, (q, d) in enumerate(plane):
                self.send(1, self.xs.at[q], self.xrecv.at[o], d)

        def second(self):
            self.wait(1, 1, self.xrecv)
            total = self.xs[p].astype(F32)
            for o in range(nxy - 1):
                total += self.xrecv[o].astype(F32)
            self.zbuf[0] = total.astype(BF16)
            for o, (d, _) in enumerate(zs):
                self.send(2, self.zbuf.at[0], self.zbuf.at[o + 1], d)

        def third(self):
            if nz > 1:
                self.wait(1, 2, self.zbuf.at[pl.ds(1, nz - 1)])
            total = self.zbuf[z].astype(F32)
            for k in range(1, nz):
                total += self.zbuf[(z + nz - k) % nz].astype(F32)
            mine_at = self.fin.at[core, p]
            mine_at[...] = total.astype(BF16)
            for _, d in plane:
                self.send(3, mine_at, mine_at, d)

        def fourth(self):
            self.wait(1, 3, self.xrecv)
            self.send(4, self.fin.at[core], self.fin.at[core], sibling)

        def last(self):
            self.wait(1, 4, self.fin.at[other])

        def drain(self):
            self.wait(0, 0, self.crecv)
            self.wait(0, 1, self.xrecv)
            if nz > 1:
                self.wait(0, 2, self.zbuf.at[pl.ds(1, nz - 1)])
            self.wait(0, 3, self.xrecv)
            self.wait(0, 4, self.crecv)

    class Wide(Chain):
        def __init__(self, refs):
            (self.gb, self.xrecv, self.zbuf, self.fin, self.sem) = refs

        def start(self):
            for o, (q, d) in enumerate(wide):
                self.send(0, self.gb.at[q], self.xrecv.at[o], d)

        def second(self):
            self.wait(1, 0, self.xrecv)
            total = self.gb[rank].astype(F32)
            for o in range(2 * nxy - 1):
                total += self.xrecv[o].astype(F32)
            self.zbuf[0] = total.astype(BF16)
            for o, (d, _) in enumerate(zs):
                self.send(1, self.zbuf.at[0], self.zbuf.at[o + 1], d)

        def third(self):
            if nz > 1:
                self.wait(1, 1, self.zbuf.at[pl.ds(1, nz - 1)])
            total = self.zbuf[z].astype(F32)
            for k in range(1, nz):
                total += self.zbuf[(z + nz - k) % nz].astype(F32)
            mine_at = self.fin.at[rank]
            mine_at[...] = total.astype(BF16)
            for _, d in wide:
                self.send(2, mine_at, mine_at, d)

        def last(self):
            self.wait(1, 2, self.xrecv)

        def drain(self):
            self.wait(0, 0, self.xrecv)
            if nz > 1:
                self.wait(0, 1, self.zbuf.at[pl.ds(1, nz - 1)])
            self.wait(0, 2, self.xrecv)

    chains = [Chain(r) for r in chunk_refs[:-1]] + [Wide(chunk_refs[-1])]

    def unpack(first, end):
        for t in range(first, end):
            i, at = tile_at(t)
            value = chains[i].fin[at].astype(F32)
            r, k = t % 24, t // 24
            rows = slice(r * 16, (r + 1) * 16)
            if k < 3:
                gout_ref[rows, k * 128:(k + 1) * 128] = value
            else:
                gqkv_ref[rows, columns_of(k)] = value

    bshare = BIAS_TILES // lon_size

    def bias_wait(side, stage):
        pltpu.make_async_copy(brecv, brecv, b_sem.at[side, stage]).wait()

    def bias_core():
        rows = jnp.concatenate(
            [
                jnp.concatenate(
                    [
                        db[g, z2 * half:(z2 + 1) * half, j * blk:(j + 1) * blk]
                        for z2 in range(LEV)
                        for g in range(groups)
                    ]
                    + [jnp.zeros((half, 96), F32)],
                    axis=1,
                )
                for j in range(WW)
            ],
            axis=0,
        ).astype(BF16)
        dr = nn(gather_ref[...], rows).astype(BF16)
        for t in range(BIAS_TILES):
            k, r = t // 9, t % 9
            tile = dr[r * 16:(r + 1) * 16, k * 128:(k + 1) * 128] if k < 3 else jnp.zeros((16, 128), BF16)
            bb[bias_at(t)] = tile
        for o, (q, d) in enumerate(line):
            remote(bb.at[q], brecv.at[o], b_sem.at[0, 0], b_sem.at[1, 0], d).start()

    def bias_at(t):
        return t // bshare, t % bshare

    def bias_back():
        bias_wait(1, 0)
        total = bb[lon].astype(F32)
        for o in range(lon_size - 1):
            total += brecv[o].astype(F32)
        mine_at = bfin.at[lon]
        mine_at[...] = total.astype(BF16)
        for _, d in line:
            remote(mine_at, mine_at, b_sem.at[0, 1], b_sem.at[1, 1], d).start()

    def bias_end():
        bias_wait(1, 1)
        turned[144:, :] = jnp.zeros((256 - 144, 384), F32)
        for t in range(27):
            k, r = t // 9, t % 9
            turned[r * 16:(r + 1) * 16, k * 128:(k + 1) * 128] = bfin[bias_at(t)].astype(F32)
        flat = turned[...].T
        for z2 in range(LEV):
            for z1 in range(LEV):
                for i1 in range(WH):
                    for g in range(groups):
                        at = z2 * groups * blk + g * blk + (z1 * WH + i1) * GROUP
                        tab[g * GROUP:(g + 1) * GROUP, segment(z1, z2, i1)] = flat[at:at + GROUP, :width]
        dr_ref[:, 0, :] = tab[...]

    def pack_out(f):
        for w, (first, size) in enumerate(RIM_OF):
            rim_osnd[f, first:first + size] = nn(rimt_ref[first:first + size], ow[f, at_of(w)]).astype(BF16)

    def finish(f, ref):
        for copy in rims_out[f]:
            copy.wait()
        upper = nn(sendt_ref[...], rim_out[f]).astype(BF16)
        lower = (nn(ownt_ref[...], ow[f]) + nn(side_ref[...], rim_out[f, 208:256])).astype(BF16)
        for s in range(WH):
            full, r = (upper, s) if s < WH // 2 else (lower, s - WH // 2)
            ref[s] = full[r * PITCH:r * PITCH + COLS * LEV].reshape(COLS, LEV, c)

    stores = []

    def store(src, dst):
        stores.append(pltpu.make_async_copy(src, dst, out_sem.at[len(stores)]))
        stores[-1].start()

    def store_columns(first, end):
        for k in range(first, end):
            at = (slice(None), columns_of(k))
            store(gqkv_ref.at[at], outs_h[2].at[at])

    c0, c1, c2 = chains
    for w in range(WINDOWS):
        forward(w)
    ow[0] = (x_w[...].astype(F32) + nn(mix[...], wout_ref[...])).astype(BF16)
    pack_out(0)
    for copy in rims_out[0]:
        copy.start()
    for w in range(WINDOWS):
        arrive(1, w, dy_w)
    out_grads()
    for w in range(WINDOWS):
        widen(w)
    for g in range(groups):
        for w in range(WINDOWS):
            values(g, w)
        column_grad(3 + g, g, 2)
    c0.start()
    for w in range(WINDOWS):
        backward(0, w)
    c0.first()
    qk_grads(0)
    for w in range(WINDOWS):
        backward(1, w)
    qk_grads(1)
    c1.start()
    backward(2, 0)
    backward(2, 1)
    c0.second()
    backward(2, 2)
    c1.first()
    qk_grads(2)
    c2.start()
    dn = nt(dproj[...], wqkv_ref[...])
    n_w = n_s[...]
    dx = dn - jnp.mean(dn, axis=-1, keepdims=True) - n_w * jnp.mean(dn * n_w, axis=-1, keepdims=True)
    ow[1] = (dx * rstd_s[...] + dy_w[...].astype(F32)).astype(BF16)
    pack_out(1)
    for copy in rims_out[1]:
        copy.start()
    c0.third()
    bias_core()
    c1.second()
    c2.second()
    finish(0, out_ref)
    store(out_ref, outs_h[0])
    c0.fourth()
    c1.third()
    bias_back()
    c0.last()
    unpack(0, 128)
    store(gout_ref, outs_h[3])
    store_columns(3, 5)
    c2.third()
    finish(1, dx_ref)
    store(dx_ref, outs_h[1])
    c1.fourth()
    bias_end()
    store(dr_ref, outs_h[4])
    c1.last()
    unpack(128, 224)
    store_columns(5, 9)
    c2.last()
    unpack(224, 288)
    store_columns(9, 12)
    for copy in stores:
        copy.wait()
    for chain in chains:
        chain.drain()
    bias_wait(0, 0)
    bias_wait(0, 1)


def fused(cells, cot, qkv_weight, out_weight, table, lon_size, lat_size, cells_total):
    c = out_weight.shape[0]
    heads, _, entries = table.shape
    groups = heads // GROUP
    consts = constants()
    ins = (cells, cot, qkv_weight, out_weight, table) + consts
    n, nz = lon_size // 4, lat_size // X_HI
    bshare = BIAS_TILES // lon_size
    gw = GROUP * HEAD
    vm = pltpu.VMEM
    dma = pltpu.SemaphoreType.DMA
    out_shape = (
        jax.ShapeDtypeStruct(cells.shape, BF16),
        jax.ShapeDtypeStruct(cells.shape, BF16),
        jax.ShapeDtypeStruct((c, 3 * c), F32),
        jax.ShapeDtypeStruct((c, c), F32),
        jax.ShapeDtypeStruct(table.shape, F32),
    )
    scratch = [vm(a.shape, a.dtype) for a in ins] + [
        dma((len(ins),)),
        vm((2, WH * PITCH, c), BF16),
        vm((2, RIM, c), BF16),
        vm((2, RIM, c), BF16),
        vm((groups, TOK, LANES), F32),
        vm((groups, TOK, LANES), F32),
        vm((ROWS, c), BF16),
        vm((ROWS, c), BF16),
        vm((ROWS, c), BF16),
        vm((c, ROWS), BF16),
        vm((ROWS, c), BF16),
        vm((ROWS, 3 * c), BF16),
        vm((3 * c, c), BF16),
        vm((2, ROWS, c), BF16),
        vm((2, RIM, c), BF16),
        vm((2, RIM, c), BF16),
        vm((ROWS, 2 * c), BF16),
        vm((WINDOWS, c, TOK), BF16),
        vm((WINDOWS, groups, gw, LANES), BF16),
        vm((WINDOWS, groups, TOK, LANES), F32),
        vm((c, LANES), BF16),
        vm((WINDOWS, groups, gw, LANES), BF16),
        vm((WINDOWS * gw, LANES), BF16),
        vm((heads, entries), F32),
        vm((heads * SLABS, WH * SPAN), F32),
        vm((256, 384), F32),
        vm((ROWS, c), F32),
        vm((ROWS, 1), F32),
        dma((2, 14)),
    ]
    tile = (16, 128)
    for tiles in CHUNKS[:-1]:
        share = tiles // (2 * n * n)
        scratch += [
            vm((2, n * n, share) + tile, BF16),
            vm((n * n, share) + tile, BF16),
            vm((n * n, share) + tile, BF16),
            vm((n * n - 1, share) + tile, BF16),
            vm((nz, share) + tile, BF16),
            vm((2, n * n, share) + tile, BF16),
            dma((2, 5)),
        ]
    share = CHUNKS[-1] // (2 * n * n)
    scratch += [
        vm((2 * n * n, share) + tile, BF16),
        vm((2 * n * n - 1, share) + tile, BF16),
        vm((nz, share) + tile, BF16),
        vm((2 * n * n, share) + tile, BF16),
        dma((2, 3)),
    ]
    scratch += [
        vm((lon_size, bshare) + tile, BF16),
        vm((lon_size - 1, bshare) + tile, BF16),
        vm((lon_size, bshare) + tile, BF16),
        dma((2, 2)),
    ]
    scratch += [vm(a.shape, a.dtype) for a in out_shape] + [dma((13,))]
    kernel = functools.partial(
        body, lon_size, lat_size, groups, (c // heads) ** -0.5, cells_total ** -0.5
    )
    results = pl.pallas_call(
        kernel,
        out_shape=out_shape,
        in_specs=[pl.BlockSpec(memory_space=pl.ANY)] * len(ins),
        out_specs=(pl.BlockSpec(memory_space=pl.ANY),) * len(out_shape),
        scratch_shapes=scratch,
        compiler_params=pltpu.CompilerParams(
            vmem_limit_bytes=60 * 1024 * 1024, collective_id=0, has_side_effects=True
        ),
        cost_estimate=pl.CostEstimate(flops=6_000_000_000, bytes_accessed=10_000_000, transcendentals=800_000),
    )(*ins)
    return handed_out(results)


def handed_out(arrays):
    cuts = [(i, k) for i, a in enumerate(arrays) for k in range(6 if i == 2 else 2 if i == 3 else 1)]

    def move(*refs):
        ins, outs, (sem, *held) = refs[:len(arrays)], refs[len(arrays):2 * len(arrays)], refs[2 * len(arrays):]
        into, out_of = [], []
        for j, (i, k) in enumerate(cuts):
            parts = sum(1 for at, _ in cuts if at == i)
            rows = arrays[i].shape[0] // parts
            at = pl.ds(k * rows, rows)
            into.append(pltpu.make_async_copy(ins[i].at[at], held[i].at[at], sem.at[0, j]))
            out_of.append(pltpu.make_async_copy(held[i].at[at], outs[i].at[at], sem.at[1, j]))
        for copy in into:
            copy.start()
        for first, second in zip(into, out_of):
            first.wait()
            second.start()
        for copy in out_of:
            copy.wait()

    return pl.pallas_call(
        move,
        out_shape=tuple(jax.ShapeDtypeStruct(a.shape, a.dtype) for a in arrays),
        in_specs=[pl.BlockSpec(memory_space=pl.ANY)] * len(arrays),
        out_specs=(pl.BlockSpec(memory_space=pl.ANY),) * len(arrays),
        scratch_shapes=[pltpu.SemaphoreType.DMA((2, len(cuts)))] + [pltpu.VMEM(a.shape, a.dtype) for a in arrays],
        compiler_params=pltpu.CompilerParams(vmem_limit_bytes=60 * 1024 * 1024),
    )(*arrays)


def on_device(cells, qkv_weight, out_weight, earth_bias, cotangent):
    lon_size, lat_size = lax.axis_size("lon"), lax.axis_size("lat")
    heads = earth_bias.shape[1]
    cells_total = LEV * cells.shape[1] * cells.shape[2] * lon_size * lat_size
    out, dx, gqkv, gout, dr = fused(
        cells.transpose(1, 2, 0, 3), cotangent.transpose(1, 2, 0, 3), qkv_weight, out_weight, earth_bias.transpose(1, 0, 2),
        lon_size, lat_size, cells_total
    )
    out, dx = out.transpose(2, 0, 1, 3), dx.transpose(2, 0, 1, 3)
    return out, dx, gqkv, gout, dr.transpose(1, 0, 2)


def solution(mesh):
    grid = P(None, "lat", "lon", None)
    return jax.shard_map(
        on_device,
        mesh=mesh,
        in_specs=(grid, P(), P(), P("lat", None, None), grid),
        out_specs=(grid, grid, P(), P(), P("lat", None, None)),
        check_vma=False,
    )
```

```python
import functools

import numpy as np
import jax
import jax.numpy as jnp
from jax import lax
from jax.experimental import pallas as pl
from jax.experimental.pallas import tpu as pltpu
from jax.sharding import PartitionSpec as P

LEV = 2
WH = 6
WW = 12
TOK = LEV * WH * WW
SLABS = LEV * WH
SPAN = 2 * WW - 1
GROUP = 4
HEAD = 32
LANES = GROUP * TOK
WINDOWS = 3
ROWS = WINDOWS * TOK
COLS = WINDOWS * WW
PITCH = 80
FINE_RIMS = ((0, 80, 0), (80, 80, 0), (160, 48, 0), (208, 48, 1), (256, 48, 2))
RIMS = ((0, 208, 0), (208, 48, 1), (256, 48, 2))
RIM_OF = ((0, 80), (80, 80), (160, 144))
RIM = 304
BIAS_TILES = 32
CHUNKS = (128, 96, 64)
X_HI = 2
F32 = jnp.float32
BF16 = jnp.bfloat16
MESH = pl.DeviceIdType.MESH


def nn(a, b):
    return lax.dot_general(a, b, (((1,), (0,)), ((), ())), preferred_element_type=F32)


def nt(a, b):
    return lax.dot_general(a, b, (((1,), (1,)), ((), ())), preferred_element_type=F32)


def constants():
    j1, i2, j2 = np.meshgrid(np.arange(WW), np.arange(WH), np.arange(WW), indexing="ij")
    spot = (i2 * SPAN + j1 - j2 + WW - 1).reshape(-1)
    spread = (spot[:, None] == np.arange(WH * SPAN)[None, :]).astype(np.float32)
    gather = np.zeros((144, spread.shape[0]), np.float32)
    gather[: WH * SPAN] = spread.T
    lane = np.arange(LANES)
    lane_col, lane_slab = lane // (SLABS * GROUP), lane // GROUP % SLABS
    token_of_lane = lane_slab * WW + lane_col
    pick = (np.arange(TOK)[:, None] == token_of_lane[None, :]).astype(np.float32)
    row_half = np.arange(TOK) // WW % WH >= WH - WH // 2
    lane_half = lane_slab % WH >= WH - WH // 2
    cross = np.where(row_half[:, None] != lane_half[None, :], -1e9, 0.0).astype(np.float32)
    own = np.zeros((ROWS, WH * PITCH), np.float32)
    rim = np.zeros((ROWS, RIM), np.float32)
    send = np.zeros((RIM, WH * PITCH), np.float32)
    h = WH // 2
    for w in range(WINDOWS):
        for z in range(LEV):
            for i in range(WH):
                for j in range(WW):
                    t = w * TOK + (z * WH + i) * WW + j
                    col = WW // 2 + w * WW + j
                    below, beside = i >= h, col >= COLS
                    row, k = ((i - h) if below else (i + h)), i % h
                    slab = row * PITCH + col % COLS * LEV + z
                    if not below and not beside:
                        own[t, slab] = 1
                        continue
                    if beside:
                        at = (256 if below else 208) + z * 18 + k * 6 + j - 6
                    elif w == WINDOWS - 1:
                        at = 160 + z * 18 + k * 6 + j
                    else:
                        at = 80 * w + z * 36 + k * 12 + j
                    rim[t, at] = 1
                    send[at, slab] = 1
    low = WH // 2 * PITCH
    rim_w = np.zeros((ROWS, 144), np.float32)
    rim_wt = np.zeros((RIM, TOK), np.float32)
    for w, (at, size) in enumerate(RIM_OF):
        block = rim[w * TOK:(w + 1) * TOK, at:at + size]
        rim_w[w * TOK:(w + 1) * TOK, :size] = block
        rim_wt[at:at + size] = block.T
    send_w = np.concatenate([send[:208, :low], send[208:256, low:], send[256:, :low]], axis=0)
    bf = lambda a: jnp.asarray(np.ascontiguousarray(a), BF16)
    return (
        bf(spread), bf(gather), bf(pick), jnp.asarray(cross, F32),
        bf(own[:, low:]), bf(rim_w), bf(send_w), bf(own[:, low:].T), bf(rim_wt), bf(send[:, :low].T),
        bf(send[208:256, low:].T),
    )


N_IN = 16


def body(lon_size, lat_size, groups, scale, grad_scale, *refs):
    (cells_h, cot_h, wqkv_h, wout_h, r_h) = refs[:5]
    consts_h = refs[5:N_IN]
    outs_h = refs[N_IN:N_IN + 5]
    (cells_v, cot_v, wqkv_ref, wout_ref, r_ref,
     spread_ref, gather_ref, pick_ref, cross_ref, own_ref, rim_ref, send_ref, ownt_ref, rimt_ref, sendt_ref,
     side_ref,
     load_sem, slab, rim_snd, rim_in, bt, db, x_w, dy_w, normed, normed_t, mix, dproj, wt, ow, rim_osnd, rim_out,
     kv, k_ts, q_ws, soft_s, m_ts, dm_ws, dq_ts, tab, rows_of, turned, n_s, rstd_s,
     halo_sem, *comm) = refs[N_IN + 5:]
    (out_ref, dx_ref, gqkv_ref, gout_ref, dr_ref, out_sem) = comm[-6:]
    many = 7 * (len(CHUNKS) - 1)
    chunk_refs = [comm[i:i + 7] for i in range(0, many, 7)] + [comm[many:many + 5]]
    (bb, brecv, bfin, b_sem) = comm[many + 5:-6]
    c = wout_ref.shape[0]
    n, nz = lon_size // 4, lat_size // X_HI
    half = WH * WW
    blk = SLABS * GROUP
    gw = GROUP * HEAD

    lon, lat = lax.axis_index("lon"), lax.axis_index("lat")
    core, x_lo, y = lon % 2, lon // 2 % 2, lon // 4
    x_hi, z = lat // nz, lat % nz
    x = x_hi * 2 + x_lo
    other = 1 - core
    nxy = n * n
    p = y * n + x

    def dev(lon_at, lat_at):
        return {"lon": lon_at, "lat": lat_at}

    def chip(x_at, y_at):
        return dev((y_at * 2 + x_at % 2) * 2 + core, x_at // 2 * nz + z)

    sibling = dev(lon + 1 - 2 * core, lat)
    plane, zs, line = [], [], []
    for o in range(1, nxy):
        q = (p + o) % nxy
        plane.append((q, chip(q % n, q // n)))
    rank = core * nxy + p
    wide = []
    for o in range(1, 2 * nxy):
        q = (rank + o) % (2 * nxy)
        at = q % nxy
        wide.append((q, dev((at // n * 2 + at % n % 2) * 2 + q // nxy, at % n // 2 * nz + z)))
    for o in range(1, lon_size):
        q = (lon + o) % lon_size
        line.append((q, dev(q, lat)))
    for o in range(1, nz):
        zs.append((dev(lon, x_hi * nz + (z + o) % nz), (z + nz - o) % nz))

    lon_prev, lon_next = (lon + lon_size - 1) % lon_size, (lon + 1) % lon_size
    lat_prev, lat_next = (lat + lat_size - 1) % lat_size, (lat + 1) % lat_size
    back = (dev(lon, lat_prev), dev(lon_prev, lat), dev(lon_prev, lat_prev))
    ahead = (dev(lon, lat_next), dev(lon_next, lat), dev(lon_next, lat_next))

    def remote(src, dst, send_sem, recv_sem, device):
        return pltpu.make_async_remote_copy(
            src_ref=src, dst_ref=dst, send_sem=send_sem, recv_sem=recv_sem, device_id=device, device_id_type=MESH
        )

    order = (
        (cells_h, cells_v), (consts_h[6], send_ref), (cot_h, cot_v), (r_h, r_ref), (consts_h[0], spread_ref),
        (consts_h[3], cross_ref), (wqkv_h, wqkv_ref), (consts_h[4], own_ref), (consts_h[5], rim_ref),
        (consts_h[2], pick_ref), (wout_h, wout_ref), (consts_h[8], rimt_ref), (consts_h[7], ownt_ref),
        (consts_h[9], sendt_ref), (consts_h[10], side_ref), (consts_h[1], gather_ref),
    )
    loads = [pltpu.make_async_copy(s, d, load_sem.at[i]) for i, (s, d) in enumerate(order)]
    for load in loads:
        load.start()

    barrier = pltpu.get_barrier_semaphore()

    def greet(device):
        pl.semaphore_signal(barrier, inc=1, device_id=device, device_id_type=MESH)

    partners = back + ahead
    partners += tuple(d for _, d in wide) + tuple(d for d, _ in zs)
    for device in partners:
        greet(device)

    def rim_copies(f, snd, rcv, devices, base, parts):
        return [
            remote(
                snd.at[f, pl.ds(at, size)], rcv.at[f, pl.ds(at, size)],
                halo_sem.at[0, base + k], halo_sem.at[1, base + k], devices[to],
            )
            for k, (at, size, to) in enumerate(parts)
        ]

    rims_in = (
        rim_copies(0, rim_snd, rim_in, back, 0, FINE_RIMS),
        rim_copies(1, rim_snd, rim_in, back, 5, RIMS),
    )
    rims_out = (
        rim_copies(0, rim_osnd, rim_out, ahead, 8, RIMS),
        rim_copies(1, rim_osnd, rim_out, ahead, 11, RIMS),
    )
    low = WH // 2 * PITCH
    for f, src in enumerate((cells_v, cot_v)):
        loads[2 * f].wait()
        for s in range(WH):
            slab[f, s * PITCH:(s + 1) * PITCH, :] = jnp.concatenate(
                [src[s].reshape(COLS * LEV, c), jnp.zeros((PITCH - COLS * LEV, c), BF16)], axis=0
            )
        if f == 0:
            loads[1].wait()
        rim_snd[f, :208] = nn(send_ref[:208], slab[f, :low]).astype(BF16)
        rim_snd[f, 208:256] = nn(send_ref[208:256], slab[f, low:]).astype(BF16)
        rim_snd[f, 256:] = nn(send_ref[256:], slab[f, :low]).astype(BF16)
        if f == 0:
            pl.semaphore_wait(barrier, len(partners))
        for copy in rims_in[f]:
            copy.start()

    for load in loads[3:6]:
        load.wait()
    last = (lat == lat_size - 1).astype(F32)
    tab[...] = r_ref[:, 0, :]
    width = WH * SPAN

    def segment(z1, z2, i1):
        return pl.ds(((z1 * LEV + z2) * WH + i1) * width, width)

    for z2 in range(LEV):
        for z1 in range(LEV):
            for i1 in range(WH):
                piece = tab[:, segment(z1, z2, i1)]
                for g in range(groups):
                    at = g * blk + (z1 * WH + i1) * GROUP
                    rows_of[at:at + GROUP, :] = piece[g * GROUP:(g + 1) * GROUP]
        table = rows_of[...]
        hi = table.astype(BF16)
        rest = table - hi.astype(F32)
        mid = rest.astype(BF16)
        lo = (rest - mid.astype(F32)).astype(BF16)
        spread = spread_ref[...]
        u = nt(spread, hi) + nt(spread, mid) + nt(spread, lo)
        for g in range(groups):
            rows = jnp.concatenate(
                [u[j * half:(j + 1) * half, g * blk:(g + 1) * blk] for j in range(WW)], axis=1
            )
            keep = pl.ds(z2 * half, half)
            bt[g, keep, :] = rows + cross_ref[keep, :] * last
    row = lax.broadcasted_iota(jnp.int32, (c, c), 0)
    col = lax.broadcasted_iota(jnp.int32, (c, c), 1)
    eye = (row == col).astype(F32).astype(BF16)
    head_row = lax.broadcasted_iota(jnp.int32, (gw, LANES), 0) // HEAD
    head_lane = lax.broadcasted_iota(jnp.int32, (gw, LANES), 1) % GROUP
    mine = (head_row == head_lane).astype(F32)
    for load in loads[6:]:
        load.wait()
    for part in range(3):
        wt[part * c:(part + 1) * c, :] = nt(eye, wqkv_ref[:, part * c:(part + 1) * c]).astype(BF16)
    pick = pick_ref[...]

    def arrive(f, w, ref):
        if f == 0:
            parts = rims_in[0][w:w + 1] if w < WINDOWS - 1 else rims_in[0][w:]
        else:
            parts = rims_in[1][:1] if w == 0 else rims_in[1][1:] if w == WINDOWS - 1 else []
        for copy in parts:
            copy.wait()
        at, (first, size) = slice(w * TOK, (w + 1) * TOK), RIM_OF[w]
        ref[at, :] = (
            nn(own_ref[at, :], slab[f, low:]) + nn(rim_ref[at, :size], rim_in[f, first:first + size])
        ).astype(BF16)

    def at_of(w):
        return slice(w * TOK, (w + 1) * TOK)

    def g_of(g, part=0):
        return slice(part * c + g * gw, part * c + (g + 1) * gw)

    def forward(w):
        at = at_of(w)
        arrive(0, w, x_w)
        cells = x_w[at, :].astype(F32)
        average = jnp.mean(cells, axis=-1, keepdims=True)
        centred = cells - average
        rstd = lax.rsqrt(jnp.mean(centred * centred, axis=-1, keepdims=True) + 1e-05)
        rstd_s[at, :] = rstd
        n_w = centred * rstd
        n_s[at, :] = n_w
        here = n_w.astype(BF16)
        normed[at, :] = here
        kv[at, :] = nn(here, wqkv_ref[:, c:]).astype(BF16)
        qkv_t = nt(wt[...], here).astype(BF16)
        q_all = nn(qkv_t[:c], pick)
        k_ts[w] = qkv_t[c:2 * c]
        for g in range(groups):
            q_wide = (q_all[g_of(g)] * mine).astype(BF16)
            q_ws[w, g] = q_wide
            s = nn(kv[at, g_of(g)], q_wide) * scale + bt[g]
            top = jnp.max(s, axis=0, keepdims=True)
            e = jnp.exp(s - top)
            soft = e * (1.0 / jnp.sum(e, axis=0, keepdims=True))
            soft_s[w, g] = soft
            m_ts[g_of(g), :] = (nn(qkv_t[g_of(g, 2)], soft.astype(BF16)) * mine).astype(BF16)
        mix[at, :] = nt(pick, m_ts[...]).astype(BF16)

    def widen(w):
        dm_t = nt(wout_ref[...], dy_w[at_of(w), :]).astype(BF16)
        dm_all = nn(dm_t, pick)
        for g in range(groups):
            dm_ws[w, g] = (dm_all[g_of(g)] * mine).astype(BF16)

    def backward(g, w):
        at = at_of(w)
        soft = soft_s[w, g]
        dm_wide = dm_ws[w, g]
        da = nn(kv[at, g_of(g, 1)], dm_wide)
        ds = soft * (da - jnp.sum(soft * da, axis=0, keepdims=True))
        if w == 0:
            db[g] = ds
        else:
            db[g] += ds
        ds = ds.astype(BF16)
        dq_ts[w * gw:(w + 1) * gw, :] = (nn(k_ts[w, g_of(g), :], ds) * (mine * scale)).astype(BF16)
        dproj[at, g_of(g, 1)] = (nt(ds, q_ws[w, g]) * scale).astype(BF16)

    def values(g, w):
        dproj[at_of(w), g_of(g, 2)] = nt(soft_s[w, g].astype(BF16), dm_ws[w, g]).astype(BF16)

    def tile_at(t):
        i = 0
        while t >= CHUNKS[i]:
            t -= CHUNKS[i]
            i += 1
        if i == len(CHUNKS) - 1:
            share = CHUNKS[i] // (2 * nxy)
            return i, (t // share, t % share)
        half_tiles = CHUNKS[i] // 2
        share = half_tiles // nxy
        return i, (t // half_tiles, t % half_tiles // share, t % share)

    def put(t, value):
        i, at = tile_at(t)
        chunk_refs[i][0][at] = value.astype(BF16)

    def out_grads():
        normed_t[...] = nt(eye, normed[...]).astype(BF16)
        grad = nn(nt(eye, mix[...]).astype(BF16), dy_w[...]) * grad_scale
        for k in range(3):
            for r in range(24):
                put(k * 24 + r, grad[r * 16:(r + 1) * 16, k * 128:(k + 1) * 128])

    def column_grad(k, g, part):
        grad = nn(normed_t[...], dproj[:, g_of(g, part)]) * grad_scale
        for r in range(24):
            put(24 * k + r, grad[r * 16:(r + 1) * 16])

    def qk_grads(g):
        dq = nt(pick, dq_ts[...]).astype(BF16)
        for w in range(WINDOWS):
            dproj[at_of(w), g_of(g)] = dq[:, w * gw:(w + 1) * gw]
        for part in range(2):
            column_grad(6 + 2 * g + part, g, part)

    def columns_of(k):
        return g_of(k - 3, 2) if k < 6 else g_of((k - 6) // 2, (k - 6) % 2)

    class Chain:
        def __init__(self, refs):
            (self.gb, self.crecv, self.xs, self.xrecv, self.zbuf, self.fin, self.sem) = refs

        def send(self, stage, src, dst, device):
            remote(src, dst, self.sem.at[0, stage], self.sem.at[1, stage], device).start()

        def wait(self, side, stage, like):
            pltpu.make_async_copy(like, like, self.sem.at[side, stage]).wait()

        def start(self):
            self.send(0, self.gb.at[other], self.crecv, sibling)

        def first(self):
            self.wait(1, 0, self.crecv)
            self.xs[...] = (self.gb[core].astype(F32) + self.crecv[...].astype(F32)).astype(BF16)
            for o, (q, d) in enumerate(plane):
                self.send(1, self.xs.at[q], self.xrecv.at[o], d)

        def second(self):
            self.wait(1, 1, self.xrecv)
            total = self.xs[p].astype(F32)
            for o in range(nxy - 1):
                total += self.xrecv[o].astype(F32)
            self.zbuf[0] = total.astype(BF16)
            for o, (d, _) in enumerate(zs):
                self.send(2, self.zbuf.at[0], self.zbuf.at[o + 1], d)

        def third(self):
            if nz > 1:
                self.wait(1, 2, self.zbuf.at[pl.ds(1, nz - 1)])
            total = self.zbuf[z].astype(F32)
            for k in range(1, nz):
                total += self.zbuf[(z + nz - k) % nz].astype(F32)
            mine_at = self.fin.at[core, p]
            mine_at[...] = total.astype(BF16)
            for _, d in plane:
                self.send(3, mine_at, mine_at, d)

        def fourth(self):
            self.wait(1, 3, self.xrecv)
            self.send(4, self.fin.at[core], self.fin.at[core], sibling)

        def last(self):
            self.wait(1, 4, self.fin.at[other])

        def drain(self):
            self.wait(0, 0, self.crecv)
            self.wait(0, 1, self.xrecv)
            if nz > 1:
                self.wait(0, 2, self.zbuf.at[pl.ds(1, nz - 1)])
            self.wait(0, 3, self.xrecv)
            self.wait(0, 4, self.crecv)

    class Wide(Chain):
        def __init__(self, refs):
            (self.gb, self.xrecv, self.zbuf, self.fin, self.sem) = refs

        def start(self):
            for o, (q, d) in enumerate(wide):
                self.send(0, self.gb.at[q], self.xrecv.at[o], d)

        def second(self):
            self.wait(1, 0, self.xrecv)
            total = self.gb[rank].astype(F32)
            for o in range(2 * nxy - 1):
                total += self.xrecv[o].astype(F32)
            self.zbuf[0] = total.astype(BF16)
            for o, (d, _) in enumerate(zs):
                self.send(1, self.zbuf.at[0], self.zbuf.at[o + 1], d)

        def third(self):
            if nz > 1:
                self.wait(1, 1, self.zbuf.at[pl.ds(1, nz - 1)])
            total = self.zbuf[z].astype(F32)
            for k in range(1, nz):
                total += self.zbuf[(z + nz - k) % nz].astype(F32)
            mine_at = self.fin.at[rank]
            mine_at[...] = total.astype(BF16)
            for _, d in wide:
                self.send(2, mine_at, mine_at, d)

        def last(self):
            self.wait(1, 2, self.xrecv)

        def drain(self):
            self.wait(0, 0, self.xrecv)
            if nz > 1:
                self.wait(0, 1, self.zbuf.at[pl.ds(1, nz - 1)])
            self.wait(0, 2, self.xrecv)

    chains = [Chain(r) for r in chunk_refs[:-1]] + [Wide(chunk_refs[-1])]

    def unpack(first, end):
        for t in range(first, end):
            i, at = tile_at(t)
            value = chains[i].fin[at].astype(F32)
            r, k = t % 24, t // 24
            rows = slice(r * 16, (r + 1) * 16)
            if k < 3:
                gout_ref[rows, k * 128:(k + 1) * 128] = value
            else:
                gqkv_ref[rows, columns_of(k)] = value

    bshare = BIAS_TILES // lon_size

    def bias_wait(side, stage):
        pltpu.make_async_copy(brecv, brecv, b_sem.at[side, stage]).wait()

    def bias_core():
        rows = jnp.concatenate(
            [
                jnp.concatenate(
                    [
                        db[g, z2 * half:(z2 + 1) * half, j * blk:(j + 1) * blk]
                        for z2 in range(LEV)
                        for g in range(groups)
                    ]
                    + [jnp.zeros((half, 96), F32)],
                    axis=1,
                )
                for j in range(WW)
            ],
            axis=0,
        ).astype(BF16)
        dr = nn(gather_ref[...], rows).astype(BF16)
        for t in range(BIAS_TILES):
            k, r = t // 9, t % 9
            tile = dr[r * 16:(r + 1) * 16, k * 128:(k + 1) * 128] if k < 3 else jnp.zeros((16, 128), BF16)
            bb[bias_at(t)] = tile
        for o, (q, d) in enumerate(line):
            remote(bb.at[q], brecv.at[o], b_sem.at[0, 0], b_sem.at[1, 0], d).start()

    def bias_at(t):
        return t // bshare, t % bshare

    def bias_back():
        bias_wait(1, 0)
        total = bb[lon].astype(F32)
        for o in range(lon_size - 1):
            total += brecv[o].astype(F32)
        mine_at = bfin.at[lon]
        mine_at[...] = total.astype(BF16)
        for _, d in line:
            remote(mine_at, mine_at, b_sem.at[0, 1], b_sem.at[1, 1], d).start()

    def bias_end():
        bias_wait(1, 1)
        turned[144:, :] = jnp.zeros((256 - 144, 384), F32)
        for t in range(27):
            k, r = t // 9, t % 9
            turned[r * 16:(r + 1) * 16, k * 128:(k + 1) * 128] = bfin[bias_at(t)].astype(F32)
        flat = turned[...].T
        for z2 in range(LEV):
            for z1 in range(LEV):
                for i1 in range(WH):
                    for g in range(groups):
                        at = z2 * groups * blk + g * blk + (z1 * WH + i1) * GROUP
                        tab[g * GROUP:(g + 1) * GROUP, segment(z1, z2, i1)] = flat[at:at + GROUP, :width]
        dr_ref[:, 0, :] = tab[...]

    def pack_out(f):
        for w, (first, size) in enumerate(RIM_OF):
            rim_osnd[f, first:first + size] = nn(rimt_ref[first:first + size], ow[f, at_of(w)]).astype(BF16)

    def finish(f, ref):
        for copy in rims_out[f]:
            copy.wait()
        upper = nn(sendt_ref[...], rim_out[f]).astype(BF16)
        lower = (nn(ownt_ref[...], ow[f]) + nn(side_ref[...], rim_out[f, 208:256])).astype(BF16)
        for s in range(WH):
            full, r = (upper, s) if s < WH // 2 else (lower, s - WH // 2)
            ref[s] = full[r * PITCH:r * PITCH + COLS * LEV].reshape(COLS, LEV, c)

    stores = []

    def store(src, dst):
        stores.append(pltpu.make_async_copy(src, dst, out_sem.at[len(stores)]))
        stores[-1].start()

    def store_columns(first, end):
        for k in range(first, end):
            at = (slice(None), columns_of(k))
            store(gqkv_ref.at[at], outs_h[2].at[at])

    c0, c1, c2 = chains
    for w in range(WINDOWS):
        forward(w)
    ow[0] = (x_w[...].astype(F32) + nn(mix[...], wout_ref[...])).astype(BF16)
    pack_out(0)
    for copy in rims_out[0]:
        copy.start()
    for w in range(WINDOWS):
        arrive(1, w, dy_w)
    out_grads()
    for w in range(WINDOWS):
        widen(w)
    for g in range(groups):
        for w in range(WINDOWS):
            values(g, w)
        column_grad(3 + g, g, 2)
    c0.start()
    for w in range(WINDOWS):
        backward(0, w)
    c0.first()
    qk_grads(0)
    for w in range(WINDOWS):
        backward(1, w)
    qk_grads(1)
    c1.start()
    backward(2, 0)
    backward(2, 1)
    backward(2, 2)
    c1.first()
    qk_grads(2)
    c2.start()
    c0.second()
    dn = nt(dproj[...], wqkv_ref[...])
    n_w = n_s[...]
    dx = dn - jnp.mean(dn, axis=-1, keepdims=True) - n_w * jnp.mean(dn * n_w, axis=-1, keepdims=True)
    ow[1] = (dx * rstd_s[...] + dy_w[...].astype(F32)).astype(BF16)
    pack_out(1)
    c1.second()
    bias_core()
    c0.third()
    c2.second()
    c1.third()
    for copy in rims_out[1]:
        copy.start()
    finish(0, out_ref)
    store(out_ref, outs_h[0])
    c0.fourth()
    bias_back()
    c0.last()
    unpack(0, 128)
    store(gout_ref, outs_h[3])
    store_columns(3, 5)
    c2.third()
    finish(1, dx_ref)
    store(dx_ref, outs_h[1])
    c1.fourth()
    bias_end()
    store(dr_ref, outs_h[4])
    c1.last()
    unpack(128, 224)
    store_columns(5, 9)
    c2.last()
    unpack(224, 288)
    store_columns(9, 12)
    for copy in stores:
        copy.wait()
    for chain in chains:
        chain.drain()
    bias_wait(0, 0)
    bias_wait(0, 1)


def fused(cells, cot, qkv_weight, out_weight, table, lon_size, lat_size, cells_total):
    c = out_weight.shape[0]
    heads, _, entries = table.shape
    groups = heads // GROUP
    consts = constants()
    ins = (cells, cot, qkv_weight, out_weight, table) + consts
    n, nz = lon_size // 4, lat_size // X_HI
    bshare = BIAS_TILES // lon_size
    gw = GROUP * HEAD
    vm = pltpu.VMEM
    dma = pltpu.SemaphoreType.DMA
    out_shape = (
        jax.ShapeDtypeStruct(cells.shape, BF16),
        jax.ShapeDtypeStruct(cells.shape, BF16),
        jax.ShapeDtypeStruct((c, 3 * c), F32),
        jax.ShapeDtypeStruct((c, c), F32),
        jax.ShapeDtypeStruct(table.shape, F32),
    )
    scratch = [vm(a.shape, a.dtype) for a in ins] + [
        dma((len(ins),)),
        vm((2, WH * PITCH, c), BF16),
        vm((2, RIM, c), BF16),
        vm((2, RIM, c), BF16),
        vm((groups, TOK, LANES), F32),
        vm((groups, TOK, LANES), F32),
        vm((ROWS, c), BF16),
        vm((ROWS, c), BF16),
        vm((ROWS, c), BF16),
        vm((c, ROWS), BF16),
        vm((ROWS, c), BF16),
        vm((ROWS, 3 * c), BF16),
        vm((3 * c, c), BF16),
        vm((2, ROWS, c), BF16),
        vm((2, RIM, c), BF16),
        vm((2, RIM, c), BF16),
        vm((ROWS, 2 * c), BF16),
        vm((WINDOWS, c, TOK), BF16),
        vm((WINDOWS, groups, gw, LANES), BF16),
        vm((WINDOWS, groups, TOK, LANES), F32),
        vm((c, LANES), BF16),
        vm((WINDOWS, groups, gw, LANES), BF16),
        vm((WINDOWS * gw, LANES), BF16),
        vm((heads, entries), F32),
        vm((heads * SLABS, WH * SPAN), F32),
        vm((256, 384), F32),
        vm((ROWS, c), F32),
        vm((ROWS, 1), F32),
        dma((2, 14)),
    ]
    tile = (16, 128)
    for tiles in CHUNKS[:-1]:
        share = tiles // (2 * n * n)
        scratch += [
            vm((2, n * n, share) + tile, BF16),
            vm((n * n, share) + tile, BF16),
            vm((n * n, share) + tile, BF16),
            vm((n * n - 1, share) + tile, BF16),
            vm((nz, share) + tile, BF16),
            vm((2, n * n, share) + tile, BF16),
            dma((2, 5)),
        ]
    share = CHUNKS[-1] // (2 * n * n)
    scratch += [
        vm((2 * n * n, share) + tile, BF16),
        vm((2 * n * n - 1, share) + tile, BF16),
        vm((nz, share) + tile, BF16),
        vm((2 * n * n, share) + tile, BF16),
        dma((2, 3)),
    ]
    scratch += [
        vm((lon_size, bshare) + tile, BF16),
        vm((lon_size - 1, bshare) + tile, BF16),
        vm((lon_size, bshare) + tile, BF16),
        dma((2, 2)),
    ]
    scratch += [vm(a.shape, a.dtype) for a in out_shape] + [dma((13,))]
    kernel = functools.partial(
        body, lon_size, lat_size, groups, (c // heads) ** -0.5, cells_total ** -0.5
    )
    results = pl.pallas_call(
        kernel,
        out_shape=out_shape,
        in_specs=[pl.BlockSpec(memory_space=pl.ANY)] * len(ins),
        out_specs=(pl.BlockSpec(memory_space=pl.ANY),) * len(out_shape),
        scratch_shapes=scratch,
        compiler_params=pltpu.CompilerParams(
            vmem_limit_bytes=60 * 1024 * 1024, collective_id=0, has_side_effects=True
        ),
        cost_estimate=pl.CostEstimate(flops=6_000_000_000, bytes_accessed=10_000_000, transcendentals=800_000),
    )(*ins)
    return handed_out(results)


def handed_out(arrays):
    cuts = [(i, k) for i, a in enumerate(arrays) for k in range(6 if i == 2 else 2 if i == 3 else 1)]

    def move(*refs):
        ins, outs, (sem, *held) = refs[:len(arrays)], refs[len(arrays):2 * len(arrays)], refs[2 * len(arrays):]
        into, out_of = [], []
        for j, (i, k) in enumerate(cuts):
            parts = sum(1 for at, _ in cuts if at == i)
            rows = arrays[i].shape[0] // parts
            at = pl.ds(k * rows, rows)
            into.append(pltpu.make_async_copy(ins[i].at[at], held[i].at[at], sem.at[0, j]))
            out_of.append(pltpu.make_async_copy(held[i].at[at], outs[i].at[at], sem.at[1, j]))
        for copy in into:
            copy.start()
        for first, second in zip(into, out_of):
            first.wait()
            second.start()
        for copy in out_of:
            copy.wait()

    return pl.pallas_call(
        move,
        out_shape=tuple(jax.ShapeDtypeStruct(a.shape, a.dtype) for a in arrays),
        in_specs=[pl.BlockSpec(memory_space=pl.ANY)] * len(arrays),
        out_specs=(pl.BlockSpec(memory_space=pl.ANY),) * len(arrays),
        scratch_shapes=[pltpu.SemaphoreType.DMA((2, len(cuts)))] + [pltpu.VMEM(a.shape, a.dtype) for a in arrays],
        compiler_params=pltpu.CompilerParams(vmem_limit_bytes=60 * 1024 * 1024),
    )(*arrays)


def on_device(cells, qkv_weight, out_weight, earth_bias, cotangent):
    lon_size, lat_size = lax.axis_size("lon"), lax.axis_size("lat")
    heads = earth_bias.shape[1]
    cells_total = LEV * cells.shape[1] * cells.shape[2] * lon_size * lat_size
    out, dx, gqkv, gout, dr = fused(
        cells.transpose(1, 2, 0, 3), cotangent.transpose(1, 2, 0, 3), qkv_weight, out_weight, earth_bias.transpose(1, 0, 2),
        lon_size, lat_size, cells_total
    )
    out, dx = out.transpose(2, 0, 1, 3), dx.transpose(2, 0, 1, 3)
    return out, dx, gqkv, gout, dr.transpose(1, 0, 2)


def solution(mesh):
    grid = P(None, "lat", "lon", None)
    return jax.shard_map(
        on_device,
        mesh=mesh,
        in_specs=(grid, P(), P(), P("lat", None, None), grid),
        out_specs=(grid, grid, P(), P(), P("lat", None, None)),
        check_vma=False,
    )
```

```python
import functools

import numpy as np
import jax
import jax.numpy as jnp
from jax import lax
from jax.experimental import pallas as pl
from jax.experimental.pallas import tpu as pltpu
from jax.sharding import PartitionSpec as P

LEV = 2
WH = 6
WW = 12
TOK = LEV * WH * WW
SLABS = LEV * WH
SPAN = 2 * WW - 1
GROUP = 4
HEAD = 32
LANES = GROUP * TOK
WINDOWS = 3
ROWS = WINDOWS * TOK
COLS = WINDOWS * WW
PITCH = 80
FINE_RIMS = ((0, 80, 0), (80, 80, 0), (160, 48, 0), (208, 48, 1), (256, 48, 2))
RIMS = ((0, 208, 0), (208, 48, 1), (256, 48, 2))
RIM_OF = ((0, 80), (80, 80), (160, 144))
RIM = 304
BIAS_TILES = 32
CHUNKS = (96, 96, 96)
X_HI = 2
F32 = jnp.float32
BF16 = jnp.bfloat16
MESH = pl.DeviceIdType.MESH


def nn(a, b):
    return lax.dot_general(a, b, (((1,), (0,)), ((), ())), preferred_element_type=F32)


def nt(a, b):
    return lax.dot_general(a, b, (((1,), (1,)), ((), ())), preferred_element_type=F32)


def constants():
    j1, i2, j2 = np.meshgrid(np.arange(WW), np.arange(WH), np.arange(WW), indexing="ij")
    spot = (i2 * SPAN + j1 - j2 + WW - 1).reshape(-1)
    spread = (spot[:, None] == np.arange(WH * SPAN)[None, :]).astype(np.float32)
    gather = np.zeros((144, spread.shape[0]), np.float32)
    gather[: WH * SPAN] = spread.T
    lane = np.arange(LANES)
    lane_col, lane_slab = lane // (SLABS * GROUP), lane // GROUP % SLABS
    token_of_lane = lane_slab * WW + lane_col
    pick = (np.arange(TOK)[:, None] == token_of_lane[None, :]).astype(np.float32)
    row_half = np.arange(TOK) // WW % WH >= WH - WH // 2
    lane_half = lane_slab % WH >= WH - WH // 2
    cross = np.where(row_half[:, None] != lane_half[None, :], -1e9, 0.0).astype(np.float32)
    own = np.zeros((ROWS, WH * PITCH), np.float32)
    rim = np.zeros((ROWS, RIM), np.float32)
    send = np.zeros((RIM, WH * PITCH), np.float32)
    h = WH // 2
    for w in range(WINDOWS):
        for z in range(LEV):
            for i in range(WH):
                for j in range(WW):
                    t = w * TOK + (z * WH + i) * WW + j
                    col = WW // 2 + w * WW + j
                    below, beside = i >= h, col >= COLS
                    row, k = ((i - h) if below else (i + h)), i % h
                    slab = row * PITCH + col % COLS * LEV + z
                    if not below and not beside:
                        own[t, slab] = 1
                        continue
                    if beside:
                        at = (256 if below else 208) + z * 18 + k * 6 + j - 6
                    elif w == WINDOWS - 1:
                        at = 160 + z * 18 + k * 6 + j
                    else:
                        at = 80 * w + z * 36 + k * 12 + j
                    rim[t, at] = 1
                    send[at, slab] = 1
    low = WH // 2 * PITCH
    rim_w = np.zeros((ROWS, 144), np.float32)
    rim_wt = np.zeros((RIM, TOK), np.float32)
    for w, (at, size) in enumerate(RIM_OF):
        block = rim[w * TOK:(w + 1) * TOK, at:at + size]
        rim_w[w * TOK:(w + 1) * TOK, :size] = block
        rim_wt[at:at + size] = block.T
    send_w = np.concatenate([send[:208, :low], send[208:256, low:], send[256:, :low]], axis=0)
    bf = lambda a: jnp.asarray(np.ascontiguousarray(a), BF16)
    return (
        bf(spread), bf(gather), bf(pick), jnp.asarray(cross, F32),
        bf(own[:, low:]), bf(rim_w), bf(send_w), bf(own[:, low:].T), bf(rim_wt), bf(send[:, :low].T),
        bf(send[208:256, low:].T),
    )


N_IN = 16


def body(lon_size, lat_size, groups, scale, grad_scale, *refs):
    (cells_h, cot_h, wqkv_h, wout_h, r_h) = refs[:5]
    consts_h = refs[5:N_IN]
    outs_h = refs[N_IN:N_IN + 5]
    (cells_v, cot_v, wqkv_ref, wout_ref, r_ref,
     spread_ref, gather_ref, pick_ref, cross_ref, own_ref, rim_ref, send_ref, ownt_ref, rimt_ref, sendt_ref,
     side_ref,
     load_sem, slab, rim_snd, rim_in, bt, db, x_w, dy_w, normed, normed_t, mix, dproj, wt, ow, rim_osnd, rim_out,
     kv, k_ts, q_ws, soft_s, m_ts, dm_ws, dq_ts, tab, rows_of, turned, n_s, rstd_s,
     halo_sem, *comm) = refs[N_IN + 5:]
    (out_ref, dx_ref, gqkv_ref, gout_ref, dr_ref, out_sem) = comm[-6:]
    chunk_refs = [comm[i * 7:i * 7 + 7] for i in range(len(CHUNKS))]
    (bb, brecv, bfin, b_sem) = comm[len(CHUNKS) * 7:-6]
    c = wout_ref.shape[0]
    n, nz = lon_size // 4, lat_size // X_HI
    half = WH * WW
    blk = SLABS * GROUP
    gw = GROUP * HEAD

    lon, lat = lax.axis_index("lon"), lax.axis_index("lat")
    core, x_lo, y = lon % 2, lon // 2 % 2, lon // 4
    x_hi, z = lat // nz, lat % nz
    x = x_hi * 2 + x_lo
    other = 1 - core
    nxy = n * n
    p = y * n + x

    def dev(lon_at, lat_at):
        return {"lon": lon_at, "lat": lat_at}

    def chip(x_at, y_at):
        return dev((y_at * 2 + x_at % 2) * 2 + core, x_at // 2 * nz + z)

    sibling = dev(lon + 1 - 2 * core, lat)
    plane, zs, line = [], [], []
    for o in range(1, nxy):
        q = (p + o) % nxy
        plane.append((q, chip(q % n, q // n)))
    for o in range(1, lon_size):
        q = (lon + o) % lon_size
        line.append((q, dev(q, lat)))
    for o in range(1, nz):
        zs.append((dev(lon, x_hi * nz + (z + o) % nz), (z + nz - o) % nz))

    lon_prev, lon_next = (lon + lon_size - 1) % lon_size, (lon + 1) % lon_size
    lat_prev, lat_next = (lat + lat_size - 1) % lat_size, (lat + 1) % lat_size
    back = (dev(lon, lat_prev), dev(lon_prev, lat), dev(lon_prev, lat_prev))
    ahead = (dev(lon, lat_next), dev(lon_next, lat), dev(lon_next, lat_next))

    def remote(src, dst, send_sem, recv_sem, device):
        return pltpu.make_async_remote_copy(
            src_ref=src, dst_ref=dst, send_sem=send_sem, recv_sem=recv_sem, device_id=device, device_id_type=MESH
        )

    order = (
        (cells_h, cells_v), (consts_h[6], send_ref), (cot_h, cot_v), (r_h, r_ref), (consts_h[0], spread_ref),
        (consts_h[3], cross_ref), (wqkv_h, wqkv_ref), (consts_h[4], own_ref), (consts_h[5], rim_ref),
        (consts_h[2], pick_ref), (wout_h, wout_ref), (consts_h[8], rimt_ref), (consts_h[7], ownt_ref),
        (consts_h[9], sendt_ref), (consts_h[10], side_ref), (consts_h[1], gather_ref),
    )
    loads = [pltpu.make_async_copy(s, d, load_sem.at[i]) for i, (s, d) in enumerate(order)]
    for load in loads:
        load.start()

    barrier = pltpu.get_barrier_semaphore()

    def greet(device):
        pl.semaphore_signal(barrier, inc=1, device_id=device, device_id_type=MESH)

    partners = back + ahead
    partners += tuple(d for _, d in plane + line) + tuple(d for d, _ in zs)
    for device in partners:
        greet(device)

    def rim_copies(f, snd, rcv, devices, base, parts):
        return [
            remote(
                snd.at[f, pl.ds(at, size)], rcv.at[f, pl.ds(at, size)],
                halo_sem.at[0, base + k], halo_sem.at[1, base + k], devices[to],
            )
            for k, (at, size, to) in enumerate(parts)
        ]

    rims_in = (
        rim_copies(0, rim_snd, rim_in, back, 0, FINE_RIMS),
        rim_copies(1, rim_snd, rim_in, back, 5, RIMS),
    )
    rims_out = (
        rim_copies(0, rim_osnd, rim_out, ahead, 8, RIMS),
        rim_copies(1, rim_osnd, rim_out, ahead, 11, RIMS),
    )
    low = WH // 2 * PITCH
    def enter(f):
        src = (cells_v, cot_v)[f]
        loads[2 * f].wait()
        for s in range(WH):
            slab[f, s * PITCH:(s + 1) * PITCH, :] = jnp.concatenate(
                [src[s].reshape(COLS * LEV, c), jnp.zeros((PITCH - COLS * LEV, c), BF16)], axis=0
            )
        if f == 0:
            loads[1].wait()
        rim_snd[f, :208] = nn(send_ref[:208], slab[f, :low]).astype(BF16)
        rim_snd[f, 208:256] = nn(send_ref[208:256], slab[f, low:]).astype(BF16)
        rim_snd[f, 256:] = nn(send_ref[256:], slab[f, :low]).astype(BF16)
        if f == 0:
            pl.semaphore_wait(barrier, len(partners))
        for copy in rims_in[f]:
            copy.start()

    enter(0)

    for load in loads[3:6]:
        load.wait()
    last = (lat == lat_size - 1).astype(F32)
    tab[...] = r_ref[:, 0, :]
    width = WH * SPAN

    def segment(z1, z2, i1):
        return pl.ds(((z1 * LEV + z2) * WH + i1) * width, width)

    for z2 in range(LEV):
        for z1 in range(LEV):
            for i1 in range(WH):
                piece = tab[:, segment(z1, z2, i1)]
                for g in range(groups):
                    at = g * blk + (z1 * WH + i1) * GROUP
                    rows_of[at:at + GROUP, :] = piece[g * GROUP:(g + 1) * GROUP]
        table = rows_of[...]
        hi = table.astype(BF16)
        rest = table - hi.astype(F32)
        mid = rest.astype(BF16)
        lo = (rest - mid.astype(F32)).astype(BF16)
        spread = spread_ref[...]
        u = nt(spread, hi) + nt(spread, mid) + nt(spread, lo)
        for g in range(groups):
            rows = jnp.concatenate(
                [u[j * half:(j + 1) * half, g * blk:(g + 1) * blk] for j in range(WW)], axis=1
            )
            keep = pl.ds(z2 * half, half)
            bt[g, keep, :] = rows + cross_ref[keep, :] * last
    row = lax.broadcasted_iota(jnp.int32, (c, c), 0)
    col = lax.broadcasted_iota(jnp.int32, (c, c), 1)
    eye = (row == col).astype(F32).astype(BF16)
    head_row = lax.broadcasted_iota(jnp.int32, (gw, LANES), 0) // HEAD
    head_lane = lax.broadcasted_iota(jnp.int32, (gw, LANES), 1) % GROUP
    mine = (head_row == head_lane).astype(F32)
    for load in loads[6:]:
        load.wait()
    for part in range(3):
        wt[part * c:(part + 1) * c, :] = nt(eye, wqkv_ref[:, part * c:(part + 1) * c]).astype(BF16)
    pick = pick_ref[...]

    def arrive(f, w, ref):
        if f == 0:
            parts = rims_in[0][w:w + 1] if w < WINDOWS - 1 else rims_in[0][w:]
        else:
            parts = rims_in[1][:1] if w == 0 else rims_in[1][1:] if w == WINDOWS - 1 else []
        for copy in parts:
            copy.wait()
        at, (first, size) = slice(w * TOK, (w + 1) * TOK), RIM_OF[w]
        ref[at, :] = (
            nn(own_ref[at, :], slab[f, low:]) + nn(rim_ref[at, :size], rim_in[f, first:first + size])
        ).astype(BF16)

    def at_of(w):
        return slice(w * TOK, (w + 1) * TOK)

    def g_of(g, part=0):
        return slice(part * c + g * gw, part * c + (g + 1) * gw)

    def forward(w):
        at = at_of(w)
        arrive(0, w, x_w)
        cells = x_w[at, :].astype(F32)
        average = jnp.mean(cells, axis=-1, keepdims=True)
        centred = cells - average
        rstd = lax.rsqrt(jnp.mean(centred * centred, axis=-1, keepdims=True) + 1e-05)
        rstd_s[at, :] = rstd
        n_w = centred * rstd
        n_s[at, :] = n_w
        here = n_w.astype(BF16)
        normed[at, :] = here
        kv[at, :] = nn(here, wqkv_ref[:, c:]).astype(BF16)
        qkv_t = nt(wt[...], here).astype(BF16)
        q_all = nn(qkv_t[:c], pick)
        k_ts[w] = qkv_t[c:2 * c]
        for g in range(groups):
            q_wide = (q_all[g_of(g)] * mine).astype(BF16)
            q_ws[w, g] = q_wide
            s = nn(kv[at, g_of(g)], q_wide) * scale + bt[g]
            top = jnp.max(s, axis=0, keepdims=True)
            e = jnp.exp(s - top)
            soft = e * (1.0 / jnp.sum(e, axis=0, keepdims=True))
            soft_s[w, g] = soft
            m_ts[g_of(g), :] = (nn(qkv_t[g_of(g, 2)], soft.astype(BF16)) * mine).astype(BF16)
        mix[at, :] = nt(pick, m_ts[...]).astype(BF16)

    def widen(w):
        dm_t = nt(wout_ref[...], dy_w[at_of(w), :]).astype(BF16)
        dm_all = nn(dm_t, pick)
        for g in range(groups):
            dm_ws[w, g] = (dm_all[g_of(g)] * mine).astype(BF16)

    def backward(g, w):
        at = at_of(w)
        soft = soft_s[w, g]
        dm_wide = dm_ws[w, g]
        da = nn(kv[at, g_of(g, 1)], dm_wide)
        ds = soft * (da - jnp.sum(soft * da, axis=0, keepdims=True))
        if w == 0:
            db[g] = ds
        else:
            db[g] += ds
        ds = ds.astype(BF16)
        dq_ts[w * gw:(w + 1) * gw, :] = (nn(k_ts[w, g_of(g), :], ds) * (mine * scale)).astype(BF16)
        dproj[at, g_of(g, 1)] = (nt(ds, q_ws[w, g]) * scale).astype(BF16)
        dproj[at, g_of(g, 2)] = nt(soft.astype(BF16), dm_wide).astype(BF16)

    def tile_at(t):
        i = 0
        while t >= CHUNKS[i]:
            t -= CHUNKS[i]
            i += 1
        half_tiles = CHUNKS[i] // 2
        share = half_tiles // nxy
        return i, (t // half_tiles, t % half_tiles // share, t % share)

    def put(t, value):
        i, at = tile_at(t)
        chunk_refs[i][0][at] = value.astype(BF16)

    def out_grads():
        normed_t[...] = nt(eye, normed[...]).astype(BF16)
        grad = nn(nt(eye, mix[...]).astype(BF16), dy_w[...]) * grad_scale
        for k in range(3):
            for r in range(24):
                put(k * 24 + r, grad[r * 16:(r + 1) * 16, k * 128:(k + 1) * 128])

    def qkv_grads(g):
        dq = nt(pick, dq_ts[...]).astype(BF16)
        for w in range(WINDOWS):
            dproj[at_of(w), g_of(g)] = dq[:, w * gw:(w + 1) * gw]
        for part in range(3):
            grad = nn(normed_t[...], dproj[:, g_of(g, part)]) * grad_scale
            for r in range(24):
                put(72 + 72 * g + part * 24 + r, grad[r * 16:(r + 1) * 16])

    class Chain:
        def __init__(self, refs):
            (self.gb, self.crecv, self.xs, self.xrecv, self.zbuf, self.fin, self.sem) = refs

        def send(self, stage, src, dst, device):
            remote(src, dst, self.sem.at[0, stage], self.sem.at[1, stage], device).start()

        def wait(self, side, stage, like):
            pltpu.make_async_copy(like, like, self.sem.at[side, stage]).wait()

        def start(self):
            self.send(0, self.gb.at[other], self.crecv, sibling)

        def first(self):
            self.wait(1, 0, self.crecv)
            self.xs[...] = (self.gb[core].astype(F32) + self.crecv[...].astype(F32)).astype(BF16)
            for o, (q, d) in enumerate(plane):
                self.send(1, self.xs.at[q], self.xrecv.at[o], d)

        def second(self):
            self.wait(1, 1, self.xrecv)
            total = self.xs[p].astype(F32)
            for o in range(nxy - 1):
                total += self.xrecv[o].astype(F32)
            self.zbuf[0] = total.astype(BF16)
            for o, (d, _) in enumerate(zs):
                self.send(2, self.zbuf.at[0], self.zbuf.at[o + 1], d)

        def third(self):
            if nz > 1:
                self.wait(1, 2, self.zbuf.at[pl.ds(1, nz - 1)])
            total = self.zbuf[z].astype(F32)
            for k in range(1, nz):
                total += self.zbuf[(z + nz - k) % nz].astype(F32)
            mine_at = self.fin.at[core, p]
            mine_at[...] = total.astype(BF16)
            for _, d in plane:
                self.send(3, mine_at, mine_at, d)

        def fourth(self):
            self.wait(1, 3, self.xrecv)
            self.send(4, self.fin.at[core], self.fin.at[core], sibling)

        def last(self):
            self.wait(1, 4, self.fin.at[other])

        def drain(self):
            self.wait(0, 0, self.crecv)
            self.wait(0, 1, self.xrecv)
            if nz > 1:
                self.wait(0, 2, self.zbuf.at[pl.ds(1, nz - 1)])
            self.wait(0, 3, self.xrecv)
            self.wait(0, 4, self.crecv)

    chains = [Chain(r) for r in chunk_refs]

    def unpack(first, end):
        for t in range(first, end):
            i, at = tile_at(t)
            value = chains[i].fin[at].astype(F32)
            r, k = t % 24, t // 24
            rows = slice(r * 16, (r + 1) * 16)
            if k < 3:
                gout_ref[rows, k * 128:(k + 1) * 128] = value
            else:
                g, part = (k - 3) // 3, (k - 3) % 3
                gqkv_ref[rows, g_of(g, part)] = value

    bshare = BIAS_TILES // lon_size

    def bias_wait(side, stage):
        pltpu.make_async_copy(brecv, brecv, b_sem.at[side, stage]).wait()

    def bias_core():
        rows = jnp.concatenate(
            [
                jnp.concatenate(
                    [
                        db[g, z2 * half:(z2 + 1) * half, j * blk:(j + 1) * blk]
                        for z2 in range(LEV)
                        for g in range(groups)
                    ]
                    + [jnp.zeros((half, 96), F32)],
                    axis=1,
                )
                for j in range(WW)
            ],
            axis=0,
        ).astype(BF16)
        dr = nn(gather_ref[...], rows).astype(BF16)
        for t in range(BIAS_TILES):
            k, r = t // 9, t % 9
            tile = dr[r * 16:(r + 1) * 16, k * 128:(k + 1) * 128] if k < 3 else jnp.zeros((16, 128), BF16)
            bb[bias_at(t)] = tile
        for o, (q, d) in enumerate(line):
            remote(bb.at[q], brecv.at[o], b_sem.at[0, 0], b_sem.at[1, 0], d).start()

    def bias_at(t):
        return t // bshare, t % bshare

    def bias_back():
        bias_wait(1, 0)
        total = bb[lon].astype(F32)
        for o in range(lon_size - 1):
            total += brecv[o].astype(F32)
        mine_at = bfin.at[lon]
        mine_at[...] = total.astype(BF16)
        for _, d in line:
            remote(mine_at, mine_at, b_sem.at[0, 1], b_sem.at[1, 1], d).start()

    def bias_end():
        bias_wait(1, 1)
        turned[144:, :] = jnp.zeros((256 - 144, 384), F32)
        for t in range(27):
            k, r = t // 9, t % 9
            turned[r * 16:(r + 1) * 16, k * 128:(k + 1) * 128] = bfin[bias_at(t)].astype(F32)
        flat = turned[...].T
        for z2 in range(LEV):
            for z1 in range(LEV):
                for i1 in range(WH):
                    for g in range(groups):
                        at = z2 * groups * blk + g * blk + (z1 * WH + i1) * GROUP
                        tab[g * GROUP:(g + 1) * GROUP, segment(z1, z2, i1)] = flat[at:at + GROUP, :width]
        dr_ref[:, 0, :] = tab[...]

    def pack_out(f):
        for w, (first, size) in enumerate(RIM_OF):
            rim_osnd[f, first:first + size] = nn(rimt_ref[first:first + size], ow[f, at_of(w)]).astype(BF16)

    def finish(f, ref):
        for copy in rims_out[f]:
            copy.wait()
        upper = nn(sendt_ref[...], rim_out[f]).astype(BF16)
        lower = (nn(ownt_ref[...], ow[f]) + nn(side_ref[...], rim_out[f, 208:256])).astype(BF16)
        for s in range(WH):
            full, r = (upper, s) if s < WH // 2 else (lower, s - WH // 2)
            ref[s] = full[r * PITCH:r * PITCH + COLS * LEV].reshape(COLS, LEV, c)

    stores = []

    def store(src, dst):
        stores.append(pltpu.make_async_copy(src, dst, out_sem.at[len(stores)]))
        stores[-1].start()

    def store_columns(first, end):
        for k in range(first, end):
            at = (slice(None), g_of(k // 3, k % 3))
            store(gqkv_ref.at[at], outs_h[2].at[at])

    c0, c1, c2 = chains
    forward(0)
    enter(1)
    forward(1)
    forward(2)
    ow[0] = (x_w[...].astype(F32) + nn(mix[...], wout_ref[...])).astype(BF16)
    pack_out(0)
    for copy in rims_out[0]:
        copy.start()
    for w in range(WINDOWS):
        arrive(1, w, dy_w)
    out_grads()
    for w in range(WINDOWS):
        widen(w)
    for w in range(WINDOWS):
        backward(0, w)
    qkv_grads(0)
    c0.start()
    backward(1, 0)
    backward(1, 1)
    c0.first()
    backward(1, 2)
    qkv_grads(1)
    c1.start()
    backward(2, 0)
    backward(2, 1)
    c1.first()
    backward(2, 2)
    qkv_grads(2)
    c2.start()
    c0.second()
    dn = nt(dproj[...], wqkv_ref[...])
    n_w = n_s[...]
    dx = dn - jnp.mean(dn, axis=-1, keepdims=True) - n_w * jnp.mean(dn * n_w, axis=-1, keepdims=True)
    ow[1] = (dx * rstd_s[...] + dy_w[...].astype(F32)).astype(BF16)
    c2.first()
    pack_out(1)
    c1.second()
    bias_core()
    c0.third()
    c2.second()
    for copy in rims_out[1]:
        copy.start()
    finish(0, out_ref)
    store(out_ref, outs_h[0])
    c1.third()
    c0.fourth()
    bias_back()
    c2.third()
    c0.last()
    unpack(0, 96)
    store(gout_ref, outs_h[3])
    c1.fourth()
    bias_end()
    store(dr_ref, outs_h[4])
    finish(1, dx_ref)
    store(dx_ref, outs_h[1])
    c1.last()
    unpack(96, 192)
    store_columns(0, 5)
    c2.fourth()
    c2.last()
    unpack(192, 288)
    store_columns(5, 9)
    for copy in stores:
        copy.wait()
    for chain in chains:
        chain.drain()
    bias_wait(0, 0)
    bias_wait(0, 1)


def fused(cells, cot, qkv_weight, out_weight, table, lon_size, lat_size, cells_total):
    c = out_weight.shape[0]
    heads, _, entries = table.shape
    groups = heads // GROUP
    consts = constants()
    ins = (cells, cot, qkv_weight, out_weight, table) + consts
    n, nz = lon_size // 4, lat_size // X_HI
    bshare = BIAS_TILES // lon_size
    gw = GROUP * HEAD
    vm = pltpu.VMEM
    dma = pltpu.SemaphoreType.DMA
    out_shape = (
        jax.ShapeDtypeStruct(cells.shape, BF16),
        jax.ShapeDtypeStruct(cells.shape, BF16),
        jax.ShapeDtypeStruct((c, 3 * c), F32),
        jax.ShapeDtypeStruct((c, c), F32),
        jax.ShapeDtypeStruct(table.shape, F32),
    )
    scratch = [vm(a.shape, a.dtype) for a in ins] + [
        dma((len(ins),)),
        vm((2, WH * PITCH, c), BF16),
        vm((2, RIM, c), BF16),
        vm((2, RIM, c), BF16),
        vm((groups, TOK, LANES), F32),
        vm((groups, TOK, LANES), F32),
        vm((ROWS, c), BF16),
        vm((ROWS, c), BF16),
        vm((ROWS, c), BF16),
        vm((c, ROWS), BF16),
        vm((ROWS, c), BF16),
        vm((ROWS, 3 * c), BF16),
        vm((3 * c, c), BF16),
        vm((2, ROWS, c), BF16),
        vm((2, RIM, c), BF16),
        vm((2, RIM, c), BF16),
        vm((ROWS, 2 * c), BF16),
        vm((WINDOWS, c, TOK), BF16),
        vm((WINDOWS, groups, gw, LANES), BF16),
        vm((WINDOWS, groups, TOK, LANES), F32),
        vm((c, LANES), BF16),
        vm((WINDOWS, groups, gw, LANES), BF16),
        vm((WINDOWS * gw, LANES), BF16),
        vm((heads, entries), F32),
        vm((heads * SLABS, WH * SPAN), F32),
        vm((256, 384), F32),
        vm((ROWS, c), F32),
        vm((ROWS, 1), F32),
        dma((2, 14)),
    ]
    tile = (16, 128)
    for tiles in CHUNKS:
        share = tiles // (2 * n * n)
        scratch += [
            vm((2, n * n, share) + tile, BF16),
            vm((n * n, share) + tile, BF16),
            vm((n * n, share) + tile, BF16),
            vm((n * n - 1, share) + tile, BF16),
            vm((nz, share) + tile, BF16),
            vm((2, n * n, share) + tile, BF16),
            dma((2, 5)),
        ]
    scratch += [
        vm((lon_size, bshare) + tile, BF16),
        vm((lon_size - 1, bshare) + tile, BF16),
        vm((lon_size, bshare) + tile, BF16),
        dma((2, 2)),
    ]
    scratch += [vm(a.shape, a.dtype) for a in out_shape] + [dma((13,))]
    kernel = functools.partial(
        body, lon_size, lat_size, groups, (c // heads) ** -0.5, cells_total ** -0.5
    )
    results = pl.pallas_call(
        kernel,
        out_shape=out_shape,
        in_specs=[pl.BlockSpec(memory_space=pl.ANY)] * len(ins),
        out_specs=(pl.BlockSpec(memory_space=pl.ANY),) * len(out_shape),
        scratch_shapes=scratch,
        compiler_params=pltpu.CompilerParams(
            vmem_limit_bytes=60 * 1024 * 1024, collective_id=0, has_side_effects=True
        ),
        cost_estimate=pl.CostEstimate(flops=6_000_000_000, bytes_accessed=10_000_000, transcendentals=800_000),
    )(*ins)
    return handed_out(results)


def handed_out(arrays):
    cuts = [(i, k) for i, a in enumerate(arrays) for k in range(6 if i == 2 else 2 if i == 3 else 1)]

    def move(*refs):
        ins, outs, (sem, *held) = refs[:len(arrays)], refs[len(arrays):2 * len(arrays)], refs[2 * len(arrays):]
        into, out_of = [], []
        for j, (i, k) in enumerate(cuts):
            parts = sum(1 for at, _ in cuts if at == i)
            rows = arrays[i].shape[0] // parts
            at = pl.ds(k * rows, rows)
            into.append(pltpu.make_async_copy(ins[i].at[at], held[i].at[at], sem.at[0, j]))
            out_of.append(pltpu.make_async_copy(held[i].at[at], outs[i].at[at], sem.at[1, j]))
        for copy in into:
            copy.start()
        for first, second in zip(into, out_of):
            first.wait()
            second.start()
        for copy in out_of:
            copy.wait()

    return pl.pallas_call(
        move,
        out_shape=tuple(jax.ShapeDtypeStruct(a.shape, a.dtype) for a in arrays),
        in_specs=[pl.BlockSpec(memory_space=pl.ANY)] * len(arrays),
        out_specs=(pl.BlockSpec(memory_space=pl.ANY),) * len(arrays),
        scratch_shapes=[pltpu.SemaphoreType.DMA((2, len(cuts)))] + [pltpu.VMEM(a.shape, a.dtype) for a in arrays],
        compiler_params=pltpu.CompilerParams(vmem_limit_bytes=60 * 1024 * 1024),
    )(*arrays)


def on_device(cells, qkv_weight, out_weight, earth_bias, cotangent):
    lon_size, lat_size = lax.axis_size("lon"), lax.axis_size("lat")
    heads = earth_bias.shape[1]
    cells_total = LEV * cells.shape[1] * cells.shape[2] * lon_size * lat_size
    out, dx, gqkv, gout, dr = fused(
        cells.transpose(1, 2, 0, 3), cotangent.transpose(1, 2, 0, 3), qkv_weight, out_weight, earth_bias.transpose(1, 0, 2),
        lon_size, lat_size, cells_total
    )
    out, dx = out.transpose(2, 0, 1, 3), dx.transpose(2, 0, 1, 3)
    return out, dx, gqkv, gout, dr.transpose(1, 0, 2)


def solution(mesh):
    grid = P(None, "lat", "lon", None)
    return jax.shard_map(
        on_device,
        mesh=mesh,
        in_specs=(grid, P(), P(), P("lat", None, None), grid),
        out_specs=(grid, grid, P(), P(), P("lat", None, None)),
        check_vma=False,
    )
```
